32 devices in a mesh: replica: 8 (over z, y), tensor: 4 (over x, core).
Axes of the slice: x: 2, y: 2, z: 4, core: 2. Of those that a mesh axis runs over, the one named last changes fastest.
Arguments:
- residual: bfloat16 [1024, 4, 5120], P('replica', None, 'tensor'), may hold values from -3 to 3
- queries: bfloat16 [1024, 4, 2560], P('replica', None, 'tensor'), may hold values from -144 to 144
- new_keys: bfloat16 [1024, 4, 512], P('replica', None, 'tensor'), may hold values from -6 to 6
- new_values: bfloat16 [1024, 4, 512], P('replica', None, 'tensor'), may hold values from -6 to 6
- cache_keys: bfloat16 [1024, 64, 512], P('replica', None, 'tensor'), may hold values from -7 to 7
- cache_values: bfloat16 [1024, 64, 512], P('replica', None, 'tensor'), may hold values from -6 to 6
- cache_lengths: int32 [1024], replicated, may hold values from 2 to 64
- finished: int32 [1024], replicated, may hold values 0 or 1
- partner: int32 [1024], P('replica'), may hold values from 0 to 1023, as said below
- row_slot: int32 [1024], replicated, may hold values from 0 to 3
- fork_table: int32 [8, 4], replicated, may hold values from 0 to 31, as said below
- prompt_keys: bfloat16 [32, 128, 512], P('replica', None, 'tensor'), may hold values from -6 to 6
- prompt_values: bfloat16 [32, 128, 512], P('replica', None, 'tensor'), may hold values from -6 to 6
- prompt_lengths: int32 [32], replicated, may hold values from 32 to 128
- out_proj: bfloat16 [2560, 5120], P('tensor'), may hold values from -0.125 to 0.125
Outputs:
- layer_out: bfloat16 [1024, 4, 5120], P('replica', None, 'tensor')
The draws below stay inside these ranges and needn't reach their ends.
Inputs may be any that keep to these rules, and one draw needn't show every extreme that they name: partner is an involution; each replica has exactly 4 rows paired with rows of 4 different other replicas, one of them the replica 8 / 2 away, and every other row is paired with itself. `fork_table`: the 4 entries of a replica name prompts of 4 different owners, prompt p being held by replica p // 4.
All inputs are finite; a program needn't handle non-finite values.
Results may differ from the reference program's by a relative error of at most 0.0034.
Values may be sent and summed in bfloat16 or wider, within the bound.
No kernel may reach another device: no remote copies, remote signals or barrier semaphores. Data moves between devices by JAX's collectives and lax.ppermute only.
A program may use at most 128 MiB of HBM per device.

```python
import math
import jax
import jax.numpy as jnp
from jax import lax

D = 5120
HEADS = 20
KV_HEADS = 4
HEAD_DIM = 128
STEPS = 4
ROWS_DEV = 128
SUFFIX = 64
PREFIX = 128
OWN = 4
SLOTS = 4
ROWS = 1024
PROBS = 32
MOVE = 4
N_REPLICA = 8


def shuffle_rows(sub_key):
    return jax.random.permutation(sub_key, ROWS_DEV).astype(jnp.int32)


def pair_rows(key):
    first, second = jax.random.split(key)
    odd_pick = jax.random.permutation(first, N_REPLICA // 2)[:MOVE - 1].astype(jnp.int32)
    totals = 2 * odd_pick + 1
    orders = jax.vmap(shuffle_rows)(jax.random.split(second, N_REPLICA))
    replicas = jnp.arange(N_REPLICA, dtype=jnp.int32)
    half_peer = (replicas + N_REPLICA // 2) % N_REPLICA
    odd_peers = (totals[None, :] - replicas[:, None]) % N_REPLICA
    peers = jnp.concatenate([half_peer[:, None], odd_peers], axis=1).astype(jnp.int32)
    rounds = jnp.arange(MOVE, dtype=jnp.int32)
    own_rows = replicas[:, None] * ROWS_DEV + orders[:, :MOVE]
    peer_rows = peers * ROWS_DEV + orders[peers, rounds[None, :]]
    result = jnp.arange(ROWS, dtype=jnp.int32)
    return result.at[own_rows.reshape(-1)].set(peer_rows.reshape(-1))


def draw_partner(key, part):
    return pair_rows(jax.random.fold_in(key, 11))


def owner_pick(sub_key):
    return jax.random.permutation(sub_key, N_REPLICA)[:SLOTS].astype(jnp.int32)


def draw_fork_table(key, part):
    first, second, third = jax.random.split(jax.random.fold_in(key, 12), 3)
    owners = jax.vmap(owner_pick)(jax.random.split(first, N_REPLICA))
    pick_a = jax.random.randint(second, (N_REPLICA, SLOTS), 0, OWN, dtype=jnp.int32)
    pick_b = jax.random.randint(third, (N_REPLICA, SLOTS), 0, OWN, dtype=jnp.int32)
    return (owners * OWN + jnp.minimum(pick_a, pick_b)).astype(jnp.int32)


def draw_cache_lengths(key, part):
    first, second = jax.random.split(jax.random.fold_in(key, 13))
    lengths = jax.random.randint(first, (ROWS,), 2, SUFFIX + 1, dtype=jnp.int32)
    spot = jax.random.randint(second, (), 0, ROWS, dtype=jnp.int32)
    return lengths.at[spot].set(SUFFIX)


def draw_prompt_lengths(key, part):
    first, second = jax.random.split(jax.random.fold_in(key, 14))
    lengths = jax.random.randint(first, (PROBS,), PREFIX // 4, PREFIX + 1, dtype=jnp.int32)
    spot = jax.random.randint(second, (), 0, PROBS, dtype=jnp.int32)
    return lengths.at[spot].set(PREFIX)


def draw_cache_keys(key, part):
    values = jax.random.normal(jax.random.fold_in(key, 22), (ROWS, SUFFIX, KV_HEADS * HEAD_DIM), jnp.float32)
    values = jnp.clip(values, -6.0, 6.0)
    return values.astype(jnp.bfloat16)


def draw_queries(key, part):
    values = jax.random.normal(jax.random.fold_in(key, 24), (ROWS, STEPS, HEADS * HEAD_DIM), jnp.float32)
    values = jnp.clip(values, -6.0, 6.0)
    return values.astype(jnp.bfloat16)


def touch_ends(values, own_key, least, top_value):
    spot = [jax.random.randint(jax.random.fold_in(own_key, axis), (), 0, length) for axis, length in enumerate(values.shape)]
    widest = values.shape.index(max(values.shape))
    neighbour = spot[:widest] + [(spot[widest] + 1) % values.shape[widest]] + spot[widest + 1:]
    return values.at[tuple(spot)].set(least).at[tuple(neighbour)].set(top_value)


def levels(own_key, shape, pieces, smallest, top_value):
    level = 1.0
    for position, parts in pieces:
        heights = jax.random.uniform(jax.random.fold_in(jax.random.fold_in(own_key, 6), position), (parts,), jnp.float32, smallest / len(pieces), top_value / len(pieces))
        level = level * jnp.repeat(jnp.exp(heights), shape[position] // parts).reshape((-1,) + (1,) * (len(shape) - 1 - position))
    return level


def scatter_about(own_key, dims, scale, bound, cuts=(), kind=jnp.bfloat16):
    loudness = levels(own_key, dims, cuts, -0.22, 0.18) if cuts else 1.0
    values = jax.random.normal(own_key, dims, jnp.float32) * scale * loudness
    return jnp.minimum(jnp.maximum(values, -bound), bound).astype(kind)


def setup_inputs(seed: int = 0) -> dict:
    arg_keys = jax.random.split(jax.random.key(seed), 16)
    residual = scatter_about(arg_keys[0], (ROWS, STEPS, D), 0.5, 3.0, ((0, 8), (2, 4)))
    queries = draw_queries(jax.random.fold_in(arg_keys[15], 71), 0)
    new_keys = scatter_about(arg_keys[2], (ROWS, STEPS, KV_HEADS * HEAD_DIM), 1.0, 6.0, ((0, 8), (2, 4)))
    new_values = scatter_about(arg_keys[3], (ROWS, STEPS, KV_HEADS * HEAD_DIM), 1.0, 6.0, ((0, 8), (2, 4)))
    cache_keys = draw_cache_keys(jax.random.fold_in(arg_keys[15], 71), 0)
    cache_values = scatter_about(arg_keys[5], (ROWS, SUFFIX, KV_HEADS * HEAD_DIM), 1.0, 6.0, ((0, 8), (2, 4)))
    cache_lengths = draw_cache_lengths(jax.random.fold_in(arg_keys[15], 71), 0)
    finished = touch_ends((jax.random.randint(arg_keys[7], (ROWS,), 0, 4) < 1).astype(jnp.int32), jax.random.fold_in(arg_keys[7], 1), 0, 1)
    partner = draw_partner(jax.random.fold_in(arg_keys[15], 71), 0)
    row_slot = touch_ends(jax.random.randint(arg_keys[9], (ROWS,), 0, SLOTS), jax.random.fold_in(arg_keys[9], 1), 0, SLOTS - 1).astype(jnp.int32)
    fork_table = draw_fork_table(jax.random.fold_in(arg_keys[15], 71), 0)
    prompt_keys = scatter_about(arg_keys[11], (PROBS, PREFIX, KV_HEADS * HEAD_DIM), 1.0, 6.0, ((0, 8), (2, 4)))
    prompt_values = scatter_about(arg_keys[12], (PROBS, PREFIX, KV_HEADS * HEAD_DIM), 1.0, 6.0, ((0, 8), (2, 4)))
    prompt_lengths = draw_prompt_lengths(jax.random.fold_in(arg_keys[15], 71), 0)
    out_proj = scatter_about(arg_keys[14], (HEADS * HEAD_DIM, D), (HEADS * HEAD_DIM) ** -0.5, 0.125, ((0, 4),))
    return dict(residual=residual, queries=queries, new_keys=new_keys, new_values=new_values, cache_keys=cache_keys, cache_values=cache_values, cache_lengths=cache_lengths, finished=finished, partner=partner, row_slot=row_slot, fork_table=fork_table, prompt_keys=prompt_keys, prompt_values=prompt_values, prompt_lengths=prompt_lengths, out_proj=out_proj)


def split_heads(block, kv_heads):
    return block.astype(jnp.float32).reshape(block.shape[0], block.shape[1], kv_heads, HEAD_DIM)

def attend(queries, new_keys, new_values, pre_keys, pre_values, pre_len, old_keys, old_values, old_len):
    row_count, step_count = (queries.shape[0], queries.shape[1])
    kv_heads = new_keys.shape[2] // HEAD_DIM
    groups = queries.shape[2] // HEAD_DIM // kv_heads
    query_split = queries.astype(jnp.float32).reshape(row_count, step_count, kv_heads, groups, HEAD_DIM)
    score_scale = 1.0 / math.sqrt(HEAD_DIM)
    part_pre = jnp.einsum('bskgd,bpkd->bkgsp', query_split, split_heads(pre_keys, kv_heads)) * score_scale
    part_old = jnp.einsum('bskgd,bpkd->bkgsp', query_split, split_heads(old_keys, kv_heads)) * score_scale
    part_new = jnp.einsum('bskgd,btkd->bkgst', query_split, split_heads(new_keys, kv_heads)) * score_scale
    mask_pre = jnp.arange(pre_keys.shape[1], dtype=jnp.int32)[None, :] < pre_len[:, None]
    mask_old = jnp.arange(old_keys.shape[1], dtype=jnp.int32)[None, :] < old_len[:, None]
    steps_idx = jnp.arange(step_count, dtype=jnp.int32)
    mask_new = steps_idx[None, :] <= steps_idx[:, None]
    part_pre = jnp.where(mask_pre[:, None, None, None, :], part_pre, -jnp.inf)
    part_old = jnp.where(mask_old[:, None, None, None, :], part_old, -jnp.inf)
    part_new = jnp.where(mask_new[None, None, None, :, :], part_new, -jnp.inf)
    scores = jnp.concatenate([part_pre, part_old, part_new], axis=-1)
    row_top = lax.optimization_barrier(jnp.max(scores, axis=-1, keepdims=True))
    exp_scores = jnp.exp(scores - row_top)
    weights = (exp_scores / lax.optimization_barrier(jnp.sum(exp_scores, axis=-1, keepdims=True))).astype(jnp.bfloat16).astype(jnp.float32)
    len_pre = pre_keys.shape[1]
    len_old = old_keys.shape[1]
    mixed = jnp.einsum('bkgsp,bpkd->bskgd', weights[..., :len_pre], split_heads(pre_values, kv_heads))
    mixed = mixed + jnp.einsum('bkgsp,bpkd->bskgd', weights[..., len_pre:len_pre + len_old], split_heads(old_values, kv_heads))
    mixed = mixed + jnp.einsum('bkgst,btkd->bskgd', weights[..., len_pre + len_old:], split_heads(new_values, kv_heads))
    return mixed.reshape(row_count, step_count, -1)

def reference(residual, queries, new_keys, new_values, cache_keys, cache_values, cache_lengths, finished, partner, row_slot, fork_table, prompt_keys, prompt_values, prompt_lengths, out_proj):
    weight_f = out_proj.astype(jnp.float32)

    def one_block(block_id):
        first_id = block_id * ROWS_DEV
        source = lax.dynamic_slice_in_dim(partner, first_id, ROWS_DEV)
        problem = fork_table[source // ROWS_DEV, row_slot[source]]
        pre_len = prompt_lengths[problem]
        old_len = cache_lengths[source]
        alive = (1 - finished[source]).astype(jnp.float32)
        block_q = lax.dynamic_slice_in_dim(queries, first_id, ROWS_DEV)
        block_k = lax.dynamic_slice_in_dim(new_keys, first_id, ROWS_DEV)
        block_v = lax.dynamic_slice_in_dim(new_values, first_id, ROWS_DEV)
        heads_out = attend(block_q, block_k, block_v, prompt_keys[problem], prompt_values[problem], pre_len, cache_keys[source], cache_values[source], old_len)
        heads_out = (heads_out * alive[:, None, None]).astype(jnp.bfloat16)
        branch = jnp.einsum('bsh,hd->bsd', heads_out.astype(jnp.float32), weight_f)
        block_res = lax.dynamic_slice_in_dim(residual, first_id, ROWS_DEV).astype(jnp.float32)
        return (block_res + branch).astype(jnp.bfloat16)
    result = lax.map(one_block, jnp.arange(N_REPLICA, dtype=jnp.int32))
    return result.reshape(ROWS, STEPS, D)
```

```python
import functools
import math

import jax
import jax.numpy as jnp
from jax import lax
from jax.experimental import pallas as pl
from jax.experimental.pallas import tpu as pltpu
from jax.sharding import PartitionSpec as P

HEAD_DIM = 128
LOWEST = -1e30
EXP2_SCALE = math.log2(math.e) / math.sqrt(HEAD_DIM)
VMEM_BYTES = 40 * 1024 * 1024
NT = (((1,), (1,)), ((), ()))
NN = (((1,), (0,)), ((), ()))

ANY = pl.BlockSpec(memory_space=pl.ANY)
SMEM = pl.BlockSpec(memory_space=pltpu.SMEM)
VMEM = pl.BlockSpec(memory_space=pltpu.VMEM)


def params(side_effects=False):
    return pltpu.CompilerParams(vmem_limit_bytes=VMEM_BYTES, has_side_effects=side_effects)


def matmul(a, b, dims):
    return lax.dot_general(a, b, dims, preferred_element_type=jnp.float32)


def iota(shape, dim):
    return lax.broadcasted_iota(jnp.int32, shape, dim)


def pack_kernel(
    fork, partner, queries, new_keys, new_values, keys, values, *rest, replicas, slots
):
    outs, (piece, row_of, sems) = rest[: replicas - 1], rest[replicas - 1 :]
    me = lax.axis_index("replica")
    held, prefix = keys.shape[0], keys.shape[1]
    local_rows = queries.shape[0]
    groups = queries.shape[2] // HEAD_DIM
    copies = []
    for k in range(1, replicas):
        peer = lax.rem(me + k, replicas)
        offset = jnp.int32(0)
        for s in range(slots):
            prompt = fork[peer * slots + s]
            offset = jnp.where(lax.div(prompt, held) == me, lax.rem(prompt, held), offset)
        for n, source in enumerate((keys, values)):
            copy = pltpu.make_async_copy(
                source.at[offset],
                outs[k - 1].at[pl.ds(n * prefix, prefix)],
                sems.at[k - 1, n],
            )
            copy.start()
            copies.append(copy)

    for j in range(replicas):
        row_of[j] = 0

    def note(r, carry):
        row_of[lax.div(partner[r], local_rows)] = r
        return carry

    lax.fori_loop(0, local_rows, note, 0, unroll=8)
    for k in range(1, replicas):
        r = row_of[lax.rem(me + k, replicas)]
        q = queries[r].astype(jnp.float32)
        parts = [q[:, h * HEAD_DIM : (h + 1) * HEAD_DIM] for h in range(groups)]
        parts += [new_keys[r].astype(jnp.float32), new_values[r].astype(jnp.float32)]
        pad = piece.shape[1] - sum(p.shape[0] for p in parts)
        parts += [jnp.zeros((pad, HEAD_DIM), jnp.float32)]
        piece[k - 1] = jnp.concatenate(parts, axis=0).astype(piece.dtype)
        copy = pltpu.make_async_copy(
            piece.at[k - 1],
            outs[k - 1].at[pl.ds(2 * prefix, piece.shape[1])],
            sems.at[k - 1, 2],
        )
        copy.start()
        copies.append(copy)
    for copy in copies:
        copy.wait()


def meta_kernel(
    fork, partner, row_slot, prompt_lengths, cache_lengths, finished, out, *, slots, local_rows, moved
):
    me = lax.axis_index("replica")
    rows = local_rows

    def note(r, count):
        g = me * rows + r
        slot = row_slot[g]
        out[r] = slot
        out[rows + r] = prompt_lengths[fork[me * slots + slot]]
        out[2 * rows + r] = cache_lengths[g]
        out[3 * rows + r] = 1 - finished[g]
        peer = lax.div(partner[r], rows)
        out[4 * rows + count] = r
        out[4 * rows + (moved + 8) + count] = peer
        return jnp.minimum(count + jnp.where(peer != me, 1, 0), moved)

    lax.fori_loop(0, rows, note, jnp.int32(0), unroll=4)


def softmax_weights(prompt, new, cache, prompt_mask, new_mask, cache_mask):
    prompt = jnp.where(prompt_mask, prompt, LOWEST)
    new = jnp.where(new_mask, new, LOWEST)
    cache = jnp.where(cache_mask, cache, LOWEST)
    top = jnp.max(jnp.maximum(jnp.maximum(prompt, new), cache), axis=1, keepdims=True)
    prompt = jnp.exp2((prompt - top) * EXP2_SCALE)
    new = jnp.exp2((new - top) * EXP2_SCALE)
    cache = jnp.exp2((cache - top) * EXP2_SCALE)
    inverse = 1.0 / jnp.sum(prompt + new + cache, axis=1, keepdims=True)
    return prompt * inverse, new * inverse, cache * inverse


def pick_slot(scores, slot, slots, prefix):
    picked = scores[:, :prefix]
    for s in range(1, slots):
        picked = jnp.where(slot == s, scores[:, s * prefix : (s + 1) * prefix], picked)
    return picked


def spread_slot(weights, slot, slots):
    return jnp.concatenate(
        [jnp.where(slot == s, weights, 0.0).astype(jnp.bfloat16) for s in range(slots)], axis=1
    )


def attend_block(
    first_row, meta, q, nk, nv, ck, cv, pk, pv, heads, row_meta, alive_rows, cache_scores, cache_weights, mixed,
    *, local_rows, steps, slots, suffix
):
    n = q.shape[0]
    rows = n // steps
    groups = q.shape[1] // HEAD_DIM
    prefix = pk.shape[0] // slots
    for b in range(rows):
        span = pl.ds(b * steps, steps)
        for i in range(3):
            row_meta[i, span, :] = jnp.full(
                (steps, HEAD_DIM), meta[i * local_rows + first_row + b], jnp.int32
            )
        alive = meta[3 * local_rows + first_row + b].astype(jnp.float32)
        alive_rows[span, :] = jnp.full((steps, HEAD_DIM), alive, jnp.float32)

    subs = n // 16
    keys_sub = 4 * suffix
    half = 2 * suffix
    for sub in range(subs):
        r0 = sub * 16
        qs = jnp.concatenate(
            [q[r0 : r0 + 16, h * HEAD_DIM : (h + 1) * HEAD_DIM] for h in range(groups)], axis=0
        )
        s = matmul(qs, ck[sub * keys_sub : (sub + 1) * keys_sub, :], NT)
        for h in range(groups):
            cache_scores[h, r0 : r0 + 8, :] = s[16 * h : 16 * h + 8, :half]
            cache_scores[h, r0 + 8 : r0 + 16, :] = s[16 * h + 8 : 16 * h + 16, half:]

    shape = (n, HEAD_DIM)
    lane, row = iota(shape, 1), iota(shape, 0)
    cache_own = (lane // suffix) == ((row % 8) // steps)
    cache_lane = jnp.where(cache_own, lane % suffix, suffix)
    new_mask = ((lane // steps) == (row // steps)) & ((lane % steps) <= (row % steps))
    first_half = (row % 16) < 8
    slot = row_meta[0]
    prompt_mask = lane < row_meta[1]
    cache_mask = cache_lane < row_meta[2]
    for h in range(groups):
        qh = q[:, h * HEAD_DIM : (h + 1) * HEAD_DIM]
        prompt = pick_slot(matmul(qh, pk[...], NT), slot, slots, prefix)
        wp, wn, wc = softmax_weights(
            prompt, matmul(qh, nk[...], NT), cache_scores[h], prompt_mask, new_mask, cache_mask
        )
        cache_weights[h, :, :half] = jnp.where(first_half, wc, 0.0).astype(jnp.bfloat16)
        cache_weights[h, :, half:] = jnp.where(first_half, 0.0, wc).astype(jnp.bfloat16)
        mixed[h] = matmul(spread_slot(wp, slot, slots), pv[...], NN) + matmul(
            wn.astype(jnp.bfloat16), nv[...], NN
        )
    for sub in range(subs):
        r0 = sub * 16
        w = jnp.concatenate([cache_weights[h, r0 : r0 + 16, :] for h in range(groups)], axis=0)
        o = matmul(w, cv[sub * keys_sub : (sub + 1) * keys_sub, :], NN)
        for h in range(groups):
            total = mixed[h, r0 : r0 + 16, :] + o[16 * h : 16 * h + 16, :]
            heads[r0 : r0 + 16, h * HEAD_DIM : (h + 1) * HEAD_DIM] = (
                total * alive_rows[r0 : r0 + 16, :]
            ).astype(heads.dtype)


def first_kernel(
    fork, meta, q, nk, nv, ck, cv, own_keys, own_values, *rest, replicas, slots, moved, local_rows, steps, suffix
):
    recvs, rest = rest[: replicas - 1], rest[replicas - 1 :]
    heads, pk, pv, moved_q = rest[:4]
    row_meta, alive_rows, cache_scores, cache_weights, mixed, sems, moved_sems = rest[4:]
    me = lax.axis_index("replica")
    held, prefix = own_keys.shape[0], own_keys.shape[1]
    extra = moved_q.shape[1]
    for s in range(slots):
        prompt = fork[me * slots + s]
        k = lax.rem(me - lax.div(prompt, held) + replicas, replicas)
        offset = lax.rem(prompt, held)
        targets = (pk.at[pl.ds(s * prefix, prefix)], pv.at[pl.ds(s * prefix, prefix)])

        @pl.when(k == 0)
        def _():
            pltpu.make_async_copy(own_keys.at[offset], targets[0], sems.at[s, 0]).start()
            pltpu.make_async_copy(own_values.at[offset], targets[1], sems.at[s, 1]).start()

        for kk in range(1, replicas):

            @pl.when(k == kk)
            def _():
                for n in range(2):
                    pltpu.make_async_copy(
                        recvs[kk - 1].at[pl.ds(n * prefix, prefix)], targets[n], sems.at[s, n]
                    ).start()

    for i in range(moved):
        k = lax.rem(me - meta[4 * local_rows + moved + 8 + i] + replicas, replicas)
        for kk in range(1, replicas):

            @pl.when(k == kk)
            def _():
                pltpu.make_async_copy(
                    recvs[kk - 1].at[pl.ds(2 * prefix, extra)], moved_q.at[i], moved_sems.at[i]
                ).start()

    for s in range(slots):
        pltpu.make_async_copy(own_keys.at[0], pk.at[pl.ds(s * prefix, prefix)], sems.at[s, 0]).wait()
        pltpu.make_async_copy(own_values.at[0], pv.at[pl.ds(s * prefix, prefix)], sems.at[s, 1]).wait()
    attend_block(
        0, meta, q, nk, nv, ck, cv, pk, pv, heads, row_meta, alive_rows, cache_scores, cache_weights, mixed,
        local_rows=local_rows, steps=steps, slots=slots, suffix=suffix,
    )
    for i in range(moved):
        pltpu.make_async_copy(
            recvs[0].at[pl.ds(2 * prefix, extra)], moved_q.at[i], moved_sems.at[i]
        ).wait()


def later_kernel(meta, *refs, start, local_rows, steps, slots, suffix):
    first_row = (start + pl.program_id(0)) * (refs[0].shape[0] // steps)
    attend_block(
        first_row, meta, *refs, local_rows=local_rows, steps=steps, slots=slots, suffix=suffix
    )


def moved_kernel(
    meta, x, pk, pv, ck, cv, out, keys, values, row_meta, alive_rows, sems,
    *, local_rows, moved, steps, slots, groups
):
    span = x.shape[1]
    suffix = ck.shape[1]
    prefix = pk.shape[0] // slots
    step = pl.program_id(0)

    @pl.when(step == 0)
    def _():
        out[...] = jnp.zeros_like(out)

    copies = []
    for i in range(4):
        r = meta[4 * local_rows + step * 4 + i]
        for n, (source, target) in enumerate(((ck, keys), (cv, values))):
            copy = pltpu.make_async_copy(
                source.at[r], target.at[pl.ds(i * suffix, suffix)], sems.at[i, n]
            )
            copy.start()
            copies.append(copy)
        for n in range(3):
            row_meta[n, i * span : (i + 1) * span, :] = jnp.full(
                (span, HEAD_DIM), meta[n * local_rows + r], jnp.int32
            )
        alive_rows[i * span : (i + 1) * span, :] = jnp.full(
            (span, HEAD_DIM), meta[3 * local_rows + r].astype(jnp.float32), jnp.float32
        )
    q = x[...].reshape(4 * span, HEAD_DIM)
    shape = (4 * span, HEAD_DIM)
    lane, row = iota(shape, 1), iota(shape, 0)
    slot = row_meta[0]
    prompt_mask = lane < row_meta[1]
    cache_mask = ((lane // suffix) == ((row // span) % 2)) & ((lane % suffix) < row_meta[2])
    past = (lane % span) - groups * steps
    new_mask = ((lane // span) == (row // span)) & (past >= 0) & (past <= row % steps)
    prompt = pick_slot(matmul(q, pk[...], NT), slot, slots, prefix)
    new = matmul(q, q, NT)
    for copy in copies:
        copy.wait()
    cache = matmul(q, keys[...], NT)
    half = 2 * suffix
    top_half = row < 2 * span
    cache = jnp.where(top_half, cache[:, :half], cache[:, half:])
    wp, wn, wc = softmax_weights(prompt, new, cache, prompt_mask, new_mask, cache_mask)
    wc = jnp.concatenate(
        [jnp.where(top_half, wc, 0.0), jnp.where(top_half, 0.0, wc)], axis=1
    ).astype(jnp.bfloat16)
    wn = pltpu.roll(wn, steps, 1).astype(jnp.bfloat16)
    mixed = (
        matmul(spread_slot(wp, slot, slots), pv[...], NN)
        + matmul(wn, q, NN)
        + matmul(wc, values[...], NN)
    )
    mixed = (mixed * alive_rows[...]).astype(out.dtype)
    for i in range(4):
        out[meta[4 * local_rows + moved + 8 + step * 4 + i]] = mixed[i * span : (i + 1) * span]


def cross_kernel(cols, h_own, h_sib, w_own, w_sib, out):
    total = matmul(h_own[...], w_own[...], NN) + matmul(h_sib[...], w_sib[0], NN)
    out[...] = total.astype(out.dtype)


def base_kernel(cols, residual, h_own, h_sib, w_own, w_sib, out):
    total = matmul(h_own[...], w_own[...], NN) + matmul(h_sib[...], w_sib[0], NN)
    out[...] = total + residual[...].astype(jnp.float32)


def moved_heads(meta, ret, *, local_rows, moved, steps, groups):
    span = ret.shape[1]
    parts = []
    for first in range(0, moved, 4):
        x = jnp.concatenate(
            [ret[meta[4 * local_rows + moved + 8 + first + i]] for i in range(4)], axis=0
        )
        shape = (4 * steps, 4 * span)
        row, col = iota(shape, 0), iota(shape, 1)
        cols = []
        for h in range(groups):
            take = ((row // steps) == (col // span)) & ((col % span) == h * steps + row % steps)
            cols.append(matmul(take.astype(jnp.bfloat16), x, NN).astype(jnp.bfloat16))
        parts.append(jnp.concatenate(cols, axis=1))
    return jnp.concatenate(parts, axis=0) if len(parts) > 1 else parts[0]


def moved_cross_kernel(
    cols, meta, ret_own, ret_sib, w_here, w_there, w_sib, out, base, *, local_rows, moved, steps, groups
):
    options = dict(local_rows=local_rows, moved=moved, steps=steps, groups=groups)
    own = moved_heads(meta, ret_own, **options)
    sib = moved_heads(meta, ret_sib, **options)
    base[...] = matmul(own, w_here[...], NN) + matmul(sib, w_sib[0], NN)
    out[...] = (matmul(own, w_there[...], NN) + matmul(sib, w_sib[1], NN)).astype(out.dtype)


def write_rows(total, out, steps):
    for b in range(out.shape[0]):
        out[b] = total[b * steps : (b + 1) * steps].astype(out.dtype)


def first_final_kernel(base, recv, out):
    write_rows(base[...] + recv[...].astype(jnp.float32), out, out.shape[1])


def later_final_kernel(earlier, base, recv, out):
    write_rows(base[...] + recv[...].astype(jnp.float32), out, out.shape[1])


def moved_final_kernel(meta, earlier, residual, base, recv, out, before, after, sems, *, local_rows, moved, steps):
    rows = [meta[4 * local_rows + i] for i in range(moved)]
    copies = [
        pltpu.make_async_copy(residual.at[r], before.at[i], sems.at[i, 0]) for i, r in enumerate(rows)
    ]
    for copy in copies:
        copy.start()
    total = base[...] + recv[...].astype(jnp.float32)
    for copy in copies:
        copy.wait()
    for i in range(moved):
        after[i] = (
            total[i * steps : (i + 1) * steps] + before[i].astype(jnp.float32)
        ).astype(after.dtype)
    copies = [
        pltpu.make_async_copy(after.at[i], out.at[r], sems.at[i, 1]) for i, r in enumerate(rows)
    ]
    for copy in copies:
        copy.start()
    for copy in copies:
        copy.wait()


def body(
    residual,
    queries,
    new_keys,
    new_values,
    cache_keys,
    cache_values,
    cache_lengths,
    finished,
    partner,
    row_slot,
    fork_table,
    prompt_keys,
    prompt_values,
    prompt_lengths,
    out_proj,
):
    replicas = lax.axis_size("replica")
    tensors = lax.axis_size("tensor")
    me = lax.axis_index("replica")
    place = lax.axis_index("tensor")
    local_rows, steps, width = queries.shape
    groups = width // HEAD_DIM
    suffix = cache_keys.shape[1]
    held, prefix = prompt_keys.shape[:2]
    slots = fork_table.shape[1]
    moved = replicas // 2
    model = residual.shape[2]
    n = local_rows * steps
    span = 32
    dtype = queries.dtype
    fork = fork_table.reshape(-1)
    chunks = 4
    rows_chunk = local_rows // chunks
    nc = rows_chunk * steps

    if replicas <= 8:
        packed = pl.pallas_call(
            functools.partial(pack_kernel, replicas=replicas, slots=slots),
            out_shape=[jax.ShapeDtypeStruct((2 * prefix + span, HEAD_DIM), dtype)] * (replicas - 1),
            in_specs=[SMEM, SMEM, VMEM, VMEM, VMEM, ANY, ANY],
            out_specs=[ANY] * (replicas - 1),
            scratch_shapes=[
                pltpu.VMEM((replicas - 1, span, HEAD_DIM), dtype),
                pltpu.SMEM((replicas,), jnp.int32),
                pltpu.SemaphoreType.DMA((replicas - 1, 3)),
            ],
            compiler_params=params(),
            name="pack",
        )(fork, partner, queries, new_keys, new_values, prompt_keys, prompt_values)
        received = [
            lax.ppermute(packed[k - 1], "replica", [(i, (i + k) % replicas) for i in range(replicas)])
            for k in range(1, replicas)
        ]
    else:
        chosen = (fork_table // held) == me
        offsets = jnp.sum(jnp.where(chosen, fork_table % held, 0), axis=1)
        peer_of = partner // local_rows
        pairing = (peer_of[None, :] == jnp.arange(replicas, dtype=jnp.int32)[:, None]) & (
            peer_of[None, :] != me
        )
        row_of = jnp.sum(
            jnp.where(pairing, jnp.arange(local_rows, dtype=jnp.int32)[None, :], 0), axis=1
        )
        q = queries[row_of].reshape(replicas, steps, groups, HEAD_DIM).transpose(0, 2, 1, 3)
        q = q.reshape(replicas, groups * steps, HEAD_DIM)
        pad = jnp.zeros((replicas, span - (groups + 2) * steps, HEAD_DIM), dtype)
        block = jnp.concatenate(
            [prompt_keys[offsets], prompt_values[offsets], q, new_keys[row_of], new_values[row_of], pad],
            axis=1,
        )
        stacked = lax.all_to_all(block, "replica", split_axis=0, concat_axis=0, tiled=True)

    meta = pl.pallas_call(
        functools.partial(meta_kernel, slots=slots, local_rows=local_rows, moved=moved),
        out_shape=jax.ShapeDtypeStruct((4 * local_rows + 2 * (moved + 8),), jnp.int32),
        in_specs=[SMEM] * 6,
        out_specs=SMEM,
        name="meta",
    )(fork, partner, row_slot, prompt_lengths, cache_lengths, finished)

    def columns(index):
        return lax.dynamic_slice_in_dim(out_proj, index * model, model, axis=1)

    sibling = [(i, i ^ 1) for i in range(tensors)]
    across = [(i, i ^ 2) for i in range(tensors)]
    w_sib = lax.ppermute(jnp.stack([columns(place ^ 1), columns(place ^ 3)]), "tensor", sibling)

    q2 = queries.reshape(n, width)
    nk2 = new_keys.reshape(n, HEAD_DIM)
    nv2 = new_values.reshape(n, HEAD_DIM)
    ck2 = cache_keys.reshape(local_rows * suffix, HEAD_DIM)
    cv2 = cache_values.reshape(local_rows * suffix, HEAD_DIM)
    res2 = residual.reshape(n, model)

    scratch = [
        pltpu.VMEM((3, nc, HEAD_DIM), jnp.int32),
        pltpu.VMEM((nc, HEAD_DIM), jnp.float32),
        pltpu.VMEM((groups, nc, HEAD_DIM), jnp.float32),
        pltpu.VMEM((groups, nc, 2 * HEAD_DIM), jnp.bfloat16),
        pltpu.VMEM((groups, nc, HEAD_DIM), jnp.float32),
    ]
    sizes = dict(local_rows=local_rows, steps=steps, slots=slots, suffix=suffix)

    def block_specs(start):
        return [
            pl.BlockSpec((nc, width), lambda i: (i + start, 0)),
            pl.BlockSpec((nc, HEAD_DIM), lambda i: (i + start, 0)),
            pl.BlockSpec((nc, HEAD_DIM), lambda i: (i + start, 0)),
            pl.BlockSpec((rows_chunk * suffix, HEAD_DIM), lambda i: (i + start, 0)),
            pl.BlockSpec((rows_chunk * suffix, HEAD_DIM), lambda i: (i + start, 0)),
        ]

    def later(start, count, pk, pv):
        return pl.pallas_call(
            functools.partial(later_kernel, start=start, **sizes),
            grid=(count,),
            out_shape=jax.ShapeDtypeStruct((count * nc, width), dtype),
            in_specs=[SMEM] + block_specs(start) + [VMEM, VMEM],
            out_specs=pl.BlockSpec((nc, width), lambda i: (i, 0)),
            scratch_shapes=scratch,
            compiler_params=params(),
            name="attend",
        )(meta, q2, nk2, nv2, ck2, cv2, pk, pv)

    if replicas <= 8:
        h_first, pk, pv, moved_q = pl.pallas_call(
            functools.partial(first_kernel, replicas=replicas, moved=moved, **sizes),
            grid=(1,),
            out_shape=[
                jax.ShapeDtypeStruct((nc, width), dtype),
                jax.ShapeDtypeStruct((slots * prefix, HEAD_DIM), dtype),
                jax.ShapeDtypeStruct((slots * prefix, HEAD_DIM), dtype),
                jax.ShapeDtypeStruct((moved, span, HEAD_DIM), dtype),
            ],
            in_specs=[SMEM, SMEM] + block_specs(0) + [ANY] * (replicas + 1),
            out_specs=[VMEM] * 4,
            scratch_shapes=scratch
            + [pltpu.SemaphoreType.DMA((slots, 2)), pltpu.SemaphoreType.DMA((moved,))],
            compiler_params=params(),
            name="attend_first",
        )(fork, meta, q2, nk2, nv2, ck2, cv2, prompt_keys, prompt_values, *received)
    else:
        mine = stacked[fork_table[me] // held]
        pk = mine[:, :prefix].reshape(slots * prefix, HEAD_DIM)
        pv = mine[:, prefix : 2 * prefix].reshape(slots * prefix, HEAD_DIM)
        peers = lax.dynamic_slice_in_dim(meta, 4 * local_rows + moved + 8, moved)
        moved_q = stacked[peers][:, 2 * prefix :]
        h_first = later(0, 1, pk, pv)

    h_later = later(1, chunks - 1, pk, pv)
    back = pl.pallas_call(
        functools.partial(
            moved_kernel, local_rows=local_rows, moved=moved, steps=steps, slots=slots, groups=groups
        ),
        grid=(moved // 4,),
        out_shape=jax.ShapeDtypeStruct((replicas, span, HEAD_DIM), dtype),
        in_specs=[SMEM, pl.BlockSpec((4, span, HEAD_DIM), lambda i: (i, 0, 0)), VMEM, VMEM, ANY, ANY],
        out_specs=VMEM,
        scratch_shapes=[
            pltpu.VMEM((4 * suffix, HEAD_DIM), dtype),
            pltpu.VMEM((4 * suffix, HEAD_DIM), dtype),
            pltpu.VMEM((3, 4 * span, HEAD_DIM), jnp.int32),
            pltpu.VMEM((4 * span, HEAD_DIM), jnp.float32),
            pltpu.SemaphoreType.DMA((4, 2)),
        ],
        compiler_params=params(),
        name="attend_moved",
    )(meta, moved_q, pk, pv, cache_keys, cache_values)
    ret = lax.all_to_all(back, "replica", split_axis=0, concat_axis=0, tiled=True)

    cols = jnp.stack([place, place ^ 2]).astype(jnp.int32)

    def project(kernel, which, count, outs, extra=()):
        def call(h_own, h_sib, *more):
            rows = h_own.shape[0] // count
            grid_spec = pltpu.PrefetchScalarGridSpec(
                num_scalar_prefetch=1,
                grid=(count,),
                in_specs=list(extra)
                + [
                    pl.BlockSpec((rows, width), lambda i, c: (i, 0)),
                    pl.BlockSpec((rows, width), lambda i, c: (i, 0)),
                    pl.BlockSpec((width, model), lambda i, c: (0, c[which])),
                    pl.BlockSpec((1, width, model), lambda i, c: (which, 0, 0)),
                ],
                out_specs=pl.BlockSpec((rows, model), lambda i, c: (i, 0)),
            )
            return pl.pallas_call(
                kernel,
                grid_spec=grid_spec,
                out_shape=jax.ShapeDtypeStruct((h_own.shape[0], model), outs),
                compiler_params=params(),
                name="project",
            )(cols, *more, h_own, h_sib, out_proj, w_sib)

        return call

    cross = project(cross_kernel, 1, 1, dtype)
    s_first = lax.ppermute(h_first, "tensor", sibling)
    got = [lax.ppermute(cross(h_first, s_first), "tensor", across)]
    s_later = lax.ppermute(h_later, "tensor", sibling)
    for c in range(1, chunks):
        part = slice((c - 1) * nc, c * nc)
        got.append(lax.ppermute(cross(h_later[part], s_later[part]), "tensor", across))

    def base_of(first, h_own, h_sib, count):
        spec = pl.BlockSpec((nc, model), lambda i, c: (i + first, 0))
        return project(base_kernel, 0, count, jnp.float32, (spec,))(h_own, h_sib, res2)

    base_first = base_of(0, h_first, s_first, 1)
    base_later = base_of(1, h_later, s_later, chunks - 1)

    ret_sib = lax.ppermute(ret, "tensor", sibling)
    whole = lambda shape: pl.BlockSpec(shape, lambda i, c, m: (0,) * len(shape))
    cross_moved, base_moved = pl.pallas_call(
        functools.partial(
            moved_cross_kernel, local_rows=local_rows, moved=moved, steps=steps, groups=groups
        ),
        grid_spec=pltpu.PrefetchScalarGridSpec(
            num_scalar_prefetch=2,
            grid=(1,),
            in_specs=[
                whole(ret.shape),
                whole(ret.shape),
                pl.BlockSpec((width, model), lambda i, c, m: (0, c[0])),
                pl.BlockSpec((width, model), lambda i, c, m: (0, c[1])),
                whole(w_sib.shape),
            ],
            out_specs=[whole((moved * steps, model))] * 2,
        ),
        out_shape=[
            jax.ShapeDtypeStruct((moved * steps, model), dtype),
            jax.ShapeDtypeStruct((moved * steps, model), jnp.float32),
        ],
        compiler_params=params(),
        name="project_moved",
    )(cols, meta, ret, ret_sib, out_proj, out_proj, w_sib)
    got_moved = lax.ppermute(cross_moved, "tensor", across)

    shape = jax.ShapeDtypeStruct(residual.shape, residual.dtype)
    out = None
    for c in range(chunks):
        base, index = (base_first, 0) if c == 0 else (base_later, c - 1)
        specs = [
            pl.BlockSpec((nc, model), lambda i, index=index: (index, 0)),
            pl.BlockSpec((nc, model), lambda i: (0, 0)),
        ]
        out_spec = pl.BlockSpec((rows_chunk, steps, model), lambda i, c=c: (c, 0, 0))
        if out is None:
            out = pl.pallas_call(
                first_final_kernel,
                grid=(1,),
                in_specs=specs,
                out_specs=out_spec,
                out_shape=shape,
                compiler_params=params(),
                name="finish",
            )(base, got[c])
        else:
            out = pl.pallas_call(
                later_final_kernel,
                grid=(1,),
                in_specs=[ANY] + specs,
                out_specs=out_spec,
                out_shape=shape,
                input_output_aliases={0: 0},
                compiler_params=params(),
                name="finish",
            )(out, base, got[c])
    return pl.pallas_call(
        functools.partial(moved_final_kernel, local_rows=local_rows, moved=moved, steps=steps),
        in_specs=[SMEM, ANY, ANY, VMEM, VMEM],
        out_specs=ANY,
        out_shape=shape,
        input_output_aliases={1: 0},
        scratch_shapes=[
            pltpu.VMEM((moved, steps, model), dtype),
            pltpu.VMEM((moved, steps, model), dtype),
            pltpu.SemaphoreType.DMA((moved, 2)),
        ],
        compiler_params=params(),
        name="finish_moved",
    )(meta, out, residual, base_moved, got_moved)


def solution(mesh):
    rows = P("replica", None, "tensor")
    in_specs = (rows,) * 6 + (P(), P(), P("replica"), P(), P(), rows, rows, P(), P("tensor", None))
    return jax.shard_map(body, mesh=mesh, in_specs=in_specs, out_specs=rows, check_vma=False)
```

```python
import functools
import math

import jax
import jax.numpy as jnp
from jax import lax
from jax.experimental import pallas as pl
from jax.experimental.pallas import tpu as pltpu
from jax.sharding import PartitionSpec as P

HEAD_DIM = 128
LOWEST = -1e30
EXP2_SCALE = math.log2(math.e) / math.sqrt(HEAD_DIM)
VMEM_BYTES = 32 * 1024 * 1024
BLOCK = 32
NT = (((1,), (1,)), ((), ()))
NN = (((1,), (0,)), ((), ()))

ANY = pl.BlockSpec(memory_space=pl.ANY)
SMEM = pl.BlockSpec(memory_space=pltpu.SMEM)
VMEM = pl.BlockSpec(memory_space=pltpu.VMEM)


def params(side_effects=False):
    return pltpu.CompilerParams(vmem_limit_bytes=VMEM_BYTES, has_side_effects=side_effects)


def matmul(a, b, dims):
    return lax.dot_general(a, b, dims, preferred_element_type=jnp.float32)


def in_hbm(*arrays):
    return [pltpu.with_memory_space_constraint(x, pltpu.HBM) for x in arrays]


def iota(shape, dim):
    return lax.broadcasted_iota(jnp.int32, shape, dim)


def load(pairs, sem):
    copies = [pltpu.make_async_copy(a, b, sem.at[i]) for i, (a, b) in enumerate(pairs)]
    for copy in copies:
        copy.start()

    def wait():
        for copy in copies:
            copy.wait()

    return wait


def list_pairs(row_of, pairs, me, replicas, moved):
    count = jnp.int32(0)
    for j in range(replicas):
        pairs[count] = row_of[j]
        pairs[moved + 1 + count] = j
        count = jnp.minimum(count + jnp.where((row_of[j] >= 0) & (j != me), 1, 0), moved)


def find_pairs(partner, row_of, replicas, local_rows):
    for j in range(replicas):
        row_of[j] = -1

    def note(r, carry):
        row_of[lax.div(partner[r], local_rows)] = r
        return carry

    lax.fori_loop(0, local_rows, note, 0, unroll=8)


def pairs_kernel(partner, pairs, row_of, *, replicas, local_rows, moved):
    find_pairs(partner, row_of, replicas, local_rows)
    list_pairs(row_of, pairs, lax.axis_index("replica"), replicas, moved)


def pack_kernel(
    fork, partner, queries, new_keys, new_values, keys, values, *rest, replicas, slots, moved
):
    outs = rest[: replicas - 1]
    pairs, qv, nkv, nvv, row_of, sems, row_sems = rest[replicas - 1 :]
    me = lax.axis_index("replica")
    held, prefix = keys.shape[0], keys.shape[1]
    local_rows = queries.shape[0]
    groups = queries.shape[2] // HEAD_DIM
    copies = []
    for k in range(1, replicas):
        peer = lax.rem(me + k, replicas)
        offset = jnp.int32(0)
        for s in range(slots):
            prompt = fork[s, peer]
            offset = jnp.where(lax.div(prompt, held) == me, lax.rem(prompt, held), offset)
        for n, source in enumerate((keys, values)):
            copy = pltpu.make_async_copy(
                source.at[offset], outs[k - 1].at[pl.ds(n * prefix, prefix)], sems.at[k - 1, n]
            )
            copy.start()
            copies.append(copy)
    find_pairs(partner, row_of, replicas, local_rows)
    rows = [jnp.maximum(row_of[lax.rem(me + k, replicas)], 0) for k in range(1, replicas)]
    fetched = [
        load([(queries.at[r], qv.at[i]), (new_keys.at[r], nkv.at[i]), (new_values.at[r], nvv.at[i])], row_sems.at[i])
        for i, r in enumerate(rows)
    ]
    for k in range(1, replicas):
        fetched[k - 1]()
        q = qv[k - 1].astype(jnp.float32)
        parts = [q[:, h * HEAD_DIM : (h + 1) * HEAD_DIM] for h in range(groups)]
        parts += [nkv[k - 1].astype(jnp.float32), nvv[k - 1].astype(jnp.float32)]
        pad = outs[k - 1].shape[0] - 2 * prefix - sum(p.shape[0] for p in parts)
        parts += [jnp.zeros((pad, HEAD_DIM), jnp.float32)]
        outs[k - 1][2 * prefix :, :] = jnp.concatenate(parts, axis=0).astype(outs[k - 1].dtype)
    list_pairs(row_of, pairs, me, replicas, moved)
    for copy in copies:
        copy.wait()


def softmax_weights(prompt, new, cache, prompt_mask, new_mask, cache_mask):
    prompt = jnp.where(prompt_mask, prompt, LOWEST)
    new = jnp.where(new_mask, new, LOWEST)
    cache = jnp.where(cache_mask, cache, LOWEST)
    top = jnp.max(jnp.maximum(jnp.maximum(prompt, new), cache), axis=1, keepdims=True)
    prompt = jnp.exp2((prompt - top) * EXP2_SCALE)
    new = jnp.exp2((new - top) * EXP2_SCALE)
    cache = jnp.exp2((cache - top) * EXP2_SCALE)
    inverse = 1.0 / jnp.sum(prompt + new + cache, axis=1, keepdims=True)
    return prompt * inverse, new * inverse, cache * inverse


def pick_slot(scores, slot, slots, prefix):
    picked = scores[:, :prefix]
    for s in range(1, slots):
        picked = jnp.where(slot == s, scores[:, s * prefix : (s + 1) * prefix], picked)
    return picked


def spread_slot(weights, slot, slots):
    return jnp.concatenate(
        [jnp.where(slot == s, weights, 0.0).astype(jnp.bfloat16) for s in range(slots)], axis=1
    )


def fill_meta(lookup, local_row, span, row_meta, alive_rows):
    row_slot, fork, prompt_lengths, cache_lengths, finished, me, slots, local_rows = lookup
    g = me * local_rows + local_row
    slot = row_slot[g]
    values = (slot, prompt_lengths[fork[slot, me]], cache_lengths[g])
    size = span.stop - span.start
    for i, value in enumerate(values):
        row_meta[i, span, :] = jnp.full((size, HEAD_DIM), value, jnp.int32)
    alive_rows[span, :] = jnp.full((size, HEAD_DIM), 1 - finished[g], jnp.int32).astype(jnp.float32)


def attend_scores(q, ck, cache_scores, *, steps, suffix):
    n = q.shape[0]
    groups = q.shape[1] // HEAD_DIM
    keys_sub = 4 * suffix
    half = 2 * suffix
    for sub in range(n // 16):
        r0 = sub * 16
        qs = jnp.concatenate(
            [q[r0 : r0 + 16, h * HEAD_DIM : (h + 1) * HEAD_DIM] for h in range(groups)], axis=0
        )
        s = matmul(qs, ck[sub * keys_sub : (sub + 1) * keys_sub, :], NT)
        for h in range(groups):
            cache_scores[h, r0 : r0 + 8, :] = s[16 * h : 16 * h + 8, :half]
            cache_scores[h, r0 + 8 : r0 + 16, :] = s[16 * h + 8 : 16 * h + 16, half:]


def attend_block(
    q, nk, nv, cv, pk, pv, heads, row_meta, alive_rows, cache_scores, weights, cache_weights, mixed,
    *, steps, slots, suffix
):
    n = q.shape[0]
    groups = q.shape[1] // HEAD_DIM
    prefix = pk.shape[0] // slots
    keys_sub = 4 * suffix
    half = 2 * suffix
    shape = (n, HEAD_DIM)
    lane, row = iota(shape, 1), iota(shape, 0)
    cache_own = (lane // suffix) == ((row % 8) // steps)
    cache_lane = jnp.where(cache_own, lane % suffix, suffix)
    new_mask = ((lane // steps) == (row // steps)) & ((lane % steps) <= (row % steps))
    first_half = (row % 16) < 8
    slot = row_meta[0]
    prompt_mask = lane < row_meta[1]
    cache_mask = cache_lane < row_meta[2]
    q_all = jnp.concatenate([q[:, h * HEAD_DIM : (h + 1) * HEAD_DIM] for h in range(groups)], axis=0)
    prompt_all = matmul(q_all, pk[...], NT)
    new_all = matmul(q_all, nk[...], NT)
    for h in range(groups):
        part = slice(h * n, (h + 1) * n)
        prompt = pick_slot(prompt_all[part], slot, slots, prefix)
        wp, wn, wc = softmax_weights(
            prompt, new_all[part], cache_scores[h], prompt_mask, new_mask, cache_mask
        )
        cache_weights[h, :, :half] = jnp.where(first_half, wc, 0.0).astype(jnp.bfloat16)
        cache_weights[h, :, half:] = jnp.where(first_half, 0.0, wc).astype(jnp.bfloat16)
        weights[part, : slots * prefix] = spread_slot(wp, slot, slots)
        weights[part, slots * prefix :] = wn.astype(jnp.bfloat16)
    mixed[...] = matmul(weights[:, : slots * prefix], pv[...], NN) + matmul(
        weights[:, slots * prefix :], nv[...], NN
    )
    for sub in range(n // 16):
        r0 = sub * 16
        w = jnp.concatenate([cache_weights[h, r0 : r0 + 16, :] for h in range(groups)], axis=0)
        o = matmul(w, cv[sub * keys_sub : (sub + 1) * keys_sub, :], NN)
        for h in range(groups):
            total = mixed[h * n + r0 : h * n + r0 + 16, :] + o[16 * h : 16 * h + 16, :]
            heads[r0 : r0 + 16, h * HEAD_DIM : (h + 1) * HEAD_DIM] = (
                total * alive_rows[r0 : r0 + 16, :]
            ).astype(heads.dtype)


def moved_block(x, pk, pv, keys, values, slot, plen, clen, alive, wait, *, steps, slots, groups, span, suffix):
    prefix = pk.shape[0] // slots
    shape = (4 * span, HEAD_DIM)
    lane, row = iota(shape, 1), iota(shape, 0)
    prompt_mask = lane < plen
    cache_mask = ((lane // suffix) == ((row // span) % 2)) & ((lane % suffix) < clen)
    past = (lane % span) - groups * steps
    new_mask = ((lane // span) == (row // span)) & (past >= 0) & (past <= row % steps)
    prompt = pick_slot(matmul(x, pk[...], NT), slot, slots, prefix)
    new = matmul(x, x, NT)
    wait()
    cache = matmul(x, keys[...], NT)
    half = 2 * suffix
    top_half = row < 2 * span
    cache = jnp.where(top_half, cache[:, :half], cache[:, half:])
    wp, wn, wc = softmax_weights(prompt, new, cache, prompt_mask, new_mask, cache_mask)
    wc = jnp.concatenate(
        [jnp.where(top_half, wc, 0.0), jnp.where(top_half, 0.0, wc)], axis=1
    ).astype(jnp.bfloat16)
    wn = pltpu.roll(wn, steps, 1).astype(jnp.bfloat16)
    mixed = (
        matmul(spread_slot(wp, slot, slots), pv[...], NN)
        + matmul(wn, x, NN)
        + matmul(wc, values[...], NN)
    )
    mixed = (mixed * alive).astype(jnp.bfloat16)
    row, col = iota((4 * steps, 4 * span), 0), iota((4 * steps, 4 * span), 1)
    cols = []
    for h in range(groups):
        take = ((row // steps) == (col // span)) & ((col % span) == h * steps + row % steps)
        cols.append(matmul(take.astype(jnp.bfloat16), mixed, NN).astype(jnp.bfloat16))
    return jnp.concatenate(cols, axis=1)


def attend_kernel(
    cols, fork, pairs, row_slot, prompt_lengths, cache_lengths, finished, q, nk, nv, ck, cv, own_keys, own_values,
    w_own, w_sib, *rest, stacked, replicas, slots, moved, local_rows, steps, suffix, span
):
    count = 1 if stacked else replicas - 1
    recvs, rest = rest[:count], rest[count:]
    heads, w_here, w_there = rest[:3]
    pk, pv, qv, nkv, nvv, ckv, cvv, x, keys, values = rest[3:13]
    row_meta, alive_rows, moved_meta, moved_alive, cache_scores, weights, cache_weights, mixed = rest[13:21]
    local_sems, sems, moved_sems, cache_sems, w_sems = rest[21:]
    me = lax.axis_index("replica")
    held, prefix = own_keys.shape[0], own_keys.shape[1]
    blocks, n = qv.shape[:2]
    groups = qv.shape[2] // HEAD_DIM
    rows = n // steps
    local = (q, nk, nv, ck, cv)
    buffers = [[v.at[i] for v in (qv, nkv, nvv, ckv, cvv)] for i in range(blocks)]
    spans = [(pl.ds(i * n, n), pl.ds(i * rows * suffix, rows * suffix)) for i in range(blocks)]
    scores_ready = [
        load([(q.at[a], qv.at[i]), (ck.at[b], ckv.at[i])], local_sems.at[i, 0]) for i, (a, b) in enumerate(spans)
    ]
    for s in range(slots):
        prompt = fork[s, me]
        owner = lax.div(prompt, held)
        offset = lax.rem(prompt, held)
        targets = (pk.at[pl.ds(s * prefix, prefix)], pv.at[pl.ds(s * prefix, prefix)])
        if stacked:
            for i in range(2):
                pltpu.make_async_copy(
                    recvs[0].at[owner, pl.ds(i * prefix, prefix)], targets[i], sems.at[s, i]
                ).start()
            continue
        k = lax.rem(me - owner + replicas, replicas)

        @pl.when(k == 0)
        def _():
            pltpu.make_async_copy(own_keys.at[offset], targets[0], sems.at[s, 0]).start()
            pltpu.make_async_copy(own_values.at[offset], targets[1], sems.at[s, 1]).start()

        for kk in range(1, replicas):

            @pl.when(k == kk)
            def _():
                for i in range(2):
                    pltpu.make_async_copy(
                        recvs[kk - 1].at[pl.ds(i * prefix, prefix)], targets[i], sems.at[s, i]
                    ).start()

    for i in range(moved):
        peer = pairs[moved + 1 + i]
        if stacked:
            pltpu.make_async_copy(
                recvs[0].at[peer, pl.ds(2 * prefix, span)], x.at[pl.ds(i * span, span)], moved_sems.at[i]
            ).start()
        else:
            k = lax.rem(me - peer + replicas, replicas)
            for kk in range(1, replicas):

                @pl.when(k == kk)
                def _():
                    pltpu.make_async_copy(
                        recvs[kk - 1].at[pl.ds(2 * prefix, span)],
                        x.at[pl.ds(i * span, span)],
                        moved_sems.at[i],
                    ).start()

    cache_copies = []
    for i in range(moved):
        r = pairs[i]
        for j, (source, target) in enumerate(((ck, keys), (cv, values))):
            copy = pltpu.make_async_copy(
                source.at[pl.ds(pl.multiple_of(r * suffix, suffix), suffix)],
                target.at[pl.ds(i * suffix, suffix)],
                cache_sems.at[i, j],
            )
            copy.start()
            cache_copies.append(copy)
    lookup = (row_slot, fork, prompt_lengths, cache_lengths, finished, me, slots, local_rows)
    for i in range(moved):
        fill_meta(lookup, pairs[i], slice(i * span, (i + 1) * span), moved_meta, moved_alive)

    rest_ready = [
        load([(nk.at[a], nkv.at[i]), (nv.at[a], nvv.at[i]), (cv.at[b], cvv.at[i])], local_sems.at[i, 1])
        for i, (a, b) in enumerate(spans)
    ]
    width, model = w_own.shape[0], w_there.shape[1]
    weights_ready = load(
        [
            (w.at[:, pl.ds(pl.multiple_of(cols[i] * model, HEAD_DIM), model)], target.at[pl.ds(j * width, width)])
            for i, target in enumerate((w_here, w_there))
            for j, w in enumerate((w_own, w_sib))
        ],
        w_sems,
    )
    for b in range(local_rows):
        i, at = b // rows, b % rows
        fill_meta(lookup, b, slice(at * steps, (at + 1) * steps), row_meta.at[i], alive_rows.at[i])
    def wait_prompts():
        for s in range(slots):
            for i, target in enumerate((pk, pv)):
                pltpu.make_async_copy(
                    own_keys.at[0], target.at[pl.ds(s * prefix, prefix)], sems.at[s, i]
                ).wait()

    sizes = dict(steps=steps, suffix=suffix)
    for i in range(blocks):
        scores_ready[i]()
        attend_scores(qv.at[i], ckv.at[i], cache_scores.at[i], **sizes)
    wait_prompts()
    for ready in rest_ready:
        ready()
    for i in range(blocks):
        attend_block(
            qv.at[i], nkv.at[i], nvv.at[i], cvv.at[i], pk, pv, heads.at[pl.ds(i * n, n)], row_meta.at[i],
            alive_rows.at[i], cache_scores.at[i], weights.at[i], cache_weights.at[i], mixed.at[i],
            slots=slots, **sizes,
        )
    for i in range(moved):
        pltpu.make_async_copy(
            own_keys.at[0, pl.ds(0, span)], x.at[pl.ds(i * span, span)], moved_sems.at[i]
        ).wait()

    def wait_caches():
        for copy in cache_copies:
            copy.wait()

    first = blocks * n
    for g in range(moved // 4):
        part = slice(g * 4 * span, (g + 1) * 4 * span)
        kpart = slice(g * 4 * suffix, (g + 1) * 4 * suffix)
        heads[first + g * 4 * steps : first + (g + 1) * 4 * steps, :] = moved_block(
            x[part, :], pk, pv, keys.at[kpart], values.at[kpart],
            moved_meta[0, part, :], moved_meta[1, part, :], moved_meta[2, part, :], moved_alive[part, :],
            wait_caches if g == 0 else (lambda: None),
            steps=steps, slots=slots, groups=groups, span=span, suffix=suffix,
        )
    weights_ready()


def project_kernel(h_own, h_sib, weights, out, moved_out):
    rows = out.shape[0]
    total = matmul(jnp.concatenate([h_own[...], h_sib[...]], axis=1), weights[...], NN)
    out[...] = total[:rows].astype(out.dtype)
    moved_out[...] = total[rows:].astype(out.dtype)


def base_kernel(h_own, h_sib, weights, residual, after, out, moved_out):
    rows = out.shape[0]
    steps = residual.shape[1]
    total = matmul(jnp.concatenate([h_own[...], h_sib[...]], axis=1), weights[...], NN)
    moved_out[...] = total[rows:]
    for b in range(rows // steps):
        part = slice(b * steps, (b + 1) * steps)
        out[part, :] = total[part] + residual[b].astype(jnp.float32)


def moved_sum_kernel(pairs, base, recv, *outs, moved, steps, replicas, split):
    me = lax.axis_index("replica")
    total = base[...] + recv[...].astype(jnp.float32)
    for i in range(moved):
        peer = pairs[moved + 1 + i]
        value = total[i * steps : (i + 1) * steps, :]
        if split:
            k = jnp.bitwise_xor(me, peer)
            place = 2 * lax.rem(lax.div(k, 2), 2) + lax.div(k, 4)

            @pl.when(lax.rem(k, 2) == 0)
            def _():
                outs[0][place] = value

            @pl.when(lax.rem(k, 2) == 1)
            def _():
                outs[1][place] = value

        else:
            outs[0][peer] = value


def finish_kernel(pairs, base, recv, residual, *rest, moved, replicas, split):
    backs, (out, branch, before, sems) = rest[:-4], rest[-4:]
    me = lax.axis_index("replica")
    step = pl.program_id(0)
    rows, steps = out.shape[:2]

    @pl.when(step == 0)
    def _():
        for i in range(moved):
            peer = pairs[moved + 1 + i]
            pltpu.make_async_copy(residual.at[pairs[i]], before.at[i], sems.at[i, 0]).start()
            if split:
                k = jnp.bitwise_xor(me, peer)
                places = {1: (0, 0), 2: (1, 0), 3: (1, 2), 4: (2, 0), 5: (2, 1), 6: (2, 2), 7: (2, 3)}
                for d, (which, index) in places.items():

                    @pl.when(k == d)
                    def _():
                        pltpu.make_async_copy(backs[which].at[index], branch.at[i], sems.at[i, 1]).start()

            else:
                pltpu.make_async_copy(backs[0].at[peer], branch.at[i], sems.at[i, 1]).start()

    part = pl.ds(pl.multiple_of(step * rows * steps, rows * steps), rows * steps)
    total = base[part, :] + recv[part, :].astype(jnp.float32)
    for b in range(rows):
        out[b] = total[b * steps : (b + 1) * steps].astype(out.dtype)

    @pl.when(step == 0)
    def _():
        for i in range(moved):
            pltpu.make_async_copy(residual.at[0], before.at[i], sems.at[i, 0]).wait()
            pltpu.make_async_copy(backs[0].at[0], branch.at[i], sems.at[i, 1]).wait()

    for i in range(moved):
        r = pairs[i]

        @pl.when(lax.div(r, rows) == step)
        def _():
            out[lax.rem(r, rows)] = (branch[i] + before[i].astype(jnp.float32)).astype(out.dtype)


def exchange_pack(
    fork, partner, row_slot, queries, new_keys, new_values, fork_table, prompt_keys, prompt_values, span, moved
):
    replicas = lax.axis_size("replica")
    me = lax.axis_index("replica")
    local_rows, steps, width = queries.shape
    groups = width // HEAD_DIM
    held, prefix = prompt_keys.shape[:2]
    dtype = queries.dtype
    pairs_shape = jax.ShapeDtypeStruct((2 * (moved + 1),), jnp.int32)
    if replicas <= 8:
        *packed, pairs = pl.pallas_call(
            functools.partial(pack_kernel, replicas=replicas, slots=fork_table.shape[1], moved=moved),
            out_shape=[pltpu.VMEM((2 * prefix + span, HEAD_DIM), dtype)] * (replicas - 1) + [pairs_shape],
            in_specs=[SMEM, SMEM] + [ANY] * 5,
            out_specs=[VMEM] * (replicas - 1) + [SMEM],
            scratch_shapes=[
                pltpu.VMEM((replicas - 1, steps, width), dtype),
                pltpu.VMEM((replicas - 1, steps, HEAD_DIM), dtype),
                pltpu.VMEM((replicas - 1, steps, HEAD_DIM), dtype),
                pltpu.SMEM((replicas,), jnp.int32),
                pltpu.SemaphoreType.DMA((replicas - 1, 2)),
                pltpu.SemaphoreType.DMA((replicas - 1, 3)),
            ],
            compiler_params=params(),
            name="pack",
        )(fork, partner, *in_hbm(queries, new_keys, new_values, prompt_keys, prompt_values))
        received = [
            lax.ppermute(packed[k - 1], "replica", [(i, (i + k) % replicas) for i in range(replicas)])
            for k in range(1, replicas)
        ]
        return received, pairs
    chosen = (fork_table // held) == me
    offsets = jnp.sum(jnp.where(chosen, fork_table % held, 0), axis=1)
    peer_of = partner // local_rows
    pairing = (peer_of[None, :] == jnp.arange(replicas, dtype=jnp.int32)[:, None]) & (
        peer_of[None, :] != me
    )
    row_of = jnp.sum(jnp.where(pairing, jnp.arange(local_rows, dtype=jnp.int32)[None, :], 0), axis=1)
    q = queries[row_of].reshape(replicas, steps, groups, HEAD_DIM).transpose(0, 2, 1, 3)
    q = q.reshape(replicas, groups * steps, HEAD_DIM)
    pad = jnp.zeros((replicas, span - (groups + 2) * steps, HEAD_DIM), dtype)
    block = jnp.concatenate(
        [prompt_keys[offsets], prompt_values[offsets], q, new_keys[row_of], new_values[row_of], pad], axis=1
    )
    pairs = pl.pallas_call(
        functools.partial(pairs_kernel, replicas=replicas, local_rows=local_rows, moved=moved),
        out_shape=pairs_shape,
        in_specs=[SMEM],
        out_specs=SMEM,
        scratch_shapes=[pltpu.SMEM((replicas,), jnp.int32)],
        name="pairs",
    )(partner)
    return [lax.all_to_all(block, "replica", split_axis=0, concat_axis=0, tiled=True)], pairs


def body(
    residual,
    queries,
    new_keys,
    new_values,
    cache_keys,
    cache_values,
    cache_lengths,
    finished,
    partner,
    row_slot,
    fork_table,
    prompt_keys,
    prompt_values,
    prompt_lengths,
    out_proj,
):
    replicas = lax.axis_size("replica")
    tensors = lax.axis_size("tensor")
    place = lax.axis_index("tensor")
    local_rows, steps, width = queries.shape
    groups = width // HEAD_DIM
    suffix = cache_keys.shape[1]
    held, prefix = prompt_keys.shape[:2]
    slots = fork_table.shape[1]
    moved = replicas // 2
    stacked = replicas > 8
    model = residual.shape[2]
    n = local_rows * steps
    span = 32
    dtype = queries.dtype
    fork = fork_table.T
    sibling = [(i, i ^ 1) for i in range(tensors)]
    across = [(i, i ^ 2) for i in range(tensors)]

    received, pairs = exchange_pack(
        fork, partner, row_slot, queries, new_keys, new_values, fork_table, prompt_keys, prompt_values, span, moved
    )
    w_sib = lax.ppermute(out_proj, "tensor", sibling)
    local = (
        queries.reshape(n, width),
        new_keys.reshape(n, HEAD_DIM),
        new_values.reshape(n, HEAD_DIM),
        cache_keys.reshape(local_rows * suffix, HEAD_DIM),
        cache_values.reshape(local_rows * suffix, HEAD_DIM),
    )
    sizes = dict(local_rows=local_rows, steps=steps, slots=slots, suffix=suffix)
    lookup = (row_slot, prompt_lengths, cache_lengths, finished)

    dma = lambda *shape: pltpu.SemaphoreType.DMA(shape)
    blocks = local_rows // BLOCK
    nb = BLOCK * steps
    assert nb == HEAD_DIM
    cols = jnp.stack([place, place ^ 2]).astype(jnp.int32)
    heads, w_here, w_there = pl.pallas_call(
        functools.partial(attend_kernel, stacked=stacked, replicas=replicas, moved=moved, span=span, **sizes),
        out_shape=[
            pltpu.VMEM(((local_rows + moved) * steps, width), dtype),
            pltpu.VMEM((2 * width, model), dtype),
            pltpu.VMEM((2 * width, model), dtype),
        ],
        in_specs=[SMEM] * 7 + [ANY] * (9 + len(received)),
        out_specs=[VMEM] * 3,
        scratch_shapes=[
            pltpu.VMEM((slots * prefix, HEAD_DIM), dtype),
            pltpu.VMEM((slots * prefix, HEAD_DIM), dtype),
            pltpu.VMEM((blocks, nb, width), dtype),
            pltpu.VMEM((blocks, nb, HEAD_DIM), dtype),
            pltpu.VMEM((blocks, nb, HEAD_DIM), dtype),
            pltpu.VMEM((blocks, BLOCK * suffix, HEAD_DIM), dtype),
            pltpu.VMEM((blocks, BLOCK * suffix, HEAD_DIM), dtype),
            pltpu.VMEM((moved * span, HEAD_DIM), dtype),
            pltpu.VMEM((moved * suffix, HEAD_DIM), dtype),
            pltpu.VMEM((moved * suffix, HEAD_DIM), dtype),
            pltpu.VMEM((blocks, 3, nb, HEAD_DIM), jnp.int32),
            pltpu.VMEM((blocks, nb, HEAD_DIM), jnp.float32),
            pltpu.VMEM((3, moved * span, HEAD_DIM), jnp.int32),
            pltpu.VMEM((moved * span, HEAD_DIM), jnp.float32),
            pltpu.VMEM((blocks, groups, nb, HEAD_DIM), jnp.float32),
            pltpu.VMEM((blocks, groups * nb, slots * prefix + HEAD_DIM), jnp.bfloat16),
            pltpu.VMEM((blocks, groups, nb, 2 * HEAD_DIM), jnp.bfloat16),
            pltpu.VMEM((blocks, groups * nb, HEAD_DIM), jnp.float32),
            dma(blocks, 2, 3),
            dma(slots, 2),
            dma(moved),
            dma(moved, 2),
            dma(4),
        ],
        compiler_params=params(),
        name="attend",
    )(cols, fork, pairs, *lookup, *in_hbm(*local, prompt_keys, prompt_values, out_proj), w_sib, *received)

    sib = lax.ppermute(heads, "tensor", sibling)
    m = moved * steps

    def call(kernel, kind, name, *operands, specs):
        return pl.pallas_call(
            kernel,
            out_shape=[pltpu.VMEM((n, model), kind), pltpu.VMEM((m, model), kind)],
            in_specs=specs,
            out_specs=[VMEM, VMEM],
            compiler_params=params(),
            name=name,
        )(*operands)

    crossed, crossed_moved = call(
        project_kernel, dtype, "project", heads, sib, w_there, specs=[VMEM] * 3
    )
    got_moved = lax.ppermute(crossed_moved, "tensor", across)
    got = lax.ppermute(crossed, "tensor", across)
    base, base_moved = call(
        base_kernel, jnp.float32, "base", heads, sib, w_here, residual, crossed, specs=[VMEM] * 4 + [ANY]
    )

    back_shape = pltpu.VMEM((replicas if stacked else 4, steps, model), jnp.float32)
    back = pl.pallas_call(
        functools.partial(moved_sum_kernel, moved=moved, steps=steps, replicas=replicas, split=not stacked),
        out_shape=[back_shape] * (1 if stacked else 2),
        in_specs=[SMEM, VMEM, VMEM],
        out_specs=[VMEM] * (1 if stacked else 2),
        compiler_params=params(),
        name="moved_sum",
    )(pairs, base_moved, got_moved)
    if stacked:
        backs = [lax.all_to_all(back[0], "replica", split_axis=0, concat_axis=0, tiled=True)]
    else:
        flip = lambda x, bit: lax.ppermute(x, "replica", [(i, i ^ bit) for i in range(replicas)])
        kept = back[0]
        one = flip(back[1], 1)
        two = flip(jnp.concatenate([kept[2:], one[2:]]), 2)
        four = flip(jnp.concatenate([kept[1:2], one[1:2], two[1:2], two[3:4]]), 4)
        backs = [one, two, four]

    return pl.pallas_call(
        functools.partial(finish_kernel, moved=moved, replicas=replicas, split=not stacked),
        grid=(blocks,),
        in_specs=[SMEM, VMEM, VMEM, ANY] + [ANY] * len(backs),
        out_specs=pl.BlockSpec((BLOCK, steps, model), lambda i: (i, 0, 0)),
        out_shape=jax.ShapeDtypeStruct(residual.shape, residual.dtype),
        scratch_shapes=[
            pltpu.VMEM((moved, steps, model), jnp.float32),
            pltpu.VMEM((moved, steps, model), dtype),
            dma(moved, 2),
        ],
        compiler_params=params(),
        name="finish",
    )(pairs, base, got, *in_hbm(residual), *backs)


def solution(mesh):
    rows = P("replica", None, "tensor")
    in_specs = (rows,) * 6 + (P(), P(), P("replica"), P(), P(), rows, rows, P(), P("tensor", None))
    return jax.shard_map(body, mesh=mesh, in_specs=in_specs, out_specs=rows, check_vma=False)
```

```python
import functools
import math

import jax
import jax.numpy as jnp
from jax import lax
from jax.experimental import pallas as pl
from jax.experimental.pallas import tpu as pltpu
from jax.sharding import PartitionSpec as P

HEAD_DIM = 128
LOWEST = -1e30
EXP2_SCALE = math.log2(math.e) / math.sqrt(HEAD_DIM)
VMEM_BYTES = 32 * 1024 * 1024
BLOCK = 32
NT = (((1,), (1,)), ((), ()))
NN = (((1,), (0,)), ((), ()))

ANY = pl.BlockSpec(memory_space=pl.ANY)
SMEM = pl.BlockSpec(memory_space=pltpu.SMEM)
VMEM = pl.BlockSpec(memory_space=pltpu.VMEM)


def params(side_effects=False):
    return pltpu.CompilerParams(vmem_limit_bytes=VMEM_BYTES, has_side_effects=side_effects)


def matmul(a, b, dims):
    return lax.dot_general(a, b, dims, preferred_element_type=jnp.float32)


def in_hbm(*arrays):
    return [pltpu.with_memory_space_constraint(x, pltpu.HBM) for x in arrays]


def iota(shape, dim):
    return lax.broadcasted_iota(jnp.int32, shape, dim)


def load(pairs, sem):
    copies = [pltpu.make_async_copy(a, b, sem.at[i]) for i, (a, b) in enumerate(pairs)]
    for copy in copies:
        copy.start()

    def wait():
        for copy in copies:
            copy.wait()

    return wait


def list_pairs(row_of, pairs, me, replicas, moved):
    count = jnp.int32(0)
    for j in range(replicas):
        pairs[count] = row_of[j]
        pairs[moved + 1 + count] = j
        count = jnp.minimum(count + jnp.where((row_of[j] >= 0) & (j != me), 1, 0), moved)


def find_pairs(partner, row_of, replicas, local_rows):
    for j in range(replicas):
        row_of[j] = -1

    def note(r, carry):
        row_of[lax.div(partner[r], local_rows)] = r
        return carry

    lax.fori_loop(0, local_rows, note, 0, unroll=8)


def pairs_kernel(partner, pairs, row_of, *, replicas, local_rows, moved):
    find_pairs(partner, row_of, replicas, local_rows)
    list_pairs(row_of, pairs, lax.axis_index("replica"), replicas, moved)


def pack_kernel(
    fork, partner, queries, new_keys, new_values, keys, values, *rest, replicas, slots, moved
):
    outs = rest[: replicas - 1]
    pairs, qv, nkv, nvv, row_of, sems, row_sems = rest[replicas - 1 :]
    me = lax.axis_index("replica")
    held, prefix = keys.shape[0], keys.shape[1]
    local_rows = queries.shape[0]
    groups = queries.shape[2] // HEAD_DIM
    copies = []
    for k in range(1, replicas):
        peer = lax.rem(me + k, replicas)
        offset = jnp.int32(0)
        for s in range(slots):
            prompt = fork[s, peer]
            offset = jnp.where(lax.div(prompt, held) == me, lax.rem(prompt, held), offset)
        for n, source in enumerate((keys, values)):
            copy = pltpu.make_async_copy(
                source.at[offset], outs[k - 1].at[pl.ds(n * prefix, prefix)], sems.at[k - 1, n]
            )
            copy.start()
            copies.append(copy)
    find_pairs(partner, row_of, replicas, local_rows)
    rows = [jnp.maximum(row_of[lax.rem(me + k, replicas)], 0) for k in range(1, replicas)]
    fetched = [
        load([(queries.at[r], qv.at[i]), (new_keys.at[r], nkv.at[i]), (new_values.at[r], nvv.at[i])], row_sems.at[i])
        for i, r in enumerate(rows)
    ]
    for k in range(1, replicas):
        fetched[k - 1]()
        q = qv[k - 1].astype(jnp.float32)
        parts = [q[:, h * HEAD_DIM : (h + 1) * HEAD_DIM] for h in range(groups)]
        parts += [nkv[k - 1].astype(jnp.float32), nvv[k - 1].astype(jnp.float32)]
        pad = outs[k - 1].shape[0] - 2 * prefix - sum(p.shape[0] for p in parts)
        parts += [jnp.zeros((pad, HEAD_DIM), jnp.float32)]
        outs[k - 1][2 * prefix :, :] = jnp.concatenate(parts, axis=0).astype(outs[k - 1].dtype)
    list_pairs(row_of, pairs, me, replicas, moved)
    for copy in copies:
        copy.wait()


def softmax_weights(prompt, new, cache, prompt_mask, new_mask, cache_mask):
    prompt = jnp.where(prompt_mask, prompt, LOWEST)
    new = jnp.where(new_mask, new, LOWEST)
    cache = jnp.where(cache_mask, cache, LOWEST)
    top = jnp.max(jnp.maximum(jnp.maximum(prompt, new), cache), axis=1, keepdims=True)
    prompt = jnp.exp2((prompt - top) * EXP2_SCALE)
    new = jnp.exp2((new - top) * EXP2_SCALE)
    cache = jnp.exp2((cache - top) * EXP2_SCALE)
    inverse = 1.0 / jnp.sum(prompt + new + cache, axis=1, keepdims=True)
    return prompt * inverse, new * inverse, cache * inverse


def pick_slot(scores, slot, slots, prefix):
    picked = scores[:, :prefix]
    for s in range(1, slots):
        picked = jnp.where(slot == s, scores[:, s * prefix : (s + 1) * prefix], picked)
    return picked


def spread_slot(weights, slot, slots):
    return jnp.concatenate(
        [jnp.where(slot == s, weights, 0.0).astype(jnp.bfloat16) for s in range(slots)], axis=1
    )


def fill_meta(lookup, local_row, span, row_meta, alive_rows):
    row_slot, fork, prompt_lengths, cache_lengths, finished, me, slots, local_rows = lookup
    g = me * local_rows + local_row
    slot = row_slot[g]
    values = (slot, prompt_lengths[fork[slot, me]], cache_lengths[g])
    size = span.stop - span.start
    for i, value in enumerate(values):
        row_meta[i, span, :] = jnp.full((size, HEAD_DIM), value, jnp.int32)
    alive_rows[span, :] = jnp.full((size, HEAD_DIM), 1 - finished[g], jnp.int32).astype(jnp.float32)


def attend_scores(q, ck, cache_scores, *, steps, suffix):
    n = q.shape[0]
    groups = q.shape[1] // HEAD_DIM
    keys_sub = 4 * suffix
    half = 2 * suffix
    for sub in range(n // 16):
        r0 = sub * 16
        qs = jnp.concatenate(
            [q[r0 : r0 + 16, h * HEAD_DIM : (h + 1) * HEAD_DIM] for h in range(groups)], axis=0
        )
        s = matmul(qs, ck[sub * keys_sub : (sub + 1) * keys_sub, :], NT)
        for h in range(groups):
            cache_scores[h, r0 : r0 + 8, :] = s[16 * h : 16 * h + 8, :half]
            cache_scores[h, r0 + 8 : r0 + 16, :] = s[16 * h + 8 : 16 * h + 16, half:]


def stage_kernel(
    cols, fork, pairs, row_slot, prompt_lengths, cache_lengths, finished, queries, keys, values, weights, sibling,
    q, scores, cv, w_there, row_meta, alive_rows, moved_keys, moved_values, moved_meta, moved_alive,
    qv, ckv, sems, *, moved, slots, suffix, span
):
    local_rows, steps, width = queries.shape
    blocks = scores.shape[0]
    rows = local_rows // blocks
    n = rows * steps
    per = 16 // steps
    first = load([(queries, qv)], sems.at[0])
    ready = [
        load([(keys.at[pl.ds(i * rows * suffix, rows * suffix)], ckv.at[i])], sems.at[1 + i]) for i in range(blocks)
    ]
    model = w_there.shape[1]
    at = pl.ds(pl.multiple_of(cols[1] * model, HEAD_DIM), model)
    copies = [
        (values, cv),
        (weights.at[:, at], w_there.at[pl.ds(0, width)]),
        (sibling.at[:, at], w_there.at[pl.ds(width, width)]),
    ]
    for i in range(moved):
        source = pl.ds(pl.multiple_of(pairs[i] * suffix, suffix), suffix)
        target = pl.ds(i * suffix, suffix)
        copies += [(keys.at[source], moved_keys.at[target]), (values.at[source], moved_values.at[target])]
    rest = load(copies, sems.at[1 + blocks])
    me = lax.axis_index("replica")
    lookup = (row_slot, fork, prompt_lengths, cache_lengths, finished, me, slots, local_rows)
    for b in range(local_rows):
        i, low = b // rows, b % rows * steps
        fill_meta(lookup, b, slice(low, low + steps), row_meta.at[i], alive_rows.at[i])
    for i in range(moved):
        fill_meta(lookup, pairs[i], slice(i * span, (i + 1) * span), moved_meta, moved_alive)
    first()
    for b in range(0, local_rows, per):
        part = [qv[b + i].astype(jnp.float32) for i in range(per)]
        q[b * steps : (b + per) * steps, :] = jnp.concatenate(part, axis=0).astype(q.dtype)
    for i in range(blocks):
        ready[i]()
        attend_scores(q.at[pl.ds(i * n, n)], ckv.at[i], scores.at[i], steps=steps, suffix=suffix)
    rest()


def attend_block(
    q, nk, nv, cv, pk, pv, heads, row_meta, alive_rows, cache_scores, weights, cache_weights, mixed,
    *, steps, slots, suffix
):
    n = q.shape[0]
    groups = q.shape[1] // HEAD_DIM
    prefix = pk.shape[0] // slots
    keys_sub = 4 * suffix
    half = 2 * suffix
    shape = (n, HEAD_DIM)
    lane, row = iota(shape, 1), iota(shape, 0)
    cache_own = (lane // suffix) == ((row % 8) // steps)
    cache_lane = jnp.where(cache_own, lane % suffix, suffix)
    new_mask = ((lane // steps) == (row // steps)) & ((lane % steps) <= (row % steps))
    first_half = (row % 16) < 8
    slot = row_meta[0]
    prompt_mask = lane < row_meta[1]
    cache_mask = cache_lane < row_meta[2]
    q_all = jnp.concatenate([q[:, h * HEAD_DIM : (h + 1) * HEAD_DIM] for h in range(groups)], axis=0)
    prompt_all = matmul(q_all, pk[...], NT)
    new_all = matmul(q_all, nk[...], NT)
    for h in range(groups):
        part = slice(h * n, (h + 1) * n)
        prompt = pick_slot(prompt_all[part], slot, slots, prefix)
        wp, wn, wc = softmax_weights(
            prompt, new_all[part], cache_scores[h], prompt_mask, new_mask, cache_mask
        )
        cache_weights[h, :, :half] = jnp.where(first_half, wc, 0.0).astype(jnp.bfloat16)
        cache_weights[h, :, half:] = jnp.where(first_half, 0.0, wc).astype(jnp.bfloat16)
        weights[part, : slots * prefix] = spread_slot(wp, slot, slots)
        weights[part, slots * prefix :] = wn.astype(jnp.bfloat16)
    mixed[...] = matmul(weights[:, : slots * prefix], pv[...], NN) + matmul(
        weights[:, slots * prefix :], nv[...], NN
    )
    for sub in range(n // 16):
        r0 = sub * 16
        w = jnp.concatenate([cache_weights[h, r0 : r0 + 16, :] for h in range(groups)], axis=0)
        o = matmul(w, cv[sub * keys_sub : (sub + 1) * keys_sub, :], NN)
        for h in range(groups):
            total = mixed[h * n + r0 : h * n + r0 + 16, :] + o[16 * h : 16 * h + 16, :]
            heads[r0 : r0 + 16, h * HEAD_DIM : (h + 1) * HEAD_DIM] = (
                total * alive_rows[r0 : r0 + 16, :]
            ).astype(heads.dtype)


def moved_block(x, pk, pv, keys, values, slot, plen, clen, alive, *, steps, slots, groups, span, suffix):
    prefix = pk.shape[0] // slots
    shape = (4 * span, HEAD_DIM)
    lane, row = iota(shape, 1), iota(shape, 0)
    prompt_mask = lane < plen
    cache_mask = ((lane // suffix) == ((row // span) % 2)) & ((lane % suffix) < clen)
    past = (lane % span) - groups * steps
    new_mask = ((lane // span) == (row // span)) & (past >= 0) & (past <= row % steps)
    prompt = pick_slot(matmul(x, pk[...], NT), slot, slots, prefix)
    new = matmul(x, x, NT)
    cache = matmul(x, keys[...], NT)
    half = 2 * suffix
    top_half = row < 2 * span
    cache = jnp.where(top_half, cache[:, :half], cache[:, half:])
    wp, wn, wc = softmax_weights(prompt, new, cache, prompt_mask, new_mask, cache_mask)
    wc = jnp.concatenate(
        [jnp.where(top_half, wc, 0.0), jnp.where(top_half, 0.0, wc)], axis=1
    ).astype(jnp.bfloat16)
    wn = pltpu.roll(wn, steps, 1).astype(jnp.bfloat16)
    mixed = (
        matmul(spread_slot(wp, slot, slots), pv[...], NN)
        + matmul(wn, x, NN)
        + matmul(wc, values[...], NN)
    )
    mixed = (mixed * alive).astype(jnp.bfloat16)
    row, col = iota((4 * steps, 4 * span), 0), iota((4 * steps, 4 * span), 1)
    cols = []
    for h in range(groups):
        take = ((row // steps) == (col // span)) & ((col % span) == h * steps + row % steps)
        cols.append(matmul(take.astype(jnp.bfloat16), mixed, NN).astype(jnp.bfloat16))
    return jnp.concatenate(cols, axis=1)


def attend_kernel(
    fork, pairs, q, nk, nv, cache_scores, cv, row_meta, alive_rows, keys, values, moved_meta, moved_alive, own_keys,
    own_values, *rest, stacked, replicas, slots, moved, steps, suffix, span
):
    count = 1 if stacked else replicas - 1
    recvs, rest = rest[:count], rest[count:]
    heads, pk, pv, x, weights, cache_weights, mixed, sems, moved_sems = rest
    me = lax.axis_index("replica")
    held, prefix = own_keys.shape[0], own_keys.shape[1]
    blocks, n = row_meta.shape[0], row_meta.shape[2]
    groups = q.shape[1] // HEAD_DIM
    rows = n // steps
    for s in range(slots):
        prompt = fork[s, me]
        owner = lax.div(prompt, held)
        offset = lax.rem(prompt, held)
        targets = (pk.at[pl.ds(s * prefix, prefix)], pv.at[pl.ds(s * prefix, prefix)])
        if stacked:
            for i in range(2):
                pltpu.make_async_copy(
                    recvs[0].at[owner, pl.ds(i * prefix, prefix)], targets[i], sems.at[s, i]
                ).start()
            continue
        k = lax.rem(me - owner + replicas, replicas)

        @pl.when(k == 0)
        def _():
            pltpu.make_async_copy(own_keys.at[offset], targets[0], sems.at[s, 0]).start()
            pltpu.make_async_copy(own_values.at[offset], targets[1], sems.at[s, 1]).start()

        for kk in range(1, replicas):

            @pl.when(k == kk)
            def _():
                for i in range(2):
                    pltpu.make_async_copy(
                        recvs[kk - 1].at[pl.ds(i * prefix, prefix)], targets[i], sems.at[s, i]
                    ).start()

    for i in range(moved):
        peer = pairs[moved + 1 + i]
        if stacked:
            pltpu.make_async_copy(
                recvs[0].at[peer, pl.ds(2 * prefix, span)], x.at[pl.ds(i * span, span)], moved_sems.at[i]
            ).start()
        else:
            k = lax.rem(me - peer + replicas, replicas)
            for kk in range(1, replicas):

                @pl.when(k == kk)
                def _():
                    pltpu.make_async_copy(
                        recvs[kk - 1].at[pl.ds(2 * prefix, span)],
                        x.at[pl.ds(i * span, span)],
                        moved_sems.at[i],
                    ).start()

    for s in range(slots):
        for i, target in enumerate((pk, pv)):
            pltpu.make_async_copy(own_keys.at[0], target.at[pl.ds(s * prefix, prefix)], sems.at[s, i]).wait()
    for i in range(blocks):
        part = pl.ds(i * n, n)
        attend_block(
            q.at[part], nk.at[part], nv.at[part], cv.at[pl.ds(i * rows * suffix, rows * suffix)], pk, pv,
            heads.at[part], row_meta.at[i], alive_rows.at[i], cache_scores.at[i], weights.at[i],
            cache_weights.at[i], mixed.at[i], steps=steps, slots=slots, suffix=suffix,
        )
    for i in range(moved):
        pltpu.make_async_copy(
            own_keys.at[0, pl.ds(0, span)], x.at[pl.ds(i * span, span)], moved_sems.at[i]
        ).wait()

    first = blocks * n
    for g in range(moved // 4):
        part = slice(g * 4 * span, (g + 1) * 4 * span)
        kpart = slice(g * 4 * suffix, (g + 1) * 4 * suffix)
        heads[first + g * 4 * steps : first + (g + 1) * 4 * steps, :] = moved_block(
            x[part, :], pk, pv, keys.at[kpart], values.at[kpart],
            moved_meta[0, part, :], moved_meta[1, part, :], moved_meta[2, part, :], moved_alive[part, :],
            steps=steps, slots=slots, groups=groups, span=span, suffix=suffix,
        )


def project_kernel(h_own, h_sib, weights, out):
    rows = pl.ds(0, out.shape[0])
    both = jnp.concatenate([h_own[rows, :], h_sib[rows, :]], axis=1)
    out[...] = matmul(both, weights[...], NN).astype(out.dtype)


def base_kernel(cols, h_own, h_sib, w_own, w_sib, residual, after, out, weights, before, sems):
    rows, model = out.shape
    width = w_own.shape[0]
    steps = residual.shape[1]
    at = pl.ds(pl.multiple_of(cols[0] * model, HEAD_DIM), model)
    ready = load(
        [
            (w_own.at[:, at], weights.at[pl.ds(0, width)]),
            (w_sib.at[:, at], weights.at[pl.ds(width, width)]),
            (residual, before),
        ],
        sems,
    )
    both = jnp.concatenate([h_own[pl.ds(0, rows), :], h_sib[pl.ds(0, rows), :]], axis=1)
    ready()
    total = matmul(both, weights[...], NN)
    for b in range(residual.shape[0]):
        part = slice(b * steps, (b + 1) * steps)
        out[part, :] = total[part] + before[b].astype(jnp.float32)


def moved_send_kernel(pairs, h_own, h_sib, after, *outs, moved, steps, split):
    me = lax.axis_index("replica")
    rows = pl.ds(h_own.shape[0] - moved * steps, moved * steps)
    both = jnp.concatenate([h_own[rows, :], h_sib[rows, :]], axis=1).astype(jnp.float32)
    for i in range(moved):
        peer = pairs[moved + 1 + i]
        value = both[i * steps : (i + 1) * steps].astype(outs[0].dtype)
        if split:
            k = jnp.bitwise_xor(me, peer)
            place = 2 * lax.rem(lax.div(k, 2), 2) + lax.div(k, 4)

            @pl.when(lax.rem(k, 2) == 0)
            def _():
                outs[0][place] = value

            @pl.when(lax.rem(k, 2) == 1)
            def _():
                outs[1][place] = value

        else:
            outs[0][peer] = value


def moved_project_kernel(pairs, w_here, w_there, *rest, moved, steps, split):
    backs, (cross, base, heads) = rest[:-3], rest[-3:]
    me = lax.axis_index("replica")
    for i in range(moved):
        peer = pairs[moved + 1 + i]
        part = slice(i * steps, (i + 1) * steps)
        if split:
            k = jnp.bitwise_xor(me, peer)
            places = {1: (0, 0), 2: (1, 0), 3: (1, 2), 4: (2, 0), 5: (2, 1), 6: (2, 2), 7: (2, 3)}
            for d, (which, index) in places.items():

                @pl.when(k == d)
                def _():
                    heads[part, :] = backs[which][index].astype(jnp.float32)

        else:
            heads[part, :] = backs[0][peer].astype(jnp.float32)
    both = heads[...].astype(cross.dtype)
    cross[...] = matmul(both, w_there[...], NN).astype(cross.dtype)
    base[...] = matmul(both, w_here[...], NN)


def finish_kernel(pairs, base, recv, base_moved, recv_moved, residual, out, before, sems, *, moved):
    step = pl.program_id(0)
    rows, steps = out.shape[:2]
    copies = [
        pltpu.make_async_copy(residual.at[pairs[i]], before.at[i], sems.at[i]) for i in range(moved)
    ]

    @pl.when(step == 0)
    def _():
        for copy in copies:
            copy.start()

    part = pl.ds(pl.multiple_of(step * rows * steps, rows * steps), rows * steps)
    total = base[part, :] + recv[part, :].astype(jnp.float32)
    for b in range(rows):
        out[b] = total[b * steps : (b + 1) * steps].astype(out.dtype)

    @pl.when(step == 0)
    def _():
        for copy in copies:
            copy.wait()

    branch = base_moved[...] + recv_moved[...].astype(jnp.float32)
    for i in range(moved):
        r = pairs[i]

        @pl.when(lax.div(r, rows) == step)
        def _():
            value = branch[i * steps : (i + 1) * steps] + before[i].astype(jnp.float32)
            out[lax.rem(r, rows)] = value.astype(out.dtype)


def exchange_pack(
    fork, partner, row_slot, queries, new_keys, new_values, fork_table, prompt_keys, prompt_values, span, moved
):
    replicas = lax.axis_size("replica")
    me = lax.axis_index("replica")
    local_rows, steps, width = queries.shape
    groups = width // HEAD_DIM
    held, prefix = prompt_keys.shape[:2]
    dtype = queries.dtype
    pairs_shape = jax.ShapeDtypeStruct((2 * (moved + 1),), jnp.int32)
    if replicas <= 8:
        *packed, pairs = pl.pallas_call(
            functools.partial(pack_kernel, replicas=replicas, slots=fork_table.shape[1], moved=moved),
            out_shape=[pltpu.VMEM((2 * prefix + span, HEAD_DIM), dtype)] * (replicas - 1) + [pairs_shape],
            in_specs=[SMEM, SMEM] + [ANY] * 5,
            out_specs=[VMEM] * (replicas - 1) + [SMEM],
            scratch_shapes=[
                pltpu.VMEM((replicas - 1, steps, width), dtype),
                pltpu.VMEM((replicas - 1, steps, HEAD_DIM), dtype),
                pltpu.VMEM((replicas - 1, steps, HEAD_DIM), dtype),
                pltpu.SMEM((replicas,), jnp.int32),
                pltpu.SemaphoreType.DMA((replicas - 1, 2)),
                pltpu.SemaphoreType.DMA((replicas - 1, 3)),
            ],
            compiler_params=params(),
            name="pack",
        )(*in_hbm(fork, partner, queries, new_keys, new_values, prompt_keys, prompt_values))
        received = [
            lax.ppermute(packed[k - 1], "replica", [(i, (i + k) % replicas) for i in range(replicas)])
            for k in range(1, replicas)
        ]
        return received, pairs
    chosen = (fork_table // held) == me
    offsets = jnp.sum(jnp.where(chosen, fork_table % held, 0), axis=1)
    peer_of = partner // local_rows
    pairing = (peer_of[None, :] == jnp.arange(replicas, dtype=jnp.int32)[:, None]) & (
        peer_of[None, :] != me
    )
    row_of = jnp.sum(jnp.where(pairing, jnp.arange(local_rows, dtype=jnp.int32)[None, :], 0), axis=1)
    q = queries[row_of].reshape(replicas, steps, groups, HEAD_DIM).transpose(0, 2, 1, 3)
    q = q.reshape(replicas, groups * steps, HEAD_DIM)
    pad = jnp.zeros((replicas, span - (groups + 2) * steps, HEAD_DIM), dtype)
    block = jnp.concatenate(
        [prompt_keys[offsets], prompt_values[offsets], q, new_keys[row_of], new_values[row_of], pad], axis=1
    )
    pairs = pl.pallas_call(
        functools.partial(pairs_kernel, replicas=replicas, local_rows=local_rows, moved=moved),
        out_shape=pairs_shape,
        in_specs=[SMEM],
        out_specs=SMEM,
        scratch_shapes=[pltpu.SMEM((replicas,), jnp.int32)],
        name="pairs",
    )(partner)
    return [lax.all_to_all(block, "replica", split_axis=0, concat_axis=0, tiled=True)], pairs


def body(
    residual,
    queries,
    new_keys,
    new_values,
    cache_keys,
    cache_values,
    cache_lengths,
    finished,
    partner,
    row_slot,
    fork_table,
    prompt_keys,
    prompt_values,
    prompt_lengths,
    out_proj,
):
    replicas = lax.axis_size("replica")
    tensors = lax.axis_size("tensor")
    place = lax.axis_index("tensor")
    local_rows, steps, width = queries.shape
    groups = width // HEAD_DIM
    suffix = cache_keys.shape[1]
    held, prefix = prompt_keys.shape[:2]
    slots = fork_table.shape[1]
    moved = replicas // 2
    stacked = replicas > 8
    model = residual.shape[2]
    n = local_rows * steps
    span = 32
    dtype = queries.dtype
    fork = fork_table.T
    sibling = [(i, i ^ 1) for i in range(tensors)]
    across = [(i, i ^ 2) for i in range(tensors)]

    received, pairs = exchange_pack(
        fork, partner, row_slot, queries, new_keys, new_values, fork_table, prompt_keys, prompt_values, span, moved
    )
    w_sib = lax.ppermute(out_proj, "tensor", sibling)
    nk2 = new_keys.reshape(n, HEAD_DIM)
    nv2 = new_values.reshape(n, HEAD_DIM)
    ck2 = cache_keys.reshape(local_rows * suffix, HEAD_DIM)
    cv2 = cache_values.reshape(local_rows * suffix, HEAD_DIM)
    lookup = (row_slot, prompt_lengths, cache_lengths, finished)

    dma = lambda *shape: pltpu.SemaphoreType.DMA(shape)
    blocks = local_rows // BLOCK
    nb = BLOCK * steps
    assert nb == HEAD_DIM
    cols = jnp.stack([place, place ^ 2]).astype(jnp.int32)
    q2, scores, cvv, w_there, *staged = pl.pallas_call(
        functools.partial(stage_kernel, moved=moved, slots=slots, suffix=suffix, span=span),
        out_shape=[
            pltpu.VMEM((n, width), dtype),
            pltpu.VMEM((blocks, groups, nb, HEAD_DIM), jnp.float32),
            pltpu.VMEM((local_rows * suffix, HEAD_DIM), dtype),
            pltpu.VMEM((2 * width, model), dtype),
            pltpu.VMEM((blocks, 3, nb, HEAD_DIM), jnp.int32),
            pltpu.VMEM((blocks, nb, HEAD_DIM), jnp.float32),
            pltpu.VMEM((moved * suffix, HEAD_DIM), dtype),
            pltpu.VMEM((moved * suffix, HEAD_DIM), dtype),
            pltpu.VMEM((3, moved * span, HEAD_DIM), jnp.int32),
            pltpu.VMEM((moved * span, HEAD_DIM), jnp.float32),
        ],
        in_specs=[SMEM] * 7 + [ANY] * 5,
        out_specs=[VMEM] * 10,
        scratch_shapes=[
            pltpu.VMEM((local_rows, steps, width), dtype),
            pltpu.VMEM((blocks, BLOCK * suffix, HEAD_DIM), dtype),
            dma(2 + blocks, 3 + 2 * moved),
        ],
        compiler_params=params(),
        name="stage",
    )(*in_hbm(cols, fork, pairs, *lookup, queries, ck2, cv2, out_proj, w_sib))
    (heads,) = pl.pallas_call(
        functools.partial(
            attend_kernel, stacked=stacked, replicas=replicas, slots=slots, moved=moved, steps=steps, suffix=suffix,
            span=span,
        ),
        out_shape=[pltpu.VMEM(((local_rows + moved) * steps, width), dtype)],
        in_specs=[SMEM] * 2 + [VMEM] * 11 + [ANY] * (2 + len(received)),
        out_specs=[VMEM],
        scratch_shapes=[
            pltpu.VMEM((slots * prefix, HEAD_DIM), dtype),
            pltpu.VMEM((slots * prefix, HEAD_DIM), dtype),
            pltpu.VMEM((moved * span, HEAD_DIM), dtype),
            pltpu.VMEM((blocks, groups * nb, slots * prefix + HEAD_DIM), jnp.bfloat16),
            pltpu.VMEM((blocks, groups, nb, 2 * HEAD_DIM), jnp.bfloat16),
            pltpu.VMEM((blocks, groups * nb, HEAD_DIM), jnp.float32),
            dma(slots, 2),
            dma(moved),
        ],
        compiler_params=params(),
        name="attend",
    )(*in_hbm(fork, pairs), q2, nk2, nv2, scores, cvv, *staged, *in_hbm(prompt_keys, prompt_values), *received)

    sib = lax.ppermute(heads, "tensor", sibling)
    m = moved * steps

    def call(kernel, name, shapes, specs, operands, extra=()):
        return pl.pallas_call(
            kernel,
            out_shape=[pltpu.VMEM(shape, kind) for shape, kind in shapes],
            in_specs=specs,
            out_specs=[VMEM] * len(shapes),
            scratch_shapes=list(extra),
            compiler_params=params(),
            name=name,
        )(*operands)

    (crossed,) = call(project_kernel, "project", [((n, model), dtype)], [VMEM] * 3, (heads, sib, w_there))
    got = lax.ppermute(crossed, "tensor", across)
    base, w_here = call(
        base_kernel,
        "base",
        [((n, model), jnp.float32), ((2 * width, model), dtype)],
        [SMEM, VMEM, VMEM, ANY, ANY, ANY, ANY],
        (*in_hbm(cols), heads, sib, *in_hbm(out_proj, w_sib, residual), crossed),
        [pltpu.VMEM(residual.shape, dtype), dma(3)],
    )

    options = dict(moved=moved, steps=steps, split=not stacked)
    shape = ((replicas if stacked else 4, steps, 2 * width), dtype)
    back = call(
        functools.partial(moved_send_kernel, **options),
        "moved_send",
        [shape] * (1 if stacked else 2),
        [SMEM, VMEM, VMEM, ANY],
        (*in_hbm(pairs), heads, sib, crossed),
    )
    if stacked:
        backs = [lax.all_to_all(back[0], "replica", split_axis=0, concat_axis=0, tiled=True)]
    else:
        flip = lambda x, bit: lax.ppermute(x, "replica", [(i, i ^ bit) for i in range(replicas)])
        kept = back[0]
        one = flip(back[1], 1)
        two = flip(jnp.concatenate([kept[2:], one[2:]]), 2)
        four = flip(jnp.concatenate([kept[1:2], one[1:2], two[1:2], two[3:4]]), 4)
        backs = [one, two, four]
    crossed_moved, base_moved = call(
        functools.partial(moved_project_kernel, **options),
        "moved_project",
        [((m, model), dtype), ((m, model), jnp.float32)],
        [SMEM] + [VMEM] * (2 + len(backs)),
        (*in_hbm(pairs), w_here, w_there, *backs),
        [pltpu.VMEM((m, 2 * width), jnp.float32)],
    )
    got_moved = lax.ppermute(crossed_moved, "tensor", across)

    return pl.pallas_call(
        functools.partial(finish_kernel, moved=moved),
        grid=(blocks,),
        in_specs=[SMEM, VMEM, VMEM, VMEM, VMEM, ANY],
        out_specs=pl.BlockSpec((BLOCK, steps, model), lambda i: (i, 0, 0)),
        out_shape=jax.ShapeDtypeStruct(residual.shape, residual.dtype),
        scratch_shapes=[pltpu.VMEM((moved, steps, model), dtype), dma(moved)],
        compiler_params=params(),
        name="finish",
    )(*in_hbm(pairs), base, got, base_moved, got_moved, *in_hbm(residual))


def solution(mesh):
    rows = P("replica", None, "tensor")
    in_specs = (rows,) * 6 + (P(), P(), P("replica"), P(), P(), rows, rows, P(), P("tensor", None))
    return jax.shard_map(body, mesh=mesh, in_specs=in_specs, out_specs=rows, check_vma=False)
```

```python
import functools
import math

import jax
import jax.numpy as jnp
from jax import lax
from jax.experimental import pallas as pl
from jax.experimental.pallas import tpu as pltpu
from jax.sharding import PartitionSpec as P

HEAD_DIM = 128
LOWEST = -1e30
EXP2_SCALE = math.log2(math.e) / math.sqrt(HEAD_DIM)
VMEM_BYTES = 24 * 1024 * 1024
SMALL = pl.CostEstimate(flops=1, bytes_accessed=1, transcendentals=0)
BLOCK = 32
FIRST = 2
NT = (((1,), (1,)), ((), ()))
NN = (((1,), (0,)), ((), ()))

ANY = pl.BlockSpec(memory_space=pl.ANY)
SMEM = pl.BlockSpec(memory_space=pltpu.SMEM)
VMEM = pl.BlockSpec(memory_space=pltpu.VMEM)


def params(side_effects=False):
    return pltpu.CompilerParams(vmem_limit_bytes=VMEM_BYTES, has_side_effects=side_effects)


def matmul(a, b, dims):
    return lax.dot_general(a, b, dims, preferred_element_type=jnp.float32)


def columns(model, flip):
    place = jnp.bitwise_xor(lax.axis_index("tensor"), flip)
    return pl.ds(pl.multiple_of(place * model, HEAD_DIM), model)


def in_hbm(*arrays):
    return [pltpu.with_memory_space_constraint(x, pltpu.HBM) for x in arrays]


def iota(shape, dim):
    return lax.broadcasted_iota(jnp.int32, shape, dim)


def load(pairs, sem):
    copies = [pltpu.make_async_copy(a, b, sem.at[i]) for i, (a, b) in enumerate(pairs)]
    for copy in copies:
        copy.start()

    def wait():
        for copy in copies:
            copy.wait()

    return wait


def list_pairs(row_of, pairs, me, replicas, moved):
    count = jnp.int32(0)
    for j in range(replicas):
        pairs[count] = row_of[j]
        pairs[moved + 1 + count] = j
        pairs[2 * (moved + 1) + j] = jnp.maximum(row_of[j], 0)
        count = jnp.minimum(count + jnp.where((row_of[j] >= 0) & (j != me), 1, 0), moved)


def find_pairs(partner, row_of, replicas, local_rows):
    for j in range(replicas):
        row_of[j] = -1

    shift = local_rows.bit_length() - 1

    def note(r, carry):
        peer = partner[r] >> shift if local_rows == 1 << shift else lax.div(partner[r], local_rows)
        row_of[peer] = r
        return carry

    lax.fori_loop(0, local_rows, note, 0, unroll=8)


def send_prompts(shifts, fork, keys, values, outs, sems, replicas):
    me = lax.axis_index("replica")
    held, prefix = keys.shape[0], keys.shape[1]
    waits = []
    for i, k in enumerate(shifts):
        peer = lax.rem(me + k, replicas)
        offset = jnp.int32(0)
        for s in range(fork.shape[0]):
            prompt = fork[s, peer]
            offset = jnp.where(lax.div(prompt, held) == me, lax.rem(prompt, held), offset)
        copies = [
            (source.at[offset], outs[i].at[pl.ds(n * prefix, prefix)]) for n, source in enumerate((keys, values))
        ]
        waits.append(load(copies, sems.at[i]))
    return waits


def send_rows(shifts, row_of, hbm, vmem, outs, sems, replicas, prefix):
    me = lax.axis_index("replica")
    width = hbm[0].shape[2]
    waits = []
    for i, k in enumerate(shifts):
        r = row_of(lax.rem(me + k, replicas))
        waits.append(load([(a.at[r], b.at[i]) for a, b in zip(hbm, vmem)], sems.at[i]))
    for i in range(len(shifts)):
        waits[i]()
        q, nk, nv = [v[i].astype(jnp.float32) for v in vmem]
        parts = [q[:, low : low + HEAD_DIM] for low in range(0, width, HEAD_DIM)] + [nk, nv]
        pad = outs[i].shape[0] - 2 * prefix - sum(p.shape[0] for p in parts)
        parts += [jnp.zeros((pad, HEAD_DIM), jnp.float32)]
        outs[i][2 * prefix :, :] = jnp.concatenate(parts, axis=0).astype(outs[i].dtype)


def pairs_kernel(partner, pairs, row_of, *, replicas, local_rows, moved):
    find_pairs(partner, row_of, replicas, local_rows)
    list_pairs(row_of, pairs, lax.axis_index("replica"), replicas, moved)


def pack_kernel(
    fork, partner, queries, new_keys, new_values, keys, values, *rest, replicas, moved, shifts
):
    outs, (pairs, qv, nkv, nvv, row_of, sems, row_sems) = rest[: len(shifts)], rest[len(shifts) :]
    waits = send_prompts(shifts, fork, keys, values, outs, sems, replicas)
    find_pairs(partner, row_of, replicas, queries.shape[0])
    list_pairs(row_of, pairs, lax.axis_index("replica"), replicas, moved)
    send_rows(
        shifts, lambda j: jnp.maximum(row_of[j], 0), (queries, new_keys, new_values), (qv, nkv, nvv), outs, row_sems,
        replicas, keys.shape[1],
    )
    for wait in waits:
        wait()


def softmax_weights(prompt, new, cache, prompt_mask, new_mask, cache_mask):
    prompt = jnp.where(prompt_mask, prompt, LOWEST)
    new = jnp.where(new_mask, new, LOWEST)
    cache = jnp.where(cache_mask, cache, LOWEST)
    top = jnp.max(jnp.maximum(jnp.maximum(prompt, new), cache), axis=1, keepdims=True)
    prompt = jnp.exp2((prompt - top) * EXP2_SCALE)
    new = jnp.exp2((new - top) * EXP2_SCALE)
    cache = jnp.exp2((cache - top) * EXP2_SCALE)
    inverse = 1.0 / jnp.sum(prompt + new + cache, axis=1, keepdims=True)
    return prompt * inverse, new * inverse, cache * inverse


def pick_slot(scores, slot, slots, prefix):
    picked = scores[:, :prefix]
    for s in range(1, slots):
        picked = jnp.where(slot == s, scores[:, s * prefix : (s + 1) * prefix], picked)
    return picked


def spread_slot(weights, slot, slots):
    return jnp.concatenate(
        [jnp.where(slot == s, weights, 0.0).astype(jnp.bfloat16) for s in range(slots)], axis=1
    )


def fill_meta(lookup, local_row, span, meta):
    row_slot, fork, prompt_lengths, cache_lengths, finished, me, local_rows = lookup
    g = me * local_rows + local_row
    slot = row_slot[g]
    values = (slot, prompt_lengths[fork[slot, me]], cache_lengths[g], 1 - finished[g])
    size = span.stop - span.start
    for i, value in enumerate(values):
        meta[i, span, :] = jnp.full((size, HEAD_DIM), value, jnp.int32)


def attend_scores(q, ck, cache_scores, *, steps, suffix):
    n = q.shape[0]
    groups = q.shape[1] // HEAD_DIM
    keys_sub = 4 * suffix
    half = 2 * suffix
    for sub in range(n // 16):
        r0 = sub * 16
        qs = jnp.concatenate(
            [q[r0 : r0 + 16, h * HEAD_DIM : (h + 1) * HEAD_DIM] for h in range(groups)], axis=0
        )
        s = matmul(qs, ck[sub * keys_sub : (sub + 1) * keys_sub, :], NT)
        for h in range(groups):
            cache_scores[h, r0 : r0 + 8, :] = s[16 * h : 16 * h + 8, :half]
            cache_scores[h, r0 + 8 : r0 + 16, :] = s[16 * h + 8 : 16 * h + 16, half:]


def attend_block(
    q, nk, nv, cv, pk, pv, heads, meta, cache_scores, weights, cache_weights, mixed, wait,
    *, steps, slots, suffix
):
    n = q.shape[0]
    groups = q.shape[1] // HEAD_DIM
    prefix = pk.shape[0] // slots
    keys_sub = 4 * suffix
    half = 2 * suffix
    shape = (n, HEAD_DIM)
    lane, row = iota(shape, 1), iota(shape, 0)
    cache_own = (lane // suffix) == ((row % 8) // steps)
    cache_lane = jnp.where(cache_own, lane % suffix, suffix)
    new_mask = ((lane // steps) == (row // steps)) & ((lane % steps) <= (row % steps))
    first_half = (row % 16) < 8
    slot = meta[0]
    prompt_mask = lane < meta[1]
    cache_mask = cache_lane < meta[2]
    alive_rows = meta[3].astype(jnp.float32)
    q_all = jnp.concatenate([q[:, h * HEAD_DIM : (h + 1) * HEAD_DIM] for h in range(groups)], axis=0)
    prompt_all = matmul(q_all, pk[...], NT)
    new_all = matmul(q_all, nk[...], NT)
    for h in range(groups):
        part = slice(h * n, (h + 1) * n)
        prompt = pick_slot(prompt_all[part], slot, slots, prefix)
        wp, wn, wc = softmax_weights(
            prompt, new_all[part], cache_scores[h], prompt_mask, new_mask, cache_mask
        )
        cache_weights[h, :, :half] = jnp.where(first_half, wc, 0.0).astype(jnp.bfloat16)
        cache_weights[h, :, half:] = jnp.where(first_half, 0.0, wc).astype(jnp.bfloat16)
        weights[part, : slots * prefix] = spread_slot(wp, slot, slots)
        weights[part, slots * prefix :] = wn.astype(jnp.bfloat16)
    mixed[...] = matmul(weights[:, : slots * prefix], pv[...], NN) + matmul(
        weights[:, slots * prefix :], nv[...], NN
    )
    if wait is not None:
        wait()
    for sub in range(n // 16):
        r0 = sub * 16
        w = jnp.concatenate([cache_weights[h, r0 : r0 + 16, :] for h in range(groups)], axis=0)
        o = matmul(w, cv[sub * keys_sub : (sub + 1) * keys_sub, :], NN)
        for h in range(groups):
            total = mixed[h * n + r0 : h * n + r0 + 16, :] + o[16 * h : 16 * h + 16, :]
            heads[r0 : r0 + 16, h * HEAD_DIM : (h + 1) * HEAD_DIM] = (
                total * alive_rows[r0 : r0 + 16, :]
            ).astype(heads.dtype)


def moved_block(x, pk, pv, keys, values, slot, plen, clen, alive, *, steps, slots, groups, span, suffix):
    prefix = pk.shape[0] // slots
    shape = (4 * span, HEAD_DIM)
    lane, row = iota(shape, 1), iota(shape, 0)
    prompt_mask = lane < plen
    cache_mask = ((lane // suffix) == ((row // span) % 2)) & ((lane % suffix) < clen)
    past = (lane % span) - groups * steps
    new_mask = ((lane // span) == (row // span)) & (past >= 0) & (past <= row % steps)
    prompt = pick_slot(matmul(x, pk[...], NT), slot, slots, prefix)
    new = matmul(x, x, NT)
    cache = matmul(x, keys[...], NT)
    half = 2 * suffix
    top_half = row < 2 * span
    cache = jnp.where(top_half, cache[:, :half], cache[:, half:])
    wp, wn, wc = softmax_weights(prompt, new, cache, prompt_mask, new_mask, cache_mask)
    wc = jnp.concatenate(
        [jnp.where(top_half, wc, 0.0), jnp.where(top_half, 0.0, wc)], axis=1
    ).astype(jnp.bfloat16)
    wn = pltpu.roll(wn, steps, 1).astype(jnp.bfloat16)
    mixed = (
        matmul(spread_slot(wp, slot, slots), pv[...], NN)
        + matmul(wn, x, NN)
        + matmul(wc, values[...], NN)
    )
    mixed = (mixed * alive).astype(jnp.bfloat16)
    row, col = iota((4 * steps, 4 * span), 0), iota((4 * steps, 4 * span), 1)
    cols = []
    for h in range(groups):
        take = ((row // steps) == (col // span)) & ((col % span) == h * steps + row % steps)
        cols.append(matmul(take.astype(jnp.bfloat16), mixed, NN).astype(jnp.bfloat16))
    return jnp.concatenate(cols, axis=1)


def start_rows(first_row, hbm, vmem, sems, steps, suffix):
    rows = vmem[0].shape[0]
    part = pl.ds(first_row * steps, rows * steps)
    keys = pl.ds(first_row * suffix, rows * suffix)
    q, nk, nv, ck, cv = hbm
    return [
        load([(q.at[pl.ds(first_row, rows)], vmem[0]), (ck.at[keys], vmem[3])], sems.at[0]),
        load([(nk.at[part], vmem[1]), (nv.at[part], vmem[2])], sems.at[1]),
        load([(cv.at[keys], vmem[4])], sems.at[2]),
    ]


def attend_rows(lookup, first_row, waits, vmem, pk, pv, heads, work, *, steps, slots, suffix):
    q3, nk, nv, ck, cv = vmem
    q, meta, cache_scores, weights, cache_weights, mixed = work
    count, _, n, _ = meta.shape
    rows = n // steps
    per = 16 // steps
    for b in range(count * rows):
        low = b % rows * steps
        fill_meta(lookup, first_row + b, slice(low, low + steps), meta.at[b // rows])
    waits[0]()
    for b in range(0, count * rows, per):
        part = [q3[b + i].astype(jnp.float32) for i in range(per)]
        q[b * steps : (b + per) * steps, :] = jnp.concatenate(part, axis=0).astype(q.dtype)
    keys = rows * suffix
    for i in range(count):
        attend_scores(
            q.at[pl.ds(i * n, n)], ck.at[pl.ds(i * keys, keys)], cache_scores.at[i], steps=steps, suffix=suffix
        )
    waits[1]()
    for i in range(count):
        part = pl.ds(i * n, n)
        attend_block(
            q.at[part], nk.at[part], nv.at[part], cv.at[pl.ds(i * keys, keys)], pk, pv, heads.at[part],
            meta.at[i], cache_scores.at[i], weights.at[i], cache_weights.at[i], mixed.at[i],
            waits[2] if i == 0 else None, steps=steps, slots=slots, suffix=suffix,
        )


def first_kernel(
    fork, pairs, row_slot, prompt_lengths, cache_lengths, finished, q, nk, nv, ck, cv, own_keys, own_values, w_own, w_sib,
    *rest, stacked, replicas, slots, moved, steps, suffix, span
):
    recvs, rest = rest[:-24], rest[-24:]
    heads, pk, pv, w_there, x, keys, values, moved_meta = rest[:8]
    vmem, work, (row_sems, slot_sems, w_sems, sems, cache_sems) = rest[8:13], rest[13:19], rest[19:]
    me = lax.axis_index("replica")
    held, prefix = own_keys.shape[0], own_keys.shape[1]
    waits = start_rows(0, (q, nk, nv, ck, cv), vmem, row_sems, steps, suffix)
    for s in range(slots):
        prompt = fork[s, me]
        owner = lax.div(prompt, held)
        offset = lax.rem(prompt, held)
        targets = (pk.at[pl.ds(s * prefix, prefix)], pv.at[pl.ds(s * prefix, prefix)])
        if stacked:
            for i in range(2):
                pltpu.make_async_copy(
                    recvs[0].at[owner, pl.ds(i * prefix, prefix)], targets[i], slot_sems.at[s, i]
                ).start()
            continue
        k = lax.rem(me - owner + replicas, replicas)

        @pl.when(k == 0)
        def _():
            pltpu.make_async_copy(own_keys.at[offset], targets[0], slot_sems.at[s, 0]).start()
            pltpu.make_async_copy(own_values.at[offset], targets[1], slot_sems.at[s, 1]).start()

        for kk in range(1, replicas):

            @pl.when(k == kk)
            def _():
                for i in range(2):
                    pltpu.make_async_copy(
                        recvs[kk - 1].at[pl.ds(i * prefix, prefix)], targets[i], slot_sems.at[s, i]
                    ).start()

    groups = q.shape[2] // HEAD_DIM
    for i in range(moved):
        peer = pairs[moved + 1 + i]
        if stacked:
            pltpu.make_async_copy(
                recvs[0].at[peer, pl.ds(2 * prefix, span)], x.at[pl.ds(i * span, span)], sems.at[i]
            ).start()
        else:
            k = lax.rem(me - peer + replicas, replicas)
            for kk in range(1, replicas):

                @pl.when(k == kk)
                def _():
                    pltpu.make_async_copy(
                        recvs[kk - 1].at[pl.ds(2 * prefix, span)], x.at[pl.ds(i * span, span)], sems.at[i]
                    ).start()

    copies = []
    for i in range(moved):
        source = pl.ds(pl.multiple_of(pairs[i] * suffix, suffix), suffix)
        target = pl.ds(i * suffix, suffix)
        copies += [(ck.at[source], keys.at[target]), (cv.at[source], values.at[target])]
    caches_ready = load(copies, cache_sems)
    width, model = w_own.shape[0], w_there.shape[1]
    at = columns(model, 2)
    weights_ready = load(
        [(w_own.at[:, at], w_there.at[pl.ds(0, width)]), (w_sib.at[:, at], w_there.at[pl.ds(width, width)])], w_sems
    )

    def wait_second():
        waits[1]()
        for s in range(slots):
            for i, target in enumerate((pk, pv)):
                pltpu.make_async_copy(own_keys.at[0], target.at[pl.ds(s * prefix, prefix)], slot_sems.at[s, i]).wait()

    lookup = (row_slot, fork, prompt_lengths, cache_lengths, finished, me, q.shape[0])
    for i in range(moved):
        fill_meta(lookup, pairs[i], slice(i * span, (i + 1) * span), moved_meta)
    n = heads.shape[0] - moved * steps
    attend_rows(
        lookup, 0, (waits[0], wait_second, waits[2]), vmem, pk, pv, heads.at[pl.ds(0, n)], work,
        steps=steps, slots=slots, suffix=suffix,
    )
    for i in range(moved):
        source = recvs[0].at[0, pl.ds(0, span)] if stacked else recvs[0].at[pl.ds(0, span)]
        pltpu.make_async_copy(source, x.at[pl.ds(i * span, span)], sems.at[i]).wait()
    caches_ready()
    for g in range(moved // 4):
        part = slice(g * 4 * span, (g + 1) * 4 * span)
        kpart = slice(g * 4 * suffix, (g + 1) * 4 * suffix)
        heads[n + g * 4 * steps : n + (g + 1) * 4 * steps, :] = moved_block(
            x[part, :], pk, pv, keys.at[kpart], values.at[kpart],
            moved_meta[0, part, :], moved_meta[1, part, :], moved_meta[2, part, :],
            moved_meta[3, part, :].astype(jnp.float32),
            steps=steps, slots=slots, groups=groups, span=span, suffix=suffix,
        )
    weights_ready()


def second_kernel(
    fork, row_slot, prompt_lengths, cache_lengths, finished, pk, pv, q, nk, nv, ck, cv, after, *rest,
    first_row, slots, steps, suffix
):
    heads, vmem, work, row_sems = rest[0], rest[1:6], rest[6:12], rest[12]
    waits = start_rows(first_row, (q, nk, nv, ck, cv), vmem, row_sems, steps, suffix)
    lookup = (row_slot, fork, prompt_lengths, cache_lengths, finished, lax.axis_index("replica"), q.shape[0])
    attend_rows(
        lookup, first_row, waits, vmem, pk, pv, heads, work, steps=steps, slots=slots, suffix=suffix
    )


def project_kernel(h_own, h_sib, weights, out):
    rows = pl.ds(0, out.shape[0])
    both = jnp.concatenate([h_own[rows, :], h_sib[rows, :]], axis=1)
    out[...] = matmul(both, weights[...], NN).astype(out.dtype)


def base_kernel(
    h_first, s_first, h_second, s_second, h_moved, w_own, w_sib, residual, out, moved_out, weights, before, sems
):
    rows, model = out.shape
    width = w_own.shape[0]
    steps = residual.shape[1]
    at = columns(model, 0)
    ready = load(
        [
            (w_own.at[:, at], weights.at[pl.ds(0, width)]),
            (w_sib.at[:, at], weights.at[pl.ds(width, width)]),
            (residual, before),
        ],
        sems,
    )
    ready()
    moved_out[...] = matmul(h_moved[...], weights[...], NN)
    low = 0
    for h_own, h_sib, size in ((h_first, s_first, rows - h_second.shape[0]), (h_second, s_second, h_second.shape[0])):
        part = pl.ds(0, size)
        total = matmul(jnp.concatenate([h_own[part, :], h_sib[part, :]], axis=1), weights[...], NN)
        for b in range(0, size, steps):
            out[low : low + steps, :] = total[b : b + steps] + before[low // steps].astype(jnp.float32)
            low += steps


def moved_send_kernel(pairs, h_own, h_sib, after, *outs, moved, steps, split):
    me = lax.axis_index("replica")
    rows = pl.ds(h_own.shape[0] - moved * steps, moved * steps)
    both = jnp.concatenate([h_own[rows, :], h_sib[rows, :]], axis=1).astype(jnp.float32)
    for i in range(moved):
        peer = pairs[moved + 1 + i]
        value = both[i * steps : (i + 1) * steps].astype(outs[0].dtype)
        if split:
            k = jnp.bitwise_xor(me, peer)
            place = 2 * lax.rem(lax.div(k, 2), 2) + lax.div(k, 4)

            @pl.when(lax.rem(k, 2) == 0)
            def _():
                outs[0][place] = value

            @pl.when(lax.rem(k, 2) == 1)
            def _():
                outs[1][place] = value

        else:
            outs[0][peer] = value


def moved_project_kernel(pairs, w_there, *rest, moved, steps, split):
    backs, (cross, both_out, heads) = rest[:-3], rest[-3:]
    me = lax.axis_index("replica")
    for i in range(moved):
        peer = pairs[moved + 1 + i]
        part = slice(i * steps, (i + 1) * steps)
        if split:
            k = jnp.bitwise_xor(me, peer)
            places = {1: (0, 0), 2: (1, 0), 3: (1, 2), 4: (2, 0), 5: (2, 1), 6: (2, 2), 7: (2, 3)}
            for d, (which, index) in places.items():

                @pl.when(k == d)
                def _():
                    heads[part, :] = backs[which][index].astype(jnp.float32)

        else:
            heads[part, :] = backs[0][peer].astype(jnp.float32)
    both = heads[...].astype(cross.dtype)
    both_out[...] = both
    cross[...] = matmul(both, w_there[...], NN).astype(cross.dtype)


def add_rows(total, out, first, steps):
    for b in range(total.shape[0] // steps):
        out[first + b] = total[b * steps : (b + 1) * steps].astype(out.dtype)


def finish_first_kernel(base, recv, out):
    rows, steps = out.shape[:2]
    part = pl.ds(pl.multiple_of(pl.program_id(0) * rows * steps, rows * steps), rows * steps)
    add_rows(base[part, :] + recv[part, :].astype(jnp.float32), out, 0, steps)


def finish_second_kernel(
    pairs, base, recv, base_moved, recv_moved, residual, earlier, out, before, after, rows_out, sems, row_sems, *, moved
):
    later, steps = rows_out.shape[:2]
    half = out.shape[0] - later
    n = half * steps
    fetch = [load([(residual.at[pairs[i]], before.at[i])], sems.at[i]) for i in range(moved)]
    add_rows(base[n:, :] + recv[...].astype(jnp.float32), rows_out, 0, steps)
    branch = base_moved[...] + recv_moved[...].astype(jnp.float32)
    for i in range(moved):
        r = pairs[i]
        fetch[i]()
        value = branch[i * steps : (i + 1) * steps] + before[i].astype(jnp.float32)
        after[i] = value.astype(after.dtype)

        @pl.when(r >= half)
        def _():
            rows_out[jnp.maximum(r - half, 0)] = after[i]

        @pl.when(r < half)
        def _():
            pltpu.make_async_copy(after.at[i], out.at[r], sems.at[i, 0]).start()

    done = load([(rows_out, out.at[pl.ds(half, later)])], row_sems)
    for i in range(moved):
        r = pairs[i]

        @pl.when(r < half)
        def _():
            pltpu.make_async_copy(after.at[i], out.at[r], sems.at[i, 0]).wait()

    done()


def row_buffers(count, steps, width, dtype):
    return [pltpu.VMEM((count, steps, size), dtype) for size in (width, HEAD_DIM, HEAD_DIM)]


def exchange_pack(
    fork, partner, row_slot, queries, new_keys, new_values, fork_table, prompt_keys, prompt_values, span, moved
):
    replicas = lax.axis_size("replica")
    me = lax.axis_index("replica")
    local_rows, steps, width = queries.shape
    groups = width // HEAD_DIM
    held, prefix = prompt_keys.shape[:2]
    dtype = queries.dtype
    pairs_shape = jax.ShapeDtypeStruct((2 * (moved + 1) + replicas,), jnp.int32)
    if replicas <= 8:
        shifts = tuple(range(1, replicas))
        count = len(shifts)
        *packed, pairs = pl.pallas_call(
            functools.partial(pack_kernel, replicas=replicas, moved=moved, shifts=shifts),
            out_shape=[pltpu.VMEM((2 * prefix + span, HEAD_DIM), dtype)] * count + [pairs_shape],
            in_specs=[SMEM, SMEM] + [ANY] * 5,
            out_specs=[VMEM] * count + [SMEM],
            scratch_shapes=row_buffers(count, steps, width, dtype)
            + [
                pltpu.SMEM((replicas,), jnp.int32),
                pltpu.SemaphoreType.DMA((count, 2)),
                pltpu.SemaphoreType.DMA((count, 3)),
            ],
            compiler_params=params(),
            name="pack",
        )(*in_hbm(fork, partner, queries, new_keys, new_values, prompt_keys, prompt_values))
        return packed, pairs
    chosen = (fork_table // held) == me
    offsets = jnp.sum(jnp.where(chosen, fork_table % held, 0), axis=1)
    peer_of = partner // local_rows
    pairing = (peer_of[None, :] == jnp.arange(replicas, dtype=jnp.int32)[:, None]) & (
        peer_of[None, :] != me
    )
    row_of = jnp.sum(jnp.where(pairing, jnp.arange(local_rows, dtype=jnp.int32)[None, :], 0), axis=1)
    q = queries[row_of].reshape(replicas, steps, groups, HEAD_DIM).transpose(0, 2, 1, 3)
    q = q.reshape(replicas, groups * steps, HEAD_DIM)
    pad = jnp.zeros((replicas, span - (groups + 2) * steps, HEAD_DIM), dtype)
    block = jnp.concatenate(
        [prompt_keys[offsets], prompt_values[offsets], q, new_keys[row_of], new_values[row_of], pad], axis=1
    )
    pairs = pl.pallas_call(
        functools.partial(pairs_kernel, replicas=replicas, local_rows=local_rows, moved=moved),
        out_shape=pairs_shape,
        in_specs=[SMEM],
        out_specs=SMEM,
        scratch_shapes=[pltpu.SMEM((replicas,), jnp.int32)],
        name="pairs",
    )(partner)
    return [block], pairs


def body(
    residual,
    queries,
    new_keys,
    new_values,
    cache_keys,
    cache_values,
    cache_lengths,
    finished,
    partner,
    row_slot,
    fork_table,
    prompt_keys,
    prompt_values,
    prompt_lengths,
    out_proj,
):
    replicas = lax.axis_size("replica")
    tensors = lax.axis_size("tensor")
    local_rows, steps, width = queries.shape
    groups = width // HEAD_DIM
    suffix = cache_keys.shape[1]
    held, prefix = prompt_keys.shape[:2]
    slots = fork_table.shape[1]
    moved = replicas // 2
    stacked = replicas > 8
    model = residual.shape[2]
    n = local_rows * steps
    span = 32
    dtype = queries.dtype
    fork = fork_table.T
    sibling = [(i, i ^ 1) for i in range(tensors)]
    across = [(i, i ^ 2) for i in range(tensors)]

    packed, pairs = exchange_pack(
        fork, partner, row_slot, queries, new_keys, new_values, fork_table, prompt_keys, prompt_values, span, moved
    )
    w_sib = lax.ppermute(out_proj, "tensor", sibling)
    nk2 = new_keys.reshape(n, HEAD_DIM)
    nv2 = new_values.reshape(n, HEAD_DIM)
    ck2 = cache_keys.reshape(local_rows * suffix, HEAD_DIM)
    cv2 = cache_values.reshape(local_rows * suffix, HEAD_DIM)
    lookup = (row_slot, prompt_lengths, cache_lengths, finished)

    dma = lambda *shape: pltpu.SemaphoreType.DMA(shape)
    blocks = local_rows // BLOCK
    nb = BLOCK * steps
    assert nb == HEAD_DIM
    if stacked:
        received = [lax.all_to_all(packed[0], "replica", split_axis=0, concat_axis=0, tiled=True)]
    else:
        received = [
            lax.ppermute(block, "replica", [(i, (i + k) % replicas) for i in range(replicas)])
            for k, block in enumerate(packed, 1)
        ]

    m = moved * steps
    half = FIRST
    nh = half * nb
    prompts = pltpu.VMEM((slots * prefix, HEAD_DIM), dtype)

    def work(count):
        rows = count * BLOCK
        return [
            pltpu.VMEM((rows, steps, width), dtype),
            pltpu.VMEM((rows * steps, HEAD_DIM), dtype),
            pltpu.VMEM((rows * steps, HEAD_DIM), dtype),
            pltpu.VMEM((rows * suffix, HEAD_DIM), dtype),
            pltpu.VMEM((rows * suffix, HEAD_DIM), dtype),
            pltpu.VMEM((rows * steps, width), dtype),
            pltpu.VMEM((count, 4, nb, HEAD_DIM), jnp.int32),
            pltpu.VMEM((count, groups, nb, HEAD_DIM), jnp.float32),
            pltpu.VMEM((count, groups * nb, slots * prefix + HEAD_DIM), jnp.bfloat16),
            pltpu.VMEM((count, groups, nb, 2 * HEAD_DIM), jnp.bfloat16),
            pltpu.VMEM((count, groups * nb, HEAD_DIM), jnp.float32),
            dma(3, 2),
        ]

    sizes = dict(slots=slots, steps=steps, suffix=suffix)
    lookup = in_hbm(row_slot, prompt_lengths, cache_lengths, finished)
    rows_in = in_hbm(queries, nk2, nv2, ck2, cv2)
    h_first, pk, pv, w_there = pl.pallas_call(
        functools.partial(first_kernel, stacked=stacked, replicas=replicas, moved=moved, span=span, **sizes),
        out_shape=[pltpu.VMEM((nh + m, width), dtype), prompts, prompts, pltpu.VMEM((2 * width, model), dtype)],
        in_specs=[SMEM] * 6 + [ANY] * (9 + len(received)),
        out_specs=[VMEM] * 4,
        scratch_shapes=[
            pltpu.VMEM((moved * span, HEAD_DIM), dtype),
            pltpu.VMEM((moved * suffix, HEAD_DIM), dtype),
            pltpu.VMEM((moved * suffix, HEAD_DIM), dtype),
            pltpu.VMEM((4, moved * span, HEAD_DIM), jnp.int32),
        ]
        + work(half)
        + [dma(slots, 2), dma(2), dma(moved), dma(2 * moved)],
        compiler_params=params(),
        cost_estimate=SMALL,
        name="attend_first",
    )(*in_hbm(fork, pairs), *lookup, *rows_in, *in_hbm(prompt_keys, prompt_values, out_proj), w_sib, *received)

    def call(kernel, name, shapes, specs, operands, extra=()):
        return pl.pallas_call(
            kernel,
            out_shape=[pltpu.VMEM(shape, kind) for shape, kind in shapes],
            in_specs=specs,
            out_specs=[VMEM] * len(shapes),
            scratch_shapes=list(extra),
            compiler_params=params(),
            cost_estimate=SMALL,
            name=name,
        )(*operands)

    def cross(heads, rows):
        sib = lax.ppermute(heads, "tensor", sibling)
        (crossed,) = call(project_kernel, "project", [((rows, model), dtype)], [VMEM] * 3, (heads, sib, w_there))
        return sib, crossed, lax.ppermute(crossed, "tensor", across)

    s_first, c_first, got_first = cross(h_first, nh)
    options = dict(moved=moved, steps=steps, split=not stacked)
    shape = ((replicas if stacked else 4, steps, 2 * width), dtype)
    back = call(
        functools.partial(moved_send_kernel, **options),
        "moved_send",
        [shape] * (1 if stacked else 2),
        [SMEM, VMEM, VMEM, ANY],
        (*in_hbm(pairs), h_first, s_first, c_first),
    )
    (h_second,) = call(
        functools.partial(second_kernel, first_row=half * BLOCK, **sizes),
        "attend_second",
        [((n - nh, width), dtype)],
        [SMEM] * 5 + [VMEM] * 2 + [ANY] * 6,
        (*in_hbm(fork), *lookup, pk, pv, *rows_in, c_first),
        work(blocks - half),
    )
    s_second, c_second, got_second = cross(h_second, n - nh)
    if stacked:
        backs = [lax.all_to_all(back[0], "replica", split_axis=0, concat_axis=0, tiled=True)]
    else:
        flip = lambda x, bit: lax.ppermute(x, "replica", [(i, i ^ bit) for i in range(replicas)])
        kept = back[0]
        one = flip(back[1], 1)
        one, *_ = lax.optimization_barrier((one, c_second))
        two = flip(jnp.concatenate([kept[2:], one[2:]]), 2)
        two, *_ = lax.optimization_barrier((two, got_first))
        four = flip(jnp.concatenate([kept[1:2], one[1:2], two[1:2], two[3:4]]), 4)
        backs = [one, two, four]
    crossed_moved, home_heads = call(
        functools.partial(moved_project_kernel, **options),
        "moved_project",
        [((m, model), dtype), ((m, 2 * width), dtype)],
        [SMEM] + [VMEM] * (1 + len(backs)),
        (*in_hbm(pairs), w_there, *backs),
        [pltpu.VMEM((m, 2 * width), jnp.float32)],
    )
    got_moved = lax.ppermute(crossed_moved, "tensor", across)
    base, base_moved = call(
        base_kernel,
        "base",
        [((n, model), jnp.float32), ((m, model), jnp.float32)],
        [VMEM] * 5 + [ANY] * 3,
        (h_first, s_first, h_second, s_second, home_heads, *in_hbm(out_proj), w_sib, *in_hbm(residual)),
        [pltpu.VMEM((2 * width, model), dtype), pltpu.VMEM(residual.shape, dtype), dma(3)],
    )

    whole = jax.ShapeDtypeStruct(residual.shape, residual.dtype)
    out = pl.pallas_call(
        finish_first_kernel,
        grid=(half,),
        in_specs=[VMEM, VMEM],
        out_specs=pl.BlockSpec((BLOCK, steps, model), lambda i: (i, 0, 0)),
        out_shape=whole,
        compiler_params=params(),
        name="finish_first",
    )(base, got_first)
    return pl.pallas_call(
        functools.partial(finish_second_kernel, moved=moved),
        in_specs=[SMEM, VMEM, VMEM, VMEM, VMEM, ANY, ANY],
        out_specs=ANY,
        out_shape=whole,
        input_output_aliases={6: 0},
        scratch_shapes=[
            pltpu.VMEM((moved, steps, model), dtype),
            pltpu.VMEM((moved, steps, model), dtype),
            pltpu.VMEM(((blocks - half) * BLOCK, steps, model), dtype),
            dma(moved, 1),
            dma(1),
        ],
        compiler_params=params(),
        name="finish_second",
    )(*in_hbm(pairs), base, got_second, base_moved, got_moved, *in_hbm(residual), out)


def solution(mesh):
    rows = P("replica", None, "tensor")
    in_specs = (rows,) * 6 + (P(), P(), P("replica"), P(), P(), rows, rows, P(), P("tensor", None))
    return jax.shard_map(body, mesh=mesh, in_specs=in_specs, out_specs=rows, check_vma=False)
```

```python
import functools
import math

import jax
import jax.numpy as jnp
from jax import lax
from jax.experimental import pallas as pl
from jax.experimental.pallas import tpu as pltpu
from jax.sharding import PartitionSpec as P

HEAD_DIM = 128
LOWEST = -1e30
EXP2_SCALE = math.log2(math.e) / math.sqrt(HEAD_DIM)
VMEM_BYTES = 24 * 1024 * 1024
SMALL = pl.CostEstimate(flops=1, bytes_accessed=1, transcendentals=0)
BLOCK = 32
FIRST = 2
NT = (((1,), (1,)), ((), ()))
NN = (((1,), (0,)), ((), ()))

ANY = pl.BlockSpec(memory_space=pl.ANY)
SMEM = pl.BlockSpec(memory_space=pltpu.SMEM)
VMEM = pl.BlockSpec(memory_space=pltpu.VMEM)


def params(side_effects=False):
    return pltpu.CompilerParams(vmem_limit_bytes=VMEM_BYTES, has_side_effects=side_effects)


def matmul(a, b, dims):
    return lax.dot_general(a, b, dims, preferred_element_type=jnp.float32)


def columns(model, flip):
    place = jnp.bitwise_xor(lax.axis_index("tensor"), flip)
    return pl.ds(pl.multiple_of(place * model, HEAD_DIM), model)


def in_hbm(*arrays):
    return [pltpu.with_memory_space_constraint(x, pltpu.HBM) for x in arrays]


def iota(shape, dim):
    return lax.broadcasted_iota(jnp.int32, shape, dim)


def load(pairs, sem):
    copies = [pltpu.make_async_copy(a, b, sem.at[i]) for i, (a, b) in enumerate(pairs)]
    for copy in copies:
        copy.start()

    def wait():
        for copy in copies:
            copy.wait()

    return wait


def quotient(a, b):
    return a >> (b.bit_length() - 1) if b & (b - 1) == 0 else lax.div(a, b)


def remainder(a, b):
    return a & (b - 1) if b & (b - 1) == 0 else lax.rem(a, b)


def list_pairs(row_of, pairs, me, replicas, moved):
    count = jnp.int32(0)
    for j in range(replicas):
        pairs[count] = row_of[j]
        pairs[moved + 1 + count] = j
        pairs[2 * (moved + 1) + j] = jnp.maximum(row_of[j], 0)
        count = jnp.minimum(count + jnp.where((row_of[j] >= 0) & (j != me), 1, 0), moved)


def find_pairs(partner, row_of, replicas, local_rows):
    for j in range(replicas):
        row_of[j] = -1

    def note(r, carry):
        row_of[quotient(partner[r], local_rows)] = r
        return carry

    lax.fori_loop(0, local_rows, note, 0, unroll=8)


def send_prompts(shifts, fork, keys, values, outs, sems, replicas):
    me = lax.axis_index("replica")
    held, prefix = keys.shape[0], keys.shape[1]
    waits = []
    for i, k in enumerate(shifts):
        peer = remainder(me + k, replicas)
        offset = jnp.int32(0)
        for s in range(fork.shape[0]):
            prompt = fork[s, peer]
            offset = jnp.where(quotient(prompt, held) == me, remainder(prompt, held), offset)
        copies = [
            (source.at[offset], outs[i].at[pl.ds(n * prefix, prefix)]) for n, source in enumerate((keys, values))
        ]
        waits.append(load(copies, sems.at[i]))
    return waits


def send_rows(shifts, row_of, hbm, vmem, outs, sems, replicas, prefix):
    me = lax.axis_index("replica")
    width = hbm[0].shape[2]
    waits = []
    for i, k in enumerate(shifts):
        r = row_of(remainder(me + k, replicas))
        waits.append(load([(a.at[r], b.at[i]) for a, b in zip(hbm, vmem)], sems.at[i]))
    for i in range(len(shifts)):
        waits[i]()
        q, nk, nv = [v[i].astype(jnp.float32) for v in vmem]
        parts = [q[:, low : low + HEAD_DIM] for low in range(0, width, HEAD_DIM)] + [nk, nv]
        pad = outs[i].shape[0] - 2 * prefix - sum(p.shape[0] for p in parts)
        parts += [jnp.zeros((pad, HEAD_DIM), jnp.float32)]
        outs[i][2 * prefix :, :] = jnp.concatenate(parts, axis=0).astype(outs[i].dtype)


def pairs_kernel(partner, pairs, row_of, *, replicas, local_rows, moved):
    find_pairs(partner, row_of, replicas, local_rows)
    list_pairs(row_of, pairs, lax.axis_index("replica"), replicas, moved)


def pack_kernel(
    fork, partner, queries, new_keys, new_values, keys, values, *rest, replicas, moved, shifts
):
    outs, (pairs, qv, nkv, nvv, row_of, sems, row_sems) = rest[: len(shifts)], rest[len(shifts) :]
    waits = send_prompts(shifts, fork, keys, values, outs, sems, replicas)
    find_pairs(partner, row_of, replicas, queries.shape[0])
    list_pairs(row_of, pairs, lax.axis_index("replica"), replicas, moved)
    send_rows(
        shifts, lambda j: jnp.maximum(row_of[j], 0), (queries, new_keys, new_values), (qv, nkv, nvv), outs, row_sems,
        replicas, keys.shape[1],
    )
    for wait in waits:
        wait()


def softmax_weights(prompt, new, cache, prompt_mask, new_mask, cache_mask):
    prompt = jnp.where(prompt_mask, prompt, LOWEST)
    new = jnp.where(new_mask, new, LOWEST)
    cache = jnp.where(cache_mask, cache, LOWEST)
    top = jnp.max(jnp.maximum(jnp.maximum(prompt, new), cache), axis=1, keepdims=True)
    prompt = jnp.exp2((prompt - top) * EXP2_SCALE)
    new = jnp.exp2((new - top) * EXP2_SCALE)
    cache = jnp.exp2((cache - top) * EXP2_SCALE)
    inverse = 1.0 / jnp.sum(prompt + new + cache, axis=1, keepdims=True)
    return prompt * inverse, new * inverse, cache * inverse


def pick_slot(scores, slot, slots, prefix):
    picked = scores[:, :prefix]
    for s in range(1, slots):
        picked = jnp.where(slot == s, scores[:, s * prefix : (s + 1) * prefix], picked)
    return picked


def spread_slot(weights, slot, slots):
    return jnp.concatenate(
        [jnp.where(slot == s, weights, 0.0).astype(jnp.bfloat16) for s in range(slots)], axis=1
    )


def row_values(slots_of, lengths, finished, fork, prompt_lengths, slots):
    me = lax.axis_index("replica")
    shape = (HEAD_DIM, slots_of.shape[1])
    slot, length, done = [jnp.broadcast_to(v[pl.ds(me, 1), :], shape) for v in (slots_of, lengths, finished)]
    prompt = jnp.zeros(shape, jnp.int32)
    for s in range(slots):
        prompt = jnp.where(slot == s, prompt_lengths[fork[s, me]], prompt)
    return [v.astype(jnp.float32).astype(jnp.bfloat16) for v in (slot, prompt, length, 1 - done)]


def fill_meta(values, row_of, meta):
    take = (row_of == iota(row_of.shape, 1)).astype(jnp.float32).astype(jnp.bfloat16)
    for i, value in enumerate(values):
        meta[i] = matmul(take, value, NT).astype(jnp.int32)


def attend_scores(q, ck, cache_scores, *, steps, suffix):
    n = q.shape[0]
    groups = q.shape[1] // HEAD_DIM
    keys_sub = 4 * suffix
    half = 2 * suffix
    for sub in range(n // 16):
        r0 = sub * 16
        qs = jnp.concatenate(
            [q[r0 : r0 + 16, h * HEAD_DIM : (h + 1) * HEAD_DIM] for h in range(groups)], axis=0
        )
        s = matmul(qs, ck[sub * keys_sub : (sub + 1) * keys_sub, :], NT)
        for h in range(groups):
            cache_scores[h, r0 : r0 + 8, :] = s[16 * h : 16 * h + 8, :half]
            cache_scores[h, r0 + 8 : r0 + 16, :] = s[16 * h + 8 : 16 * h + 16, half:]


def attend_block(
    q, nk, nv, cv, pk, pv, heads, meta, cache_scores, weights, cache_weights, mixed, wait,
    *, steps, slots, suffix
):
    n = q.shape[0]
    groups = q.shape[1] // HEAD_DIM
    prefix = pk.shape[0] // slots
    keys_sub = 4 * suffix
    half = 2 * suffix
    shape = (n, HEAD_DIM)
    lane, row = iota(shape, 1), iota(shape, 0)
    cache_own = (lane // suffix) == ((row % 8) // steps)
    cache_lane = jnp.where(cache_own, lane % suffix, suffix)
    new_mask = ((lane // steps) == (row // steps)) & ((lane % steps) <= (row % steps))
    first_half = (row % 16) < 8
    slot = meta[0]
    prompt_mask = lane < meta[1]
    cache_mask = cache_lane < meta[2]
    alive_rows = meta[3].astype(jnp.float32)
    q_all = jnp.concatenate([q[:, h * HEAD_DIM : (h + 1) * HEAD_DIM] for h in range(groups)], axis=0)
    prompt_all = matmul(q_all, pk[...], NT)
    new_all = matmul(q_all, nk[...], NT)
    for h in range(groups):
        part = slice(h * n, (h + 1) * n)
        prompt = pick_slot(prompt_all[part], slot, slots, prefix)
        wp, wn, wc = softmax_weights(
            prompt, new_all[part], cache_scores[h], prompt_mask, new_mask, cache_mask
        )
        cache_weights[h, :, :half] = jnp.where(first_half, wc, 0.0).astype(jnp.bfloat16)
        cache_weights[h, :, half:] = jnp.where(first_half, 0.0, wc).astype(jnp.bfloat16)
        weights[part, : slots * prefix] = spread_slot(wp, slot, slots)
        weights[part, slots * prefix :] = wn.astype(jnp.bfloat16)
    mixed[...] = matmul(weights[:, : slots * prefix], pv[...], NN) + matmul(
        weights[:, slots * prefix :], nv[...], NN
    )
    if wait is not None:
        wait()
    for sub in range(n // 16):
        r0 = sub * 16
        w = jnp.concatenate([cache_weights[h, r0 : r0 + 16, :] for h in range(groups)], axis=0)
        o = matmul(w, cv[sub * keys_sub : (sub + 1) * keys_sub, :], NN)
        for h in range(groups):
            total = mixed[h * n + r0 : h * n + r0 + 16, :] + o[16 * h : 16 * h + 16, :]
            heads[r0 : r0 + 16, h * HEAD_DIM : (h + 1) * HEAD_DIM] = (
                total * alive_rows[r0 : r0 + 16, :]
            ).astype(heads.dtype)


def moved_block(x, pk, pv, keys, values, slot, plen, clen, alive, *, steps, slots, groups, span, suffix):
    prefix = pk.shape[0] // slots
    shape = (4 * span, HEAD_DIM)
    lane, row = iota(shape, 1), iota(shape, 0)
    prompt_mask = lane < plen
    cache_mask = ((lane // suffix) == ((row // span) % 2)) & ((lane % suffix) < clen)
    past = (lane % span) - groups * steps
    new_mask = ((lane // span) == (row // span)) & (past >= 0) & (past <= row % steps)
    prompt = pick_slot(matmul(x, pk[...], NT), slot, slots, prefix)
    new = matmul(x, x, NT)
    cache = matmul(x, keys[...], NT)
    half = 2 * suffix
    top_half = row < 2 * span
    cache = jnp.where(top_half, cache[:, :half], cache[:, half:])
    wp, wn, wc = softmax_weights(prompt, new, cache, prompt_mask, new_mask, cache_mask)
    wc = jnp.concatenate(
        [jnp.where(top_half, wc, 0.0), jnp.where(top_half, 0.0, wc)], axis=1
    ).astype(jnp.bfloat16)
    wn = pltpu.roll(wn, steps, 1).astype(jnp.bfloat16)
    mixed = (
        matmul(spread_slot(wp, slot, slots), pv[...], NN)
        + matmul(wn, x, NN)
        + matmul(wc, values[...], NN)
    )
    mixed = (mixed * alive).astype(jnp.bfloat16)
    row, col = iota((4 * steps, 4 * span), 0), iota((4 * steps, 4 * span), 1)
    cols = []
    for h in range(groups):
        take = ((row // steps) == (col // span)) & ((col % span) == h * steps + row % steps)
        cols.append(matmul(take.astype(jnp.bfloat16), mixed, NN).astype(jnp.bfloat16))
    return jnp.concatenate(cols, axis=1)


def start_rows(first_row, hbm, vmem, sems, steps, suffix):
    rows = vmem[0].shape[0]
    part = pl.ds(first_row * steps, rows * steps)
    keys = pl.ds(first_row * suffix, rows * suffix)
    q, nk, nv, ck, cv = hbm
    first = load([(q.at[pl.ds(first_row, rows)], vmem[0]), (ck.at[keys], vmem[3])], sems.at[0])

    def rest():
        return [
            load([(nk.at[part], vmem[1]), (nv.at[part], vmem[2])], sems.at[1]),
            load([(cv.at[keys], vmem[4])], sems.at[2]),
        ]

    return first, rest


def attend_rows(lookup, first_row, waits, vmem, pk, pv, heads, work, *, steps, slots, suffix):
    q3, nk, nv, ck, cv = vmem
    q, meta, cache_scores, weights, cache_weights, mixed = work
    count, _, n, _ = meta.shape
    rows = n // steps
    per = 16 // steps
    shape = (n, lookup[0].shape[1])
    for i in range(count):
        fill_meta(lookup, first_row + i * rows + iota(shape, 0) // steps, meta.at[i])
    waits[0]()
    for b in range(0, count * rows, per):
        part = [q3[b + i].astype(jnp.float32) for i in range(per)]
        q[b * steps : (b + per) * steps, :] = jnp.concatenate(part, axis=0).astype(q.dtype)
    keys = rows * suffix
    for i in range(count):
        attend_scores(
            q.at[pl.ds(i * n, n)], ck.at[pl.ds(i * keys, keys)], cache_scores.at[i], steps=steps, suffix=suffix
        )
    waits[1]()
    for i in range(count):
        part = pl.ds(i * n, n)
        attend_block(
            q.at[part], nk.at[part], nv.at[part], cv.at[pl.ds(i * keys, keys)], pk, pv, heads.at[part],
            meta.at[i], cache_scores.at[i], weights.at[i], cache_weights.at[i], mixed.at[i],
            waits[2] if i == 0 else None, steps=steps, slots=slots, suffix=suffix,
        )


def first_kernel(
    fork, pairs, prompt_lengths, row_slot, cache_lengths, finished, q, nk, nv, ck, cv, own_keys, own_values, w_own, w_sib,
    *rest, stacked, replicas, slots, moved, steps, suffix, span
):
    recvs, rest = rest[:-24], rest[-24:]
    heads, pk, pv, w_there, x, keys, values, moved_meta = rest[:8]
    vmem, work, (row_sems, slot_sems, w_sems, sems, cache_sems) = rest[8:13], rest[13:19], rest[19:]
    me = lax.axis_index("replica")
    held, prefix = own_keys.shape[0], own_keys.shape[1]
    scores_ready, start_rest = start_rows(0, (q, nk, nv, ck, cv), vmem, row_sems, steps, suffix)
    for s in range(slots):
        prompt = fork[s, me]
        owner = quotient(prompt, held)
        offset = remainder(prompt, held)
        targets = (pk.at[pl.ds(s * prefix, prefix)], pv.at[pl.ds(s * prefix, prefix)])
        if stacked:
            for i in range(2):
                pltpu.make_async_copy(
                    recvs[0].at[owner, pl.ds(i * prefix, prefix)], targets[i], slot_sems.at[s, i]
                ).start()
            continue
        k = remainder(me - owner + replicas, replicas)

        @pl.when(k == 0)
        def _():
            pltpu.make_async_copy(own_keys.at[offset], targets[0], slot_sems.at[s, 0]).start()
            pltpu.make_async_copy(own_values.at[offset], targets[1], slot_sems.at[s, 1]).start()

        for kk in range(1, replicas):

            @pl.when(k == kk)
            def _():
                for i in range(2):
                    pltpu.make_async_copy(
                        recvs[kk - 1].at[pl.ds(i * prefix, prefix)], targets[i], slot_sems.at[s, i]
                    ).start()

    waits = [scores_ready, *start_rest()]
    groups = q.shape[2] // HEAD_DIM
    for i in range(moved):
        peer = pairs[moved + 1 + i]
        if stacked:
            pltpu.make_async_copy(
                recvs[0].at[peer, pl.ds(2 * prefix, span)], x.at[pl.ds(i * span, span)], sems.at[i]
            ).start()
        else:
            k = remainder(me - peer + replicas, replicas)
            for kk in range(1, replicas):

                @pl.when(k == kk)
                def _():
                    pltpu.make_async_copy(
                        recvs[kk - 1].at[pl.ds(2 * prefix, span)], x.at[pl.ds(i * span, span)], sems.at[i]
                    ).start()

    copies = []
    for i in range(moved):
        source = pl.ds(pl.multiple_of(pairs[i] * suffix, suffix), suffix)
        target = pl.ds(i * suffix, suffix)
        copies += [(ck.at[source], keys.at[target]), (cv.at[source], values.at[target])]
    caches_ready = load(copies, cache_sems)
    width, model = w_own.shape[0], w_there.shape[1]
    at = columns(model, 2)
    weights_ready = load(
        [(w_own.at[:, at], w_there.at[pl.ds(0, width)]), (w_sib.at[:, at], w_there.at[pl.ds(width, width)])], w_sems
    )

    def wait_second():
        waits[1]()
        for s in range(slots):
            for i, target in enumerate((pk, pv)):
                pltpu.make_async_copy(own_keys.at[0], target.at[pl.ds(s * prefix, prefix)], slot_sems.at[s, i]).wait()

    lookup = row_values(row_slot, cache_lengths, finished, fork, prompt_lengths, slots)
    shape = (moved * span, row_slot.shape[1])
    item = iota(shape, 0) // span
    row_of = jnp.zeros(shape, jnp.int32)
    for i in range(moved):
        row_of = jnp.where(item == i, pairs[i], row_of)
    fill_meta(lookup, row_of, moved_meta)
    n = heads.shape[0] - moved * steps
    attend_rows(
        lookup, 0, (waits[0], wait_second, waits[2]), vmem, pk, pv, heads.at[pl.ds(0, n)], work,
        steps=steps, slots=slots, suffix=suffix,
    )
    for i in range(moved):
        source = recvs[0].at[0, pl.ds(0, span)] if stacked else recvs[0].at[pl.ds(0, span)]
        pltpu.make_async_copy(source, x.at[pl.ds(i * span, span)], sems.at[i]).wait()
    caches_ready()
    for g in range(moved // 4):
        part = slice(g * 4 * span, (g + 1) * 4 * span)
        kpart = slice(g * 4 * suffix, (g + 1) * 4 * suffix)
        heads[n + g * 4 * steps : n + (g + 1) * 4 * steps, :] = moved_block(
            x[part, :], pk, pv, keys.at[kpart], values.at[kpart],
            moved_meta[0, part, :], moved_meta[1, part, :], moved_meta[2, part, :],
            moved_meta[3, part, :].astype(jnp.float32),
            steps=steps, slots=slots, groups=groups, span=span, suffix=suffix,
        )
    weights_ready()


def second_kernel(
    fork, prompt_lengths, row_slot, cache_lengths, finished, pk, pv, q, nk, nv, ck, cv, after, *rest,
    first_row, slots, steps, suffix
):
    heads, vmem, work, row_sems = rest[0], rest[1:6], rest[6:12], rest[12]
    scores_ready, start_rest = start_rows(first_row, (q, nk, nv, ck, cv), vmem, row_sems, steps, suffix)
    waits = [scores_ready, *start_rest()]
    lookup = row_values(row_slot, cache_lengths, finished, fork, prompt_lengths, slots)
    attend_rows(
        lookup, first_row, waits, vmem, pk, pv, heads, work, steps=steps, slots=slots, suffix=suffix
    )


def project_kernel(h_own, h_sib, weights, out):
    rows = pl.ds(0, out.shape[0])
    both = jnp.concatenate([h_own[rows, :], h_sib[rows, :]], axis=1)
    out[...] = matmul(both, weights[...], NN).astype(out.dtype)


def base_kernel(
    pairs, h_first, s_first, h_second, s_second, h_moved, w_own, w_sib, residual, out, moved_out, weights, before, sems
):
    rows, model = out.shape
    width = w_own.shape[0]
    steps = residual.shape[1]
    at = columns(model, 0)
    ready = load(
        [
            (w_own.at[:, at], weights.at[pl.ds(0, width)]),
            (w_sib.at[:, at], weights.at[pl.ds(width, width)]),
            (residual, before),
        ],
        sems,
    )
    ready()
    moved_total = matmul(h_moved[...], weights[...], NN)
    for i in range(h_moved.shape[0] // steps):
        part = slice(i * steps, (i + 1) * steps)
        moved_out[part, :] = moved_total[part] + before[pairs[i]].astype(jnp.float32)
    low = 0
    for h_own, h_sib, size in ((h_first, s_first, rows - h_second.shape[0]), (h_second, s_second, h_second.shape[0])):
        part = pl.ds(0, size)
        total = matmul(jnp.concatenate([h_own[part, :], h_sib[part, :]], axis=1), weights[...], NN)
        for b in range(0, size, steps):
            out[low : low + steps, :] = total[b : b + steps] + before[low // steps].astype(jnp.float32)
            low += steps


def moved_send_kernel(pairs, h_own, h_sib, after, *outs, moved, steps, split):
    me = lax.axis_index("replica")
    rows = pl.ds(h_own.shape[0] - moved * steps, moved * steps)
    both = jnp.concatenate([h_own[rows, :], h_sib[rows, :]], axis=1).astype(jnp.float32)
    for i in range(moved):
        peer = pairs[moved + 1 + i]
        value = both[i * steps : (i + 1) * steps].astype(outs[0].dtype)
        if split:
            k = jnp.bitwise_xor(me, peer)
            place = 2 * remainder(quotient(k, 2), 2) + quotient(k, 4)

            @pl.when(remainder(k, 2) == 0)
            def _():
                outs[0][place] = value

            @pl.when(remainder(k, 2) == 1)
            def _():
                outs[1][place] = value

        else:
            outs[0][peer] = value


def moved_project_kernel(pairs, w_there, *rest, moved, steps, split):
    backs, (cross, both_out, heads) = rest[:-3], rest[-3:]
    me = lax.axis_index("replica")
    for i in range(moved):
        peer = pairs[moved + 1 + i]
        part = slice(i * steps, (i + 1) * steps)
        if split:
            k = jnp.bitwise_xor(me, peer)
            places = {1: (0, 0), 2: (1, 0), 3: (1, 2), 4: (2, 0), 5: (2, 1), 6: (2, 2), 7: (2, 3)}
            for d, (which, index) in places.items():

                @pl.when(k == d)
                def _():
                    heads[part, :] = backs[which][index].astype(jnp.float32)

        else:
            heads[part, :] = backs[0][peer].astype(jnp.float32)
    both = heads[...].astype(cross.dtype)
    both_out[...] = both
    cross[...] = matmul(both, w_there[...], NN).astype(cross.dtype)


def add_rows(total, out, first, steps):
    for b in range(total.shape[0] // steps):
        out[first + b] = total[b * steps : (b + 1) * steps].astype(out.dtype)


def finish_first_kernel(base, recv, out):
    rows, steps = out.shape[:2]
    part = pl.ds(pl.multiple_of(pl.program_id(0) * rows * steps, rows * steps), rows * steps)
    add_rows(base[part, :] + recv[part, :].astype(jnp.float32), out, 0, steps)


def finish_second_kernel(pairs, base, recv, base_moved, recv_moved, earlier, out, after, rows_out, sems, row_sems, *, moved):
    later, steps = rows_out.shape[:2]
    half = out.shape[0] - later
    branch = base_moved[...] + recv_moved[...].astype(jnp.float32)
    for i in range(moved):
        after[i] = branch[i * steps : (i + 1) * steps].astype(after.dtype)

        @pl.when(pairs[i] < half)
        def _():
            pltpu.make_async_copy(after.at[i], out.at[pairs[i]], sems.at[i]).start()

    size = 16
    done = []
    for part in range(later // size):
        low = part * size
        rows = slice((half + low) * steps, (half + low + size) * steps)
        got = slice(low * steps, (low + size) * steps)
        add_rows(base[rows, :] + recv[got, :].astype(jnp.float32), rows_out, low, steps)
        for i in range(moved):
            r = pairs[i] - half

            @pl.when((r >= low) & (r < low + size))
            def _():
                rows_out[r] = after[i]

        piece = pl.ds(low, size)
        done.append(load([(rows_out.at[piece], out.at[pl.ds(half + low, size)])], row_sems.at[part]))
    for i in range(moved):

        @pl.when(pairs[i] < half)
        def _():
            pltpu.make_async_copy(after.at[i], out.at[pairs[i]], sems.at[i]).wait()

    for wait in done:
        wait()


def row_buffers(count, steps, width, dtype):
    return [pltpu.VMEM((count, steps, size), dtype) for size in (width, HEAD_DIM, HEAD_DIM)]


def exchange_pack(
    fork, partner, row_slot, queries, new_keys, new_values, fork_table, prompt_keys, prompt_values, span, moved
):
    replicas = lax.axis_size("replica")
    me = lax.axis_index("replica")
    local_rows, steps, width = queries.shape
    groups = width // HEAD_DIM
    held, prefix = prompt_keys.shape[:2]
    dtype = queries.dtype
    pairs_shape = jax.ShapeDtypeStruct((2 * (moved + 1) + replicas,), jnp.int32)
    if replicas <= 8:
        shifts = tuple(range(1, replicas))
        count = len(shifts)
        *packed, pairs = pl.pallas_call(
            functools.partial(pack_kernel, replicas=replicas, moved=moved, shifts=shifts),
            out_shape=[pltpu.VMEM((2 * prefix + span, HEAD_DIM), dtype)] * count + [pairs_shape],
            in_specs=[SMEM, SMEM] + [ANY] * 5,
            out_specs=[VMEM] * count + [SMEM],
            scratch_shapes=row_buffers(count, steps, width, dtype)
            + [
                pltpu.SMEM((replicas,), jnp.int32),
                pltpu.SemaphoreType.DMA((count, 2)),
                pltpu.SemaphoreType.DMA((count, 3)),
            ],
            compiler_params=params(),
            name="pack",
        )(*in_hbm(fork, partner, queries, new_keys, new_values, prompt_keys, prompt_values))
        return packed, pairs
    chosen = (fork_table // held) == me
    offsets = jnp.sum(jnp.where(chosen, fork_table % held, 0), axis=1)
    peer_of = partner // local_rows
    pairing = (peer_of[None, :] == jnp.arange(replicas, dtype=jnp.int32)[:, None]) & (
        peer_of[None, :] != me
    )
    row_of = jnp.sum(jnp.where(pairing, jnp.arange(local_rows, dtype=jnp.int32)[None, :], 0), axis=1)
    q = queries[row_of].reshape(replicas, steps, groups, HEAD_DIM).transpose(0, 2, 1, 3)
    q = q.reshape(replicas, groups * steps, HEAD_DIM)
    pad = jnp.zeros((replicas, span - (groups + 2) * steps, HEAD_DIM), dtype)
    block = jnp.concatenate(
        [prompt_keys[offsets], prompt_values[offsets], q, new_keys[row_of], new_values[row_of], pad], axis=1
    )
    pairs = pl.pallas_call(
        functools.partial(pairs_kernel, replicas=replicas, local_rows=local_rows, moved=moved),
        out_shape=pairs_shape,
        in_specs=[SMEM],
        out_specs=SMEM,
        scratch_shapes=[pltpu.SMEM((replicas,), jnp.int32)],
        name="pairs",
    )(partner)
    return [block], pairs


def body(
    residual,
    queries,
    new_keys,
    new_values,
    cache_keys,
    cache_values,
    cache_lengths,
    finished,
    partner,
    row_slot,
    fork_table,
    prompt_keys,
    prompt_values,
    prompt_lengths,
    out_proj,
):
    replicas = lax.axis_size("replica")
    tensors = lax.axis_size("tensor")
    local_rows, steps, width = queries.shape
    groups = width // HEAD_DIM
    suffix = cache_keys.shape[1]
    held, prefix = prompt_keys.shape[:2]
    slots = fork_table.shape[1]
    moved = replicas // 2
    stacked = replicas > 8
    model = residual.shape[2]
    n = local_rows * steps
    span = 32
    dtype = queries.dtype
    fork = fork_table.T
    sibling = [(i, i ^ 1) for i in range(tensors)]
    across = [(i, i ^ 2) for i in range(tensors)]

    packed, pairs = exchange_pack(
        fork, partner, row_slot, queries, new_keys, new_values, fork_table, prompt_keys, prompt_values, span, moved
    )
    w_sib = lax.ppermute(out_proj, "tensor", sibling)
    nk2 = new_keys.reshape(n, HEAD_DIM)
    nv2 = new_values.reshape(n, HEAD_DIM)
    ck2 = cache_keys.reshape(local_rows * suffix, HEAD_DIM)
    cv2 = cache_values.reshape(local_rows * suffix, HEAD_DIM)
    lookup = (row_slot, prompt_lengths, cache_lengths, finished)

    dma = lambda *shape: pltpu.SemaphoreType.DMA(shape)
    blocks = local_rows // BLOCK
    nb = BLOCK * steps
    assert nb == HEAD_DIM
    if stacked:
        received = [lax.all_to_all(packed[0], "replica", split_axis=0, concat_axis=0, tiled=True)]
    else:
        received = [
            lax.ppermute(block, "replica", [(i, (i + k) % replicas) for i in range(replicas)])
            for k, block in enumerate(packed, 1)
        ]

    m = moved * steps
    half = FIRST
    nh = half * nb
    prompts = pltpu.VMEM((slots * prefix, HEAD_DIM), dtype)

    def work(count):
        rows = count * BLOCK
        return [
            pltpu.VMEM((rows, steps, width), dtype),
            pltpu.VMEM((rows * steps, HEAD_DIM), dtype),
            pltpu.VMEM((rows * steps, HEAD_DIM), dtype),
            pltpu.VMEM((rows * suffix, HEAD_DIM), dtype),
            pltpu.VMEM((rows * suffix, HEAD_DIM), dtype),
            pltpu.VMEM((rows * steps, width), dtype),
            pltpu.VMEM((count, 4, nb, HEAD_DIM), jnp.int32),
            pltpu.VMEM((count, groups, nb, HEAD_DIM), jnp.float32),
            pltpu.VMEM((count, groups * nb, slots * prefix + HEAD_DIM), jnp.bfloat16),
            pltpu.VMEM((count, groups, nb, 2 * HEAD_DIM), jnp.bfloat16),
            pltpu.VMEM((count, groups * nb, HEAD_DIM), jnp.float32),
            dma(3, 2),
        ]

    sizes = dict(slots=slots, steps=steps, suffix=suffix)
    by_replica = [x.reshape(replicas, local_rows) for x in (row_slot, cache_lengths, finished)]
    lookup = in_hbm(prompt_lengths, *by_replica)
    rows_in = in_hbm(queries, nk2, nv2, ck2, cv2)
    h_first, pk, pv, w_there = pl.pallas_call(
        functools.partial(first_kernel, stacked=stacked, replicas=replicas, moved=moved, span=span, **sizes),
        out_shape=[pltpu.VMEM((nh + m, width), dtype), prompts, prompts, pltpu.VMEM((2 * width, model), dtype)],
        in_specs=[SMEM] * 3 + [VMEM] * 3 + [ANY] * (9 + len(received)),
        out_specs=[VMEM] * 4,
        scratch_shapes=[
            pltpu.VMEM((moved * span, HEAD_DIM), dtype),
            pltpu.VMEM((moved * suffix, HEAD_DIM), dtype),
            pltpu.VMEM((moved * suffix, HEAD_DIM), dtype),
            pltpu.VMEM((4, moved * span, HEAD_DIM), jnp.int32),
        ]
        + work(half)
        + [dma(slots, 2), dma(2), dma(moved), dma(2 * moved)],
        compiler_params=params(),
        cost_estimate=SMALL,
        name="attend_first",
    )(*in_hbm(fork, pairs), *lookup, *rows_in, *in_hbm(prompt_keys, prompt_values, out_proj), w_sib, *received)

    def call(kernel, name, shapes, specs, operands, extra=()):
        return pl.pallas_call(
            kernel,
            out_shape=[pltpu.VMEM(shape, kind) for shape, kind in shapes],
            in_specs=specs,
            out_specs=[VMEM] * len(shapes),
            scratch_shapes=list(extra),
            compiler_params=params(),
            cost_estimate=SMALL,
            name=name,
        )(*operands)

    def cross(heads, rows):
        sib = lax.ppermute(heads, "tensor", sibling)
        (crossed,) = call(project_kernel, "project", [((rows, model), dtype)], [VMEM] * 3, (heads, sib, w_there))
        return sib, crossed, lax.ppermute(crossed, "tensor", across)

    s_first, c_first, got_first = cross(h_first, nh)
    options = dict(moved=moved, steps=steps, split=not stacked)
    shape = ((replicas if stacked else 4, steps, 2 * width), dtype)
    back = call(
        functools.partial(moved_send_kernel, **options),
        "moved_send",
        [shape] * (1 if stacked else 2),
        [SMEM, VMEM, VMEM, ANY],
        (*in_hbm(pairs), h_first, s_first, c_first),
    )
    (h_second,) = call(
        functools.partial(second_kernel, first_row=half * BLOCK, **sizes),
        "attend_second",
        [((n - nh, width), dtype)],
        [SMEM] * 2 + [VMEM] * 5 + [ANY] * 6,
        (*in_hbm(fork), *lookup, pk, pv, *rows_in, c_first),
        work(blocks - half),
    )
    s_second, c_second, got_second = cross(h_second, n - nh)
    if stacked:
        backs = [lax.all_to_all(back[0], "replica", split_axis=0, concat_axis=0, tiled=True)]
    else:
        flip = lambda x, bit: lax.ppermute(x, "replica", [(i, i ^ bit) for i in range(replicas)])
        kept = back[0]
        one = flip(back[1], 1)
        one, *_ = lax.optimization_barrier((one, c_second))
        two = flip(jnp.concatenate([kept[2:], one[2:]]), 2)
        two, *_ = lax.optimization_barrier((two, got_first))
        four = flip(jnp.concatenate([kept[1:2], one[1:2], two[1:2], two[3:4]]), 4)
        backs = [one, two, four]
    crossed_moved, home_heads = call(
        functools.partial(moved_project_kernel, **options),
        "moved_project",
        [((m, model), dtype), ((m, 2 * width), dtype)],
        [SMEM] + [VMEM] * (1 + len(backs)),
        (*in_hbm(pairs), w_there, *backs),
        [pltpu.VMEM((m, 2 * width), jnp.float32)],
    )
    got_moved = lax.ppermute(crossed_moved, "tensor", across)
    base, base_moved = call(
        base_kernel,
        "base",
        [((n, model), jnp.float32), ((m, model), jnp.float32)],
        [SMEM] + [VMEM] * 5 + [ANY] * 3,
        (*in_hbm(pairs), h_first, s_first, h_second, s_second, home_heads, *in_hbm(out_proj), w_sib, *in_hbm(residual)),
        [pltpu.VMEM((2 * width, model), dtype), pltpu.VMEM(residual.shape, dtype), dma(3)],
    )

    whole = jax.ShapeDtypeStruct(residual.shape, residual.dtype)
    out = pl.pallas_call(
        finish_first_kernel,
        grid=(half,),
        in_specs=[VMEM, VMEM],
        out_specs=pl.BlockSpec((BLOCK, steps, model), lambda i: (i, 0, 0)),
        out_shape=whole,
        compiler_params=params(),
        name="finish_first",
    )(base, got_first)
    return pl.pallas_call(
        functools.partial(finish_second_kernel, moved=moved),
        in_specs=[SMEM, VMEM, VMEM, VMEM, VMEM, ANY],
        out_specs=ANY,
        out_shape=whole,
        input_output_aliases={5: 0},
        scratch_shapes=[
            pltpu.VMEM((moved, steps, model), dtype),
            pltpu.VMEM(((blocks - half) * BLOCK, steps, model), dtype),
            dma(moved),
            dma((blocks - half) * BLOCK // 16, 1),
        ],
        compiler_params=params(),
        name="finish_second",
    )(*in_hbm(pairs), base, got_second, base_moved, got_moved, out)


def solution(mesh):
    rows = P("replica", None, "tensor")
    in_specs = (rows,) * 6 + (P(), P(), P("replica"), P(), P(), rows, rows, P(), P("tensor", None))
    return jax.shard_map(body, mesh=mesh, in_specs=in_specs, out_specs=rows, check_vma=False)
```

```python
import functools
import math

import jax
import jax.numpy as jnp
from jax import lax
from jax.experimental import pallas as pl
from jax.experimental.pallas import tpu as pltpu
from jax.sharding import PartitionSpec as P

HEAD_DIM = 128
LOWEST = -1e30
EXP2_SCALE = math.log2(math.e) / math.sqrt(HEAD_DIM)
VMEM_BYTES = 24 * 1024 * 1024
SMALL = pl.CostEstimate(flops=1, bytes_accessed=1, transcendentals=0)
BLOCK = 32
FIRST = 2
NT = (((1,), (1,)), ((), ()))
NN = (((1,), (0,)), ((), ()))

ANY = pl.BlockSpec(memory_space=pl.ANY)
SMEM = pl.BlockSpec(memory_space=pltpu.SMEM)
VMEM = pl.BlockSpec(memory_space=pltpu.VMEM)


def params(side_effects=False):
    return pltpu.CompilerParams(vmem_limit_bytes=VMEM_BYTES, has_side_effects=side_effects)


def matmul(a, b, dims):
    return lax.dot_general(a, b, dims, preferred_element_type=jnp.float32)


def columns(model, flip):
    place = jnp.bitwise_xor(lax.axis_index("tensor"), flip)
    return pl.ds(pl.multiple_of(place * model, HEAD_DIM), model)


def in_hbm(*arrays):
    return [pltpu.with_memory_space_constraint(x, pltpu.HBM) for x in arrays]


def iota(shape, dim):
    return lax.broadcasted_iota(jnp.int32, shape, dim)


def load(pairs, sem):
    copies = [pltpu.make_async_copy(a, b, sem.at[i]) for i, (a, b) in enumerate(pairs)]
    for copy in copies:
        copy.start()

    def wait():
        for copy in copies:
            copy.wait()

    return wait


def quotient(a, b):
    return a >> (b.bit_length() - 1) if b & (b - 1) == 0 else lax.div(a, b)


def remainder(a, b):
    return a & (b - 1) if b & (b - 1) == 0 else lax.rem(a, b)


def list_pairs(row_of, pairs, me, replicas, moved):
    count = jnp.int32(0)
    for j in range(replicas):
        pairs[count] = row_of[j]
        pairs[moved + 1 + count] = j
        pairs[2 * (moved + 1) + j] = jnp.maximum(row_of[j], 0)
        count = jnp.minimum(count + jnp.where((row_of[j] >= 0) & (j != me), 1, 0), moved)


def find_pairs(partner, row_of, replicas, local_rows):
    for j in range(replicas):
        row_of[j] = -1

    def note(r, carry):
        row_of[quotient(partner[r], local_rows)] = r
        return carry

    lax.fori_loop(0, local_rows, note, 0, unroll=8)


def send_prompts(shifts, fork, keys, values, outs, sems, replicas):
    me = lax.axis_index("replica")
    held, prefix = keys.shape[0], keys.shape[1]
    waits = []
    for i, k in enumerate(shifts):
        peer = remainder(me + k, replicas)
        offset = jnp.int32(0)
        for s in range(fork.shape[0]):
            prompt = fork[s, peer]
            offset = jnp.where(quotient(prompt, held) == me, remainder(prompt, held), offset)
        copies = [
            (source.at[offset], outs[i].at[pl.ds(n * prefix, prefix)]) for n, source in enumerate((keys, values))
        ]
        waits.append(load(copies, sems.at[i]))
    return waits


def send_rows(shifts, row_of, hbm, vmem, outs, sems, replicas, prefix):
    me = lax.axis_index("replica")
    width = hbm[0].shape[2]
    waits = []
    for i, k in enumerate(shifts):
        r = row_of(remainder(me + k, replicas))
        waits.append(load([(a.at[r], b.at[i]) for a, b in zip(hbm, vmem)], sems.at[i]))
    for i in range(len(shifts)):
        waits[i]()
        q, nk, nv = [v[i].astype(jnp.float32) for v in vmem]
        parts = [q[:, low : low + HEAD_DIM] for low in range(0, width, HEAD_DIM)] + [nk, nv]
        pad = outs[i].shape[0] - 2 * prefix - sum(p.shape[0] for p in parts)
        parts += [jnp.zeros((pad, HEAD_DIM), jnp.float32)]
        outs[i][2 * prefix :, :] = jnp.concatenate(parts, axis=0).astype(outs[i].dtype)


def pairs_kernel(partner, pairs, row_of, *, replicas, local_rows, moved):
    find_pairs(partner, row_of, replicas, local_rows)
    list_pairs(row_of, pairs, lax.axis_index("replica"), replicas, moved)


def pack_kernel(
    fork, partner, queries, new_keys, new_values, keys, values, *rest, replicas, moved, shifts
):
    outs, (pairs, qv, nkv, nvv, row_of, sems, row_sems) = rest[: len(shifts)], rest[len(shifts) :]
    waits = send_prompts(shifts, fork, keys, values, outs, sems, replicas)
    find_pairs(partner, row_of, replicas, queries.shape[0])
    list_pairs(row_of, pairs, lax.axis_index("replica"), replicas, moved)
    send_rows(
        shifts, lambda j: jnp.maximum(row_of[j], 0), (queries, new_keys, new_values), (qv, nkv, nvv), outs, row_sems,
        replicas, keys.shape[1],
    )
    for wait in waits:
        wait()


def softmax_weights(prompt, new, cache, prompt_mask, new_mask, cache_mask):
    prompt = jnp.where(prompt_mask, prompt, LOWEST)
    new = jnp.where(new_mask, new, LOWEST)
    cache = jnp.where(cache_mask, cache, LOWEST)
    top = jnp.max(jnp.maximum(jnp.maximum(prompt, new), cache), axis=1, keepdims=True)
    prompt = jnp.exp2((prompt - top) * EXP2_SCALE)
    new = jnp.exp2((new - top) * EXP2_SCALE)
    cache = jnp.exp2((cache - top) * EXP2_SCALE)
    inverse = 1.0 / jnp.sum(prompt + new + cache, axis=1, keepdims=True)
    return prompt * inverse, new * inverse, cache * inverse


def pick_slot(scores, slot, slots, prefix):
    picked = scores[:, :prefix]
    for s in range(1, slots):
        picked = jnp.where(slot == s, scores[:, s * prefix : (s + 1) * prefix], picked)
    return picked


def ones_where(mask):
    return mask.astype(jnp.float32).astype(jnp.bfloat16)


def spread_slot(weights, masks):
    return jnp.concatenate([weights * mask for mask in masks], axis=1)


def row_values(slots_of, lengths, finished, fork, prompt_lengths, slots):
    me = lax.axis_index("replica")
    shape = (HEAD_DIM, slots_of.shape[1])
    slot, length, done = [jnp.broadcast_to(v[pl.ds(me, 1), :], shape) for v in (slots_of, lengths, finished)]
    prompt = jnp.zeros(shape, jnp.int32)
    for s in range(slots):
        prompt = jnp.where(slot == s, prompt_lengths[fork[s, me]], prompt)
    return [v.astype(jnp.float32).astype(jnp.bfloat16) for v in (slot, prompt, length, 1 - done)]


def fill_meta(values, row_of, meta):
    take = (row_of == iota(row_of.shape, 1)).astype(jnp.float32).astype(jnp.bfloat16)
    for i, value in enumerate(values):
        meta[i] = matmul(take, value, NT).astype(jnp.int32)


def attend_scores(q, ck, cache_scores, *, steps, suffix):
    n = q.shape[0]
    groups = q.shape[1] // HEAD_DIM
    keys_sub = 4 * suffix
    half = 2 * suffix
    for sub in range(n // 16):
        r0 = sub * 16
        qs = jnp.concatenate(
            [q[r0 : r0 + 16, h * HEAD_DIM : (h + 1) * HEAD_DIM] for h in range(groups)], axis=0
        )
        s = matmul(qs, ck[sub * keys_sub : (sub + 1) * keys_sub, :], NT)
        for h in range(groups):
            cache_scores[h, r0 : r0 + 8, :] = s[16 * h : 16 * h + 8, :half]
            cache_scores[h, r0 + 8 : r0 + 16, :] = s[16 * h + 8 : 16 * h + 16, half:]


def attend_block(
    q, nk, nv, cv, pk, pv, heads, meta, cache_scores, weights, cache_weights, mixed, wait,
    *, steps, slots, suffix
):
    n = q.shape[0]
    groups = q.shape[1] // HEAD_DIM
    prefix = pk.shape[0] // slots
    keys_sub = 4 * suffix
    half = 2 * suffix
    shape = (n, HEAD_DIM)
    lane, row = iota(shape, 1), iota(shape, 0)
    cache_own = (lane // suffix) == ((row % 8) // steps)
    cache_lane = jnp.where(cache_own, lane % suffix, suffix)
    new_mask = ((lane // steps) == (row // steps)) & ((lane % steps) <= (row % steps))
    first_half = (row % 16) < 8
    slot = meta[0]
    prompt_mask = lane < meta[1]
    cache_mask = cache_lane < meta[2]
    alive_rows = meta[3].astype(jnp.float32)
    masks = [ones_where(slot == s) for s in range(slots)]
    halves = [ones_where(first_half), ones_where(jnp.logical_not(first_half))]
    q_all = jnp.concatenate([q[:, h * HEAD_DIM : (h + 1) * HEAD_DIM] for h in range(groups)], axis=0)
    prompt_all = matmul(q_all, pk[...], NT)
    new_all = matmul(q_all, nk[...], NT)
    for h in range(groups):
        part = slice(h * n, (h + 1) * n)
        prompt = pick_slot(prompt_all[part], slot, slots, prefix)
        wp, wn, wc = softmax_weights(
            prompt, new_all[part], cache_scores[h], prompt_mask, new_mask, cache_mask
        )
        wc = wc.astype(jnp.bfloat16)
        cache_weights[h, :, :half] = wc * halves[0]
        cache_weights[h, :, half:] = wc * halves[1]
        weights[part, : slots * prefix] = spread_slot(wp.astype(jnp.bfloat16), masks)
        weights[part, slots * prefix :] = wn.astype(jnp.bfloat16)
    mixed[...] = matmul(weights[:, : slots * prefix], pv[...], NN) + matmul(
        weights[:, slots * prefix :], nv[...], NN
    )
    if wait is not None:
        wait()
    for sub in range(n // 16):
        r0 = sub * 16
        w = jnp.concatenate([cache_weights[h, r0 : r0 + 16, :] for h in range(groups)], axis=0)
        o = matmul(w, cv[sub * keys_sub : (sub + 1) * keys_sub, :], NN)
        for h in range(groups):
            total = mixed[h * n + r0 : h * n + r0 + 16, :] + o[16 * h : 16 * h + 16, :]
            heads[r0 : r0 + 16, h * HEAD_DIM : (h + 1) * HEAD_DIM] = (
                total * alive_rows[r0 : r0 + 16, :]
            ).astype(heads.dtype)


def moved_block(x, pk, pv, keys, values, slot, plen, clen, alive, *, steps, slots, groups, span, suffix):
    prefix = pk.shape[0] // slots
    shape = (4 * span, HEAD_DIM)
    lane, row = iota(shape, 1), iota(shape, 0)
    prompt_mask = lane < plen
    cache_mask = ((lane // suffix) == ((row // span) % 2)) & ((lane % suffix) < clen)
    past = (lane % span) - groups * steps
    new_mask = ((lane // span) == (row // span)) & (past >= 0) & (past <= row % steps)
    prompt = pick_slot(matmul(x, pk[...], NT), slot, slots, prefix)
    new = matmul(x, x, NT)
    cache = matmul(x, keys[...], NT)
    half = 2 * suffix
    top_half = row < 2 * span
    cache = jnp.where(top_half, cache[:, :half], cache[:, half:])
    wp, wn, wc = softmax_weights(prompt, new, cache, prompt_mask, new_mask, cache_mask)
    wc = jnp.concatenate(
        [jnp.where(top_half, wc, 0.0), jnp.where(top_half, 0.0, wc)], axis=1
    ).astype(jnp.bfloat16)
    wn = pltpu.roll(wn, steps, 1).astype(jnp.bfloat16)
    mixed = (
        matmul(spread_slot(wp.astype(jnp.bfloat16), [ones_where(slot == s) for s in range(slots)]), pv[...], NN)
        + matmul(wn, x, NN)
        + matmul(wc, values[...], NN)
    )
    mixed = (mixed * alive).astype(jnp.bfloat16)
    row, col = iota((4 * steps, 4 * span), 0), iota((4 * steps, 4 * span), 1)
    cols = []
    for h in range(groups):
        take = ((row // steps) == (col // span)) & ((col % span) == h * steps + row % steps)
        cols.append(matmul(take.astype(jnp.bfloat16), mixed, NN).astype(jnp.bfloat16))
    return jnp.concatenate(cols, axis=1)


def start_rows(first_row, hbm, vmem, sems, steps, suffix):
    rows = vmem[0].shape[0]
    part = pl.ds(first_row * steps, rows * steps)
    keys = pl.ds(first_row * suffix, rows * suffix)
    q, nk, nv, ck, cv = hbm
    first = load([(q.at[pl.ds(first_row, rows)], vmem[0]), (ck.at[keys], vmem[3])], sems.at[0])

    def rest():
        return [
            load([(nk.at[part], vmem[1]), (nv.at[part], vmem[2])], sems.at[1]),
            load([(cv.at[keys], vmem[4])], sems.at[2]),
        ]

    return first, rest


def attend_rows(lookup, first_row, waits, vmem, pk, pv, heads, work, *, steps, slots, suffix):
    q3, nk, nv, ck, cv = vmem
    q, meta, cache_scores, weights, cache_weights, mixed = work
    count, _, n, _ = meta.shape
    rows = n // steps
    per = 16 // steps
    shape = (n, lookup[0].shape[1])
    for i in range(count):
        fill_meta(lookup, first_row + i * rows + iota(shape, 0) // steps, meta.at[i])
    waits[0]()
    for b in range(0, count * rows, per):
        part = [q3[b + i].astype(jnp.float32) for i in range(per)]
        q[b * steps : (b + per) * steps, :] = jnp.concatenate(part, axis=0).astype(q.dtype)
    keys = rows * suffix
    for i in range(count):
        attend_scores(
            q.at[pl.ds(i * n, n)], ck.at[pl.ds(i * keys, keys)], cache_scores.at[i], steps=steps, suffix=suffix
        )
    waits[1]()
    for i in range(count):
        part = pl.ds(i * n, n)
        attend_block(
            q.at[part], nk.at[part], nv.at[part], cv.at[pl.ds(i * keys, keys)], pk, pv, heads.at[part],
            meta.at[i], cache_scores.at[i], weights.at[i], cache_weights.at[i], mixed.at[i],
            waits[2] if i == 0 else None, steps=steps, slots=slots, suffix=suffix,
        )


def first_kernel(
    fork, pairs, prompt_lengths, row_slot, cache_lengths, finished, q, nk, nv, ck, cv, own_keys, own_values, w_own, w_sib,
    *rest, stacked, replicas, slots, moved, steps, suffix, span
):
    recvs, rest = rest[:-24], rest[-24:]
    heads, pk, pv, w_there, x, keys, values, moved_meta = rest[:8]
    vmem, work, (row_sems, slot_sems, w_sems, sems, cache_sems) = rest[8:13], rest[13:19], rest[19:]
    me = lax.axis_index("replica")
    held, prefix = own_keys.shape[0], own_keys.shape[1]
    scores_ready, start_rest = start_rows(0, (q, nk, nv, ck, cv), vmem, row_sems, steps, suffix)
    for s in range(slots):
        prompt = fork[s, me]
        owner = quotient(prompt, held)
        offset = remainder(prompt, held)
        targets = (pk.at[pl.ds(s * prefix, prefix)], pv.at[pl.ds(s * prefix, prefix)])
        if stacked:
            for i in range(2):
                pltpu.make_async_copy(
                    recvs[0].at[owner, pl.ds(i * prefix, prefix)], targets[i], slot_sems.at[s, i]
                ).start()
            continue
        k = remainder(me - owner + replicas, replicas)

        @pl.when(k == 0)
        def _():
            pltpu.make_async_copy(own_keys.at[offset], targets[0], slot_sems.at[s, 0]).start()
            pltpu.make_async_copy(own_values.at[offset], targets[1], slot_sems.at[s, 1]).start()

        for kk in range(1, replicas):

            @pl.when(k == kk)
            def _():
                for i in range(2):
                    pltpu.make_async_copy(
                        recvs[kk - 1].at[pl.ds(i * prefix, prefix)], targets[i], slot_sems.at[s, i]
                    ).start()

    waits = [scores_ready, *start_rest()]
    groups = q.shape[2] // HEAD_DIM
    for i in range(moved):
        peer = pairs[moved + 1 + i]
        if stacked:
            pltpu.make_async_copy(
                recvs[0].at[peer, pl.ds(2 * prefix, span)], x.at[pl.ds(i * span, span)], sems.at[i]
            ).start()
        else:
            k = remainder(me - peer + replicas, replicas)
            for kk in range(1, replicas):

                @pl.when(k == kk)
                def _():
                    pltpu.make_async_copy(
                        recvs[kk - 1].at[pl.ds(2 * prefix, span)], x.at[pl.ds(i * span, span)], sems.at[i]
                    ).start()

    copies = []
    for i in range(moved):
        source = pl.ds(pl.multiple_of(pairs[i] * suffix, suffix), suffix)
        target = pl.ds(i * suffix, suffix)
        copies += [(ck.at[source], keys.at[target]), (cv.at[source], values.at[target])]
    caches_ready = load(copies, cache_sems)
    width, model = w_own.shape[0], w_there.shape[1]
    at = columns(model, 2)
    weights_ready = load(
        [(w_own.at[:, at], w_there.at[pl.ds(0, width)]), (w_sib.at[:, at], w_there.at[pl.ds(width, width)])], w_sems
    )

    def wait_second():
        waits[1]()
        for s in range(slots):
            for i, target in enumerate((pk, pv)):
                pltpu.make_async_copy(own_keys.at[0], target.at[pl.ds(s * prefix, prefix)], slot_sems.at[s, i]).wait()

    lookup = row_values(row_slot, cache_lengths, finished, fork, prompt_lengths, slots)
    shape = (moved * span, row_slot.shape[1])
    item = iota(shape, 0) // span
    row_of = jnp.zeros(shape, jnp.int32)
    for i in range(moved):
        row_of = jnp.where(item == i, pairs[i], row_of)
    fill_meta(lookup, row_of, moved_meta)
    n = heads.shape[0] - moved * steps
    attend_rows(
        lookup, 0, (waits[0], wait_second, waits[2]), vmem, pk, pv, heads.at[pl.ds(0, n)], work,
        steps=steps, slots=slots, suffix=suffix,
    )
    for i in range(moved):
        source = recvs[0].at[0, pl.ds(0, span)] if stacked else recvs[0].at[pl.ds(0, span)]
        pltpu.make_async_copy(source, x.at[pl.ds(i * span, span)], sems.at[i]).wait()
    caches_ready()
    for g in range(moved // 4):
        part = slice(g * 4 * span, (g + 1) * 4 * span)
        kpart = slice(g * 4 * suffix, (g + 1) * 4 * suffix)
        heads[n + g * 4 * steps : n + (g + 1) * 4 * steps, :] = moved_block(
            x[part, :], pk, pv, keys.at[kpart], values.at[kpart],
            moved_meta[0, part, :], moved_meta[1, part, :], moved_meta[2, part, :],
            moved_meta[3, part, :].astype(jnp.float32),
            steps=steps, slots=slots, groups=groups, span=span, suffix=suffix,
        )
    weights_ready()


def second_kernel(
    fork, prompt_lengths, row_slot, cache_lengths, finished, pk, pv, q, nk, nv, ck, cv, after, *rest,
    first_row, slots, steps, suffix
):
    heads, vmem, work, row_sems = rest[0], rest[1:6], rest[6:12], rest[12]
    scores_ready, start_rest = start_rows(first_row, (q, nk, nv, ck, cv), vmem, row_sems, steps, suffix)
    waits = [scores_ready, *start_rest()]
    lookup = row_values(row_slot, cache_lengths, finished, fork, prompt_lengths, slots)
    attend_rows(
        lookup, first_row, waits, vmem, pk, pv, heads, work, steps=steps, slots=slots, suffix=suffix
    )


def project_kernel(h_own, h_sib, weights, out):
    rows = pl.ds(0, out.shape[0])
    both = jnp.concatenate([h_own[rows, :], h_sib[rows, :]], axis=1)
    out[...] = matmul(both, weights[...], NN).astype(out.dtype)


def base_kernel(
    pairs, h_first, s_first, h_second, s_second, h_moved, w_own, w_sib, residual, out, moved_out, weights, before, sems
):
    rows, model = out.shape
    width = w_own.shape[0]
    steps = residual.shape[1]
    at = columns(model, 0)
    ready = load(
        [
            (w_own.at[:, at], weights.at[pl.ds(0, width)]),
            (w_sib.at[:, at], weights.at[pl.ds(width, width)]),
            (residual, before),
        ],
        sems,
    )
    ready()
    moved_total = matmul(h_moved[...], weights[...], NN)
    for i in range(h_moved.shape[0] // steps):
        part = slice(i * steps, (i + 1) * steps)
        moved_out[part, :] = moved_total[part] + before[pairs[i]].astype(jnp.float32)
    low = 0
    for h_own, h_sib, size in ((h_first, s_first, rows - h_second.shape[0]), (h_second, s_second, h_second.shape[0])):
        part = pl.ds(0, size)
        total = matmul(jnp.concatenate([h_own[part, :], h_sib[part, :]], axis=1), weights[...], NN)
        for b in range(0, size, steps):
            out[low : low + steps, :] = total[b : b + steps] + before[low // steps].astype(jnp.float32)
            low += steps


def moved_send_kernel(pairs, h_own, h_sib, after, *outs, moved, steps, split):
    me = lax.axis_index("replica")
    rows = pl.ds(h_own.shape[0] - moved * steps, moved * steps)
    both = jnp.concatenate([h_own[rows, :], h_sib[rows, :]], axis=1).astype(jnp.float32)
    for i in range(moved):
        peer = pairs[moved + 1 + i]
        value = both[i * steps : (i + 1) * steps].astype(outs[0].dtype)
        if split:
            k = jnp.bitwise_xor(me, peer)
            place = 2 * remainder(quotient(k, 2), 2) + quotient(k, 4)

            @pl.when(remainder(k, 2) == 0)
            def _():
                outs[0][place] = value

            @pl.when(remainder(k, 2) == 1)
            def _():
                outs[1][place] = value

        else:
            outs[0][peer] = value


def moved_project_kernel(pairs, w_there, *rest, moved, steps, split):
    backs, (cross, both_out, heads) = rest[:-3], rest[-3:]
    me = lax.axis_index("replica")
    for i in range(moved):
        peer = pairs[moved + 1 + i]
        part = slice(i * steps, (i + 1) * steps)
        if split:
            k = jnp.bitwise_xor(me, peer)
            places = {1: (0, 0), 2: (1, 0), 3: (1, 2), 4: (2, 0), 5: (2, 1), 6: (2, 2), 7: (2, 3)}
            for d, (which, index) in places.items():

                @pl.when(k == d)
                def _():
                    heads[part, :] = backs[which][index].astype(jnp.float32)

        else:
            heads[part, :] = backs[0][peer].astype(jnp.float32)
    both = heads[...].astype(cross.dtype)
    both_out[...] = both
    cross[...] = matmul(both, w_there[...], NN).astype(cross.dtype)


def add_rows(total, out, first, steps):
    for b in range(total.shape[0] // steps):
        out[first + b] = total[b * steps : (b + 1) * steps].astype(out.dtype)


def finish_first_kernel(base, recv, out):
    rows, steps = out.shape[:2]
    part = pl.ds(pl.multiple_of(pl.program_id(0) * rows * steps, rows * steps), rows * steps)
    add_rows(base[part, :] + recv[part, :].astype(jnp.float32), out, 0, steps)


def finish_second_kernel(pairs, base, recv, base_moved, recv_moved, earlier, out, after, rows_out, sems, row_sems, *, moved):
    later, steps = rows_out.shape[:2]
    half = out.shape[0] - later
    branch = base_moved[...] + recv_moved[...].astype(jnp.float32)
    for i in range(moved):
        after[i] = branch[i * steps : (i + 1) * steps].astype(after.dtype)

        @pl.when(pairs[i] < half)
        def _():
            pltpu.make_async_copy(after.at[i], out.at[pairs[i]], sems.at[i]).start()

    size = 16
    done = []
    for part in range(later // size):
        low = part * size
        rows = slice((half + low) * steps, (half + low + size) * steps)
        got = slice(low * steps, (low + size) * steps)
        add_rows(base[rows, :] + recv[got, :].astype(jnp.float32), rows_out, low, steps)
        for i in range(moved):
            r = pairs[i] - half

            @pl.when((r >= low) & (r < low + size))
            def _():
                rows_out[r] = after[i]

        piece = pl.ds(low, size)
        done.append(load([(rows_out.at[piece], out.at[pl.ds(half + low, size)])], row_sems.at[part]))
    for i in range(moved):

        @pl.when(pairs[i] < half)
        def _():
            pltpu.make_async_copy(after.at[i], out.at[pairs[i]], sems.at[i]).wait()

    for wait in done:
        wait()


def row_buffers(count, steps, width, dtype):
    return [pltpu.VMEM((count, steps, size), dtype) for size in (width, HEAD_DIM, HEAD_DIM)]


def exchange_pack(
    fork, partner, row_slot, queries, new_keys, new_values, fork_table, prompt_keys, prompt_values, span, moved
):
    replicas = lax.axis_size("replica")
    me = lax.axis_index("replica")
    local_rows, steps, width = queries.shape
    groups = width // HEAD_DIM
    held, prefix = prompt_keys.shape[:2]
    dtype = queries.dtype
    pairs_shape = jax.ShapeDtypeStruct((2 * (moved + 1) + replicas,), jnp.int32)
    if replicas <= 8:
        shifts = tuple(range(1, replicas))
        count = len(shifts)
        *packed, pairs = pl.pallas_call(
            functools.partial(pack_kernel, replicas=replicas, moved=moved, shifts=shifts),
            out_shape=[pltpu.VMEM((2 * prefix + span, HEAD_DIM), dtype)] * count + [pairs_shape],
            in_specs=[SMEM, SMEM] + [ANY] * 5,
            out_specs=[VMEM] * count + [SMEM],
            scratch_shapes=row_buffers(count, steps, width, dtype)
            + [
                pltpu.SMEM((replicas,), jnp.int32),
                pltpu.SemaphoreType.DMA((count, 2)),
                pltpu.SemaphoreType.DMA((count, 3)),
            ],
            compiler_params=params(),
            name="pack",
        )(*in_hbm(fork, partner, queries, new_keys, new_values, prompt_keys, prompt_values))
        return packed, pairs
    chosen = (fork_table // held) == me
    offsets = jnp.sum(jnp.where(chosen, fork_table % held, 0), axis=1)
    peer_of = partner // local_rows
    pairing = (peer_of[None, :] == jnp.arange(replicas, dtype=jnp.int32)[:, None]) & (
        peer_of[None, :] != me
    )
    row_of = jnp.sum(jnp.where(pairing, jnp.arange(local_rows, dtype=jnp.int32)[None, :], 0), axis=1)
    q = queries[row_of].reshape(replicas, steps, groups, HEAD_DIM).transpose(0, 2, 1, 3)
    q = q.reshape(replicas, groups * steps, HEAD_DIM)
    pad = jnp.zeros((replicas, span - (groups + 2) * steps, HEAD_DIM), dtype)
    block = jnp.concatenate(
        [prompt_keys[offsets], prompt_values[offsets], q, new_keys[row_of], new_values[row_of], pad], axis=1
    )
    pairs = pl.pallas_call(
        functools.partial(pairs_kernel, replicas=replicas, local_rows=local_rows, moved=moved),
        out_shape=pairs_shape,
        in_specs=[SMEM],
        out_specs=SMEM,
        scratch_shapes=[pltpu.SMEM((replicas,), jnp.int32)],
        name="pairs",
    )(partner)
    return [block], pairs


def body(
    residual,
    queries,
    new_keys,
    new_values,
    cache_keys,
    cache_values,
    cache_lengths,
    finished,
    partner,
    row_slot,
    fork_table,
    prompt_keys,
    prompt_values,
    prompt_lengths,
    out_proj,
):
    replicas = lax.axis_size("replica")
    tensors = lax.axis_size("tensor")
    local_rows, steps, width = queries.shape
    groups = width // HEAD_DIM
    suffix = cache_keys.shape[1]
    held, prefix = prompt_keys.shape[:2]
    slots = fork_table.shape[1]
    moved = replicas // 2
    stacked = replicas > 8
    model = residual.shape[2]
    n = local_rows * steps
    span = 32
    dtype = queries.dtype
    fork = fork_table.T
    sibling = [(i, i ^ 1) for i in range(tensors)]
    across = [(i, i ^ 2) for i in range(tensors)]

    packed, pairs = exchange_pack(
        fork, partner, row_slot, queries, new_keys, new_values, fork_table, prompt_keys, prompt_values, span, moved
    )
    w_sib = lax.ppermute(out_proj, "tensor", sibling)
    nk2 = new_keys.reshape(n, HEAD_DIM)
    nv2 = new_values.reshape(n, HEAD_DIM)
    ck2 = cache_keys.reshape(local_rows * suffix, HEAD_DIM)
    cv2 = cache_values.reshape(local_rows * suffix, HEAD_DIM)
    lookup = (row_slot, prompt_lengths, cache_lengths, finished)

    dma = lambda *shape: pltpu.SemaphoreType.DMA(shape)
    blocks = local_rows // BLOCK
    nb = BLOCK * steps
    assert nb == HEAD_DIM
    if stacked:
        received = [lax.all_to_all(packed[0], "replica", split_axis=0, concat_axis=0, tiled=True)]
    else:
        received = [
            lax.ppermute(block, "replica", [(i, (i + k) % replicas) for i in range(replicas)])
            for k, block in enumerate(packed, 1)
        ]

    m = moved * steps
    half = FIRST
    nh = half * nb
    prompts = pltpu.VMEM((slots * prefix, HEAD_DIM), dtype)

    def work(count):
        rows = count * BLOCK
        return [
            pltpu.VMEM((rows, steps, width), dtype),
            pltpu.VMEM((rows * steps, HEAD_DIM), dtype),
            pltpu.VMEM((rows * steps, HEAD_DIM), dtype),
            pltpu.VMEM((rows * suffix, HEAD_DIM), dtype),
            pltpu.VMEM((rows * suffix, HEAD_DIM), dtype),
            pltpu.VMEM((rows * steps, width), dtype),
            pltpu.VMEM((count, 4, nb, HEAD_DIM), jnp.int32),
            pltpu.VMEM((count, groups, nb, HEAD_DIM), jnp.float32),
            pltpu.VMEM((count, groups * nb, slots * prefix + HEAD_DIM), jnp.bfloat16),
            pltpu.VMEM((count, groups, nb, 2 * HEAD_DIM), jnp.bfloat16),
            pltpu.VMEM((count, groups * nb, HEAD_DIM), jnp.float32),
            dma(3, 2),
        ]

    sizes = dict(slots=slots, steps=steps, suffix=suffix)
    by_replica = [x.reshape(replicas, local_rows) for x in (row_slot, cache_lengths, finished)]
    lookup = in_hbm(prompt_lengths, *by_replica)
    rows_in = in_hbm(queries, nk2, nv2, ck2, cv2)
    h_first, pk, pv, w_there = pl.pallas_call(
        functools.partial(first_kernel, stacked=stacked, replicas=replicas, moved=moved, span=span, **sizes),
        out_shape=[pltpu.VMEM((nh + m, width), dtype), prompts, prompts, pltpu.VMEM((2 * width, model), dtype)],
        in_specs=[SMEM] * 3 + [VMEM] * 3 + [ANY] * (9 + len(received)),
        out_specs=[VMEM] * 4,
        scratch_shapes=[
            pltpu.VMEM((moved * span, HEAD_DIM), dtype),
            pltpu.VMEM((moved * suffix, HEAD_DIM), dtype),
            pltpu.VMEM((moved * suffix, HEAD_DIM), dtype),
            pltpu.VMEM((4, moved * span, HEAD_DIM), jnp.int32),
        ]
        + work(half)
        + [dma(slots, 2), dma(2), dma(moved), dma(2 * moved)],
        compiler_params=params(),
        cost_estimate=SMALL,
        name="attend_first",
    )(*in_hbm(fork, pairs), *lookup, *rows_in, *in_hbm(prompt_keys, prompt_values, out_proj), w_sib, *received)

    def call(kernel, name, shapes, specs, operands, extra=()):
        return pl.pallas_call(
            kernel,
            out_shape=[pltpu.VMEM(shape, kind) for shape, kind in shapes],
            in_specs=specs,
            out_specs=[VMEM] * len(shapes),
            scratch_shapes=list(extra),
            compiler_params=params(),
            cost_estimate=SMALL,
            name=name,
        )(*operands)

    def cross(heads, rows):
        sib = lax.ppermute(heads, "tensor", sibling)
        (crossed,) = call(project_kernel, "project", [((rows, model), dtype)], [VMEM] * 3, (heads, sib, w_there))
        return sib, crossed, lax.ppermute(crossed, "tensor", across)

    s_first, c_first, got_first = cross(h_first, nh)
    options = dict(moved=moved, steps=steps, split=not stacked)
    shape = ((replicas if stacked else 4, steps, 2 * width), dtype)
    back = call(
        functools.partial(moved_send_kernel, **options),
        "moved_send",
        [shape] * (1 if stacked else 2),
        [SMEM, VMEM, VMEM, ANY],
        (*in_hbm(pairs), h_first, s_first, c_first),
    )
    (h_second,) = call(
        functools.partial(second_kernel, first_row=half * BLOCK, **sizes),
        "attend_second",
        [((n - nh, width), dtype)],
        [SMEM] * 2 + [VMEM] * 5 + [ANY] * 6,
        (*in_hbm(fork), *lookup, pk, pv, *rows_in, c_first),
        work(blocks - half),
    )
    s_second, c_second, got_second = cross(h_second, n - nh)
    if stacked:
        backs = [lax.all_to_all(back[0], "replica", split_axis=0, concat_axis=0, tiled=True)]
    else:
        flip = lambda x, bit: lax.ppermute(x, "replica", [(i, i ^ bit) for i in range(replicas)])
        kept = back[0]
        one = flip(back[1], 1)
        one, *_ = lax.optimization_barrier((one, c_second))
        two = flip(jnp.concatenate([kept[2:], one[2:]]), 2)
        two, *_ = lax.optimization_barrier((two, got_first))
        four = flip(jnp.concatenate([kept[1:2], one[1:2], two[1:2], two[3:4]]), 4)
        backs = [one, two, four]
    crossed_moved, home_heads = call(
        functools.partial(moved_project_kernel, **options),
        "moved_project",
        [((m, model), dtype), ((m, 2 * width), dtype)],
        [SMEM] + [VMEM] * (1 + len(backs)),
        (*in_hbm(pairs), w_there, *backs),
        [pltpu.VMEM((m, 2 * width), jnp.float32)],
    )
    got_moved = lax.ppermute(crossed_moved, "tensor", across)
    base, base_moved = call(
        base_kernel,
        "base",
        [((n, model), jnp.float32), ((m, model), jnp.float32)],
        [SMEM] + [VMEM] * 5 + [ANY] * 3,
        (*in_hbm(pairs), h_first, s_first, h_second, s_second, home_heads, *in_hbm(out_proj), w_sib, *in_hbm(residual)),
        [pltpu.VMEM((2 * width, model), dtype), pltpu.VMEM(residual.shape, dtype), dma(3)],
    )

    whole = jax.ShapeDtypeStruct(residual.shape, residual.dtype)
    out = pl.pallas_call(
        finish_first_kernel,
        grid=(half,),
        in_specs=[VMEM, VMEM],
        out_specs=pl.BlockSpec((BLOCK, steps, model), lambda i: (i, 0, 0)),
        out_shape=whole,
        compiler_params=params(),
        name="finish_first",
    )(base, got_first)
    return pl.pallas_call(
        functools.partial(finish_second_kernel, moved=moved),
        in_specs=[SMEM, VMEM, VMEM, VMEM, VMEM, ANY],
        out_specs=ANY,
        out_shape=whole,
        input_output_aliases={5: 0},
        scratch_shapes=[
            pltpu.VMEM((moved, steps, model), dtype),
            pltpu.VMEM(((blocks - half) * BLOCK, steps, model), dtype),
            dma(moved),
            dma((blocks - half) * BLOCK // 16, 1),
        ],
        compiler_params=params(),
        name="finish_second",
    )(*in_hbm(pairs), base, got_second, base_moved, got_moved, out)


def solution(mesh):
    rows = P("replica", None, "tensor")
    in_specs = (rows,) * 6 + (P(), P(), P("replica"), P(), P(), rows, rows, P(), P("tensor", None))
    return jax.shard_map(body, mesh=mesh, in_specs=in_specs, out_specs=rows, check_vma=False)
```

```python
import functools
import math

import jax
import jax.numpy as jnp
from jax import lax
from jax.experimental import pallas as pl
from jax.experimental.pallas import tpu as pltpu
from jax.sharding import PartitionSpec as P

HEAD_DIM = 128
LOWEST = -1e30
EXP2_SCALE = math.log2(math.e) / math.sqrt(HEAD_DIM)
VMEM_BYTES = 24 * 1024 * 1024
SMALL = pl.CostEstimate(flops=1, bytes_accessed=1, transcendentals=0)
BLOCK = 32
FIRST = 2
NT = (((1,), (1,)), ((), ()))
NN = (((1,), (0,)), ((), ()))

ANY = pl.BlockSpec(memory_space=pl.ANY)
SMEM = pl.BlockSpec(memory_space=pltpu.SMEM)
VMEM = pl.BlockSpec(memory_space=pltpu.VMEM)


def params(side_effects=False):
    return pltpu.CompilerParams(vmem_limit_bytes=VMEM_BYTES, has_side_effects=side_effects)


def matmul(a, b, dims):
    return lax.dot_general(a, b, dims, preferred_element_type=jnp.float32)


def columns(model, flip):
    place = jnp.bitwise_xor(lax.axis_index("tensor"), flip)
    return pl.ds(pl.multiple_of(place * model, HEAD_DIM), model)


def in_hbm(*arrays):
    return [pltpu.with_memory_space_constraint(x, pltpu.HBM) for x in arrays]


def iota(shape, dim):
    return lax.broadcasted_iota(jnp.int32, shape, dim)


def load(pairs, sem):
    copies = [pltpu.make_async_copy(a, b, sem.at[i]) for i, (a, b) in enumerate(pairs)]
    for copy in copies:
        copy.start()

    def wait():
        for copy in copies:
            copy.wait()

    return wait


def quotient(a, b):
    return a >> (b.bit_length() - 1) if b & (b - 1) == 0 else lax.div(a, b)


def remainder(a, b):
    return a & (b - 1) if b & (b - 1) == 0 else lax.rem(a, b)


def list_pairs(row_of, pairs, me, replicas, moved):
    count = jnp.int32(0)
    for j in range(replicas):
        pairs[count] = row_of[j]
        pairs[moved + 1 + count] = j
        pairs[2 * (moved + 1) + j] = jnp.maximum(row_of[j], 0)
        count = jnp.minimum(count + jnp.where((row_of[j] >= 0) & (j != me), 1, 0), moved)


def find_pairs(partner, row_of, replicas, local_rows):
    for j in range(replicas):
        row_of[j] = -1

    def note(r, carry):
        row_of[quotient(partner[r], local_rows)] = r
        return carry

    lax.fori_loop(0, local_rows, note, 0, unroll=8)


def send_prompts(shifts, fork, keys, values, outs, sems, replicas):
    me = lax.axis_index("replica")
    held, prefix = keys.shape[0], keys.shape[1]
    waits = []
    for i, k in enumerate(shifts):
        peer = remainder(me + k, replicas)
        offset = jnp.int32(0)
        for s in range(fork.shape[0]):
            prompt = fork[s, peer]
            offset = jnp.where(quotient(prompt, held) == me, remainder(prompt, held), offset)
        copies = [
            (source.at[offset], outs[i].at[pl.ds(n * prefix, prefix)]) for n, source in enumerate((keys, values))
        ]
        waits.append(load(copies, sems.at[i]))
    return waits


def send_rows(shifts, row_of, hbm, vmem, outs, sems, replicas, prefix):
    me = lax.axis_index("replica")
    width = hbm[0].shape[2]
    waits = []
    for i, k in enumerate(shifts):
        r = row_of(remainder(me + k, replicas))
        waits.append(load([(a.at[r], b.at[i]) for a, b in zip(hbm, vmem)], sems.at[i]))
    for i in range(len(shifts)):
        waits[i]()
        q, nk, nv = [v[i].astype(jnp.float32) for v in vmem]
        parts = [q[:, low : low + HEAD_DIM] for low in range(0, width, HEAD_DIM)] + [nk, nv]
        pad = outs[i].shape[0] - 2 * prefix - sum(p.shape[0] for p in parts)
        parts += [jnp.zeros((pad, HEAD_DIM), jnp.float32)]
        outs[i][2 * prefix :, :] = jnp.concatenate(parts, axis=0).astype(outs[i].dtype)


def pairs_kernel(partner, pairs, row_of, *, replicas, local_rows, moved):
    find_pairs(partner, row_of, replicas, local_rows)
    list_pairs(row_of, pairs, lax.axis_index("replica"), replicas, moved)


def pack_kernel(
    fork, partner, queries, new_keys, new_values, keys, values, *rest, replicas, moved, shifts
):
    outs, (pairs, qv, nkv, nvv, row_of, sems, row_sems) = rest[: len(shifts)], rest[len(shifts) :]
    waits = send_prompts(shifts, fork, keys, values, outs, sems, replicas)
    find_pairs(partner, row_of, replicas, queries.shape[0])
    list_pairs(row_of, pairs, lax.axis_index("replica"), replicas, moved)
    send_rows(
        shifts, lambda j: jnp.maximum(row_of[j], 0), (queries, new_keys, new_values), (qv, nkv, nvv), outs, row_sems,
        replicas, keys.shape[1],
    )
    for wait in waits:
        wait()


def softmax_weights(prompt, new, cache, prompt_mask, new_mask, cache_mask):
    prompt = jnp.where(prompt_mask, prompt, LOWEST)
    new = jnp.where(new_mask, new, LOWEST)
    cache = jnp.where(cache_mask, cache, LOWEST)
    top = jnp.max(jnp.maximum(jnp.maximum(prompt, new), cache), axis=1, keepdims=True)
    prompt = jnp.exp2((prompt - top) * EXP2_SCALE)
    new = jnp.exp2((new - top) * EXP2_SCALE)
    cache = jnp.exp2((cache - top) * EXP2_SCALE)
    inverse = 1.0 / jnp.sum(prompt + new + cache, axis=1, keepdims=True)
    return prompt * inverse, new * inverse, cache * inverse


def pick_slot(scores, slot, slots, prefix):
    picked = scores[:, :prefix]
    for s in range(1, slots):
        picked = jnp.where(slot == s, scores[:, s * prefix : (s + 1) * prefix], picked)
    return picked


def spread_slot(weights, slot, slots):
    return jnp.concatenate(
        [jnp.where(slot == s, weights, 0.0).astype(jnp.bfloat16) for s in range(slots)], axis=1
    )


def row_values(slots_of, lengths, finished, fork, prompt_lengths, slots):
    me = lax.axis_index("replica")
    shape = (HEAD_DIM, slots_of.shape[1])
    slot, length, done = [jnp.broadcast_to(v[pl.ds(me, 1), :], shape) for v in (slots_of, lengths, finished)]
    prompt = jnp.zeros(shape, jnp.int32)
    for s in range(slots):
        prompt = jnp.where(slot == s, prompt_lengths[fork[s, me]], prompt)
    return [v.astype(jnp.float32).astype(jnp.bfloat16) for v in (slot, prompt, length, 1 - done)]


def fill_meta(values, row_of, meta):
    take = (row_of == iota(row_of.shape, 1)).astype(jnp.float32).astype(jnp.bfloat16)
    for i, value in enumerate(values):
        meta[i] = matmul(take, value, NT).astype(jnp.int32)


def attend_scores(q, ck, cache_scores, *, steps, suffix):
    n = q.shape[0]
    groups = q.shape[1] // HEAD_DIM
    keys_sub = 4 * suffix
    half = 2 * suffix
    for sub in range(n // 16):
        r0 = sub * 16
        qs = jnp.concatenate(
            [q[r0 : r0 + 16, h * HEAD_DIM : (h + 1) * HEAD_DIM] for h in range(groups)], axis=0
        )
        s = matmul(qs, ck[sub * keys_sub : (sub + 1) * keys_sub, :], NT)
        for h in range(groups):
            cache_scores[h, r0 : r0 + 8, :] = s[16 * h : 16 * h + 8, :half]
            cache_scores[h, r0 + 8 : r0 + 16, :] = s[16 * h + 8 : 16 * h + 16, half:]


def attend_block(
    q, nk, nv, cv, pk, pv, heads, meta, cache_scores, weights, cache_weights, mixed, wait,
    *, steps, slots, suffix
):
    n = q.shape[0]
    groups = q.shape[1] // HEAD_DIM
    prefix = pk.shape[0] // slots
    keys_sub = 4 * suffix
    half = 2 * suffix
    shape = (n, HEAD_DIM)
    lane, row = iota(shape, 1), iota(shape, 0)
    cache_own = (lane // suffix) == ((row % 8) // steps)
    cache_lane = jnp.where(cache_own, lane % suffix, suffix)
    new_mask = ((lane // steps) == (row // steps)) & ((lane % steps) <= (row % steps))
    first_half = (row % 16) < 8
    slot = meta[0]
    prompt_mask = lane < meta[1]
    cache_mask = cache_lane < meta[2]
    alive_rows = meta[3].astype(jnp.float32)
    q_all = jnp.concatenate([q[:, h * HEAD_DIM : (h + 1) * HEAD_DIM] for h in range(groups)], axis=0)
    prompt_all = matmul(q_all, pk[...], NT)
    new_all = matmul(q_all, nk[...], NT)
    for h in range(groups):
        part = slice(h * n, (h + 1) * n)
        prompt = pick_slot(prompt_all[part], slot, slots, prefix)
        wp, wn, wc = softmax_weights(
            prompt, new_all[part], cache_scores[h], prompt_mask, new_mask, cache_mask
        )
        cache_weights[h, :, :half] = jnp.where(first_half, wc, 0.0).astype(jnp.bfloat16)
        cache_weights[h, :, half:] = jnp.where(first_half, 0.0, wc).astype(jnp.bfloat16)
        weights[part, : slots * prefix] = spread_slot(wp, slot, slots)
        weights[part, slots * prefix :] = wn.astype(jnp.bfloat16)
    mixed[...] = matmul(weights[:, : slots * prefix], pv[...], NN) + matmul(
        weights[:, slots * prefix :], nv[...], NN
    )
    if wait is not None:
        wait()
    for sub in range(n // 16):
        r0 = sub * 16
        w = jnp.concatenate([cache_weights[h, r0 : r0 + 16, :] for h in range(groups)], axis=0)
        o = matmul(w, cv[sub * keys_sub : (sub + 1) * keys_sub, :], NN)
        for h in range(groups):
            total = mixed[h * n + r0 : h * n + r0 + 16, :] + o[16 * h : 16 * h + 16, :]
            heads[r0 : r0 + 16, h * HEAD_DIM : (h + 1) * HEAD_DIM] = (
                total * alive_rows[r0 : r0 + 16, :]
            ).astype(heads.dtype)


def moved_block(x, pk, pv, keys, values, slot, plen, clen, alive, *, steps, slots, groups, span, suffix):
    prefix = pk.shape[0] // slots
    shape = (4 * span, HEAD_DIM)
    lane, row = iota(shape, 1), iota(shape, 0)
    prompt_mask = lane < plen
    cache_mask = ((lane // suffix) == ((row // span) % 2)) & ((lane % suffix) < clen)
    past = (lane % span) - groups * steps
    new_mask = ((lane // span) == (row // span)) & (past >= 0) & (past <= row % steps)
    prompt = pick_slot(matmul(x, pk[...], NT), slot, slots, prefix)
    new = matmul(x, x, NT)
    cache = matmul(x, keys[...], NT)
    half = 2 * suffix
    top_half = row < 2 * span
    cache = jnp.where(top_half, cache[:, :half], cache[:, half:])
    wp, wn, wc = softmax_weights(prompt, new, cache, prompt_mask, new_mask, cache_mask)
    wc = jnp.concatenate(
        [jnp.where(top_half, wc, 0.0), jnp.where(top_half, 0.0, wc)], axis=1
    ).astype(jnp.bfloat16)
    wn = pltpu.roll(wn, steps, 1).astype(jnp.bfloat16)
    mixed = (
        matmul(spread_slot(wp, slot, slots), pv[...], NN)
        + matmul(wn, x, NN)
        + matmul(wc, values[...], NN)
    )
    mixed = (mixed * alive).astype(jnp.bfloat16)
    row, col = iota((4 * steps, 4 * span), 0), iota((4 * steps, 4 * span), 1)
    cols = []
    for h in range(groups):
        take = ((row // steps) == (col // span)) & ((col % span) == h * steps + row % steps)
        cols.append(matmul(take.astype(jnp.bfloat16), mixed, NN).astype(jnp.bfloat16))
    return jnp.concatenate(cols, axis=1)


def start_rows(first_row, hbm, vmem, sems, steps, suffix):
    rows = vmem[0].shape[0]
    part = pl.ds(first_row * steps, rows * steps)
    keys = pl.ds(first_row * suffix, rows * suffix)
    q, nk, nv, ck, cv = hbm
    first = load([(q.at[pl.ds(first_row, rows)], vmem[0]), (ck.at[keys], vmem[3])], sems.at[0])

    def rest():
        return [
            load([(nk.at[part], vmem[1]), (nv.at[part], vmem[2])], sems.at[1]),
            load([(cv.at[keys], vmem[4])], sems.at[2]),
        ]

    return first, rest


def attend_rows(lookup, first_row, waits, vmem, pk, pv, heads, work, *, steps, slots, suffix):
    q3, nk, nv, ck, cv = vmem
    q, meta, cache_scores, weights, cache_weights, mixed = work
    count, _, n, _ = meta.shape
    rows = n // steps
    per = 16 // steps
    shape = (n, lookup[0].shape[1])
    for i in range(count):
        fill_meta(lookup, first_row + i * rows + iota(shape, 0) // steps, meta.at[i])
    waits[0]()
    for b in range(0, count * rows, per):
        part = [q3[b + i].astype(jnp.float32) for i in range(per)]
        q[b * steps : (b + per) * steps, :] = jnp.concatenate(part, axis=0).astype(q.dtype)
    keys = rows * suffix
    for i in range(count):
        attend_scores(
            q.at[pl.ds(i * n, n)], ck.at[pl.ds(i * keys, keys)], cache_scores.at[i], steps=steps, suffix=suffix
        )
    waits[1]()
    for i in range(count):
        part = pl.ds(i * n, n)
        attend_block(
            q.at[part], nk.at[part], nv.at[part], cv.at[pl.ds(i * keys, keys)], pk, pv, heads.at[part],
            meta.at[i], cache_scores.at[i], weights.at[i], cache_weights.at[i], mixed.at[i],
            waits[2] if i == 0 else None, steps=steps, slots=slots, suffix=suffix,
        )


def first_kernel(
    fork, pairs, prompt_lengths, row_slot, cache_lengths, finished, q, nk, nv, ck, cv, own_keys, own_values, w_own, w_sib,
    *rest, stacked, replicas, slots, moved, steps, suffix, span
):
    recvs, rest = rest[:-24], rest[-24:]
    heads, pk, pv, w_there, x, keys, values, moved_meta = rest[:8]
    vmem, work, (row_sems, slot_sems, w_sems, sems, cache_sems) = rest[8:13], rest[13:19], rest[19:]
    me = lax.axis_index("replica")
    held, prefix = own_keys.shape[0], own_keys.shape[1]
    scores_ready, start_rest = start_rows(0, (q, nk, nv, ck, cv), vmem, row_sems, steps, suffix)
    for s in range(slots):
        prompt = fork[s, me]
        owner = quotient(prompt, held)
        offset = remainder(prompt, held)
        targets = (pk.at[pl.ds(s * prefix, prefix)], pv.at[pl.ds(s * prefix, prefix)])
        if stacked:
            for i in range(2):
                pltpu.make_async_copy(
                    recvs[0].at[owner, pl.ds(i * prefix, prefix)], targets[i], slot_sems.at[s, i]
                ).start()
            continue
        k = remainder(me - owner + replicas, replicas)

        @pl.when(k == 0)
        def _():
            pltpu.make_async_copy(own_keys.at[offset], targets[0], slot_sems.at[s, 0]).start()
            pltpu.make_async_copy(own_values.at[offset], targets[1], slot_sems.at[s, 1]).start()

        for kk in range(1, replicas):

            @pl.when(k == kk)
            def _():
                for i in range(2):
                    pltpu.make_async_copy(
                        recvs[kk - 1].at[pl.ds(i * prefix, prefix)], targets[i], slot_sems.at[s, i]
                    ).start()

    waits = [scores_ready, *start_rest()]
    groups = q.shape[2] // HEAD_DIM
    for i in range(moved):
        peer = pairs[moved + 1 + i]
        if stacked:
            pltpu.make_async_copy(
                recvs[0].at[peer, pl.ds(2 * prefix, span)], x.at[pl.ds(i * span, span)], sems.at[i]
            ).start()
        else:
            k = remainder(me - peer + replicas, replicas)
            for kk in range(1, replicas):

                @pl.when(k == kk)
                def _():
                    pltpu.make_async_copy(
                        recvs[kk - 1].at[pl.ds(2 * prefix, span)], x.at[pl.ds(i * span, span)], sems.at[i]
                    ).start()

    copies = []
    for i in range(moved):
        source = pl.ds(pl.multiple_of(pairs[i] * suffix, suffix), suffix)
        target = pl.ds(i * suffix, suffix)
        copies += [(ck.at[source], keys.at[target]), (cv.at[source], values.at[target])]
    caches_ready = load(copies, cache_sems)
    width, model = w_own.shape[0], w_there.shape[1]
    at = columns(model, 2)
    weights_ready = load(
        [(w_own.at[:, at], w_there.at[pl.ds(0, width)]), (w_sib.at[:, at], w_there.at[pl.ds(width, width)])], w_sems
    )

    def wait_second():
        waits[1]()
        for s in range(slots):
            for i, target in enumerate((pk, pv)):
                pltpu.make_async_copy(own_keys.at[0], target.at[pl.ds(s * prefix, prefix)], slot_sems.at[s, i]).wait()

    lookup = row_values(row_slot, cache_lengths, finished, fork, prompt_lengths, slots)
    shape = (moved * span, row_slot.shape[1])
    item = iota(shape, 0) // span
    row_of = jnp.zeros(shape, jnp.int32)
    for i in range(moved):
        row_of = jnp.where(item == i, pairs[i], row_of)
    fill_meta(lookup, row_of, moved_meta)
    n = heads.shape[0] - moved * steps
    attend_rows(
        lookup, 0, (waits[0], wait_second, waits[2]), vmem, pk, pv, heads.at[pl.ds(0, n)], work,
        steps=steps, slots=slots, suffix=suffix,
    )
    for i in range(moved):
        source = recvs[0].at[0, pl.ds(0, span)] if stacked else recvs[0].at[pl.ds(0, span)]
        pltpu.make_async_copy(source, x.at[pl.ds(i * span, span)], sems.at[i]).wait()
    caches_ready()
    for g in range(moved // 4):
        part = slice(g * 4 * span, (g + 1) * 4 * span)
        kpart = slice(g * 4 * suffix, (g + 1) * 4 * suffix)
        heads[n + g * 4 * steps : n + (g + 1) * 4 * steps, :] = moved_block(
            x[part, :], pk, pv, keys.at[kpart], values.at[kpart],
            moved_meta[0, part, :], moved_meta[1, part, :], moved_meta[2, part, :],
            moved_meta[3, part, :].astype(jnp.float32),
            steps=steps, slots=slots, groups=groups, span=span, suffix=suffix,
        )
    weights_ready()


def second_kernel(
    fork, prompt_lengths, row_slot, cache_lengths, finished, pk, pv, q, nk, nv, ck, cv, after, *rest,
    first_row, slots, steps, suffix
):
    heads, vmem, work, row_sems = rest[0], rest[1:6], rest[6:12], rest[12]
    scores_ready, start_rest = start_rows(first_row, (q, nk, nv, ck, cv), vmem, row_sems, steps, suffix)
    waits = [scores_ready, *start_rest()]
    lookup = row_values(row_slot, cache_lengths, finished, fork, prompt_lengths, slots)
    attend_rows(
        lookup, first_row, waits, vmem, pk, pv, heads, work, steps=steps, slots=slots, suffix=suffix
    )


def project_kernel(h_own, h_sib, weights, out):
    rows = pl.ds(0, out.shape[0])
    both = jnp.concatenate([h_own[rows, :], h_sib[rows, :]], axis=1)
    out[...] = matmul(both, weights[...], NN).astype(out.dtype)


def base_kernel(
    pairs, h_first, s_first, h_second, s_second, w_own, w_sib, residual, out, weights, moved_out, before, sems
):
    rows, model = out.shape
    width = w_own.shape[0]
    steps = residual.shape[1]
    at = columns(model, 0)
    ready = load(
        [
            (w_own.at[:, at], weights.at[pl.ds(0, width)]),
            (w_sib.at[:, at], weights.at[pl.ds(width, width)]),
            (residual, before),
        ],
        sems,
    )
    ready()
    for i in range(moved_out.shape[0] // steps):
        moved_out[i * steps : (i + 1) * steps, :] = before[pairs[i]].astype(jnp.float32)
    low = 0
    for h_own, h_sib, size in ((h_first, s_first, rows - h_second.shape[0]), (h_second, s_second, h_second.shape[0])):
        part = pl.ds(0, size)
        total = matmul(jnp.concatenate([h_own[part, :], h_sib[part, :]], axis=1), weights[...], NN)
        for b in range(0, size, steps):
            out[low : low + steps, :] = total[b : b + steps] + before[low // steps].astype(jnp.float32)
            low += steps


def moved_send_kernel(pairs, h_own, h_sib, after, *outs, moved, steps, split):
    me = lax.axis_index("replica")
    rows = pl.ds(h_own.shape[0] - moved * steps, moved * steps)
    both = jnp.concatenate([h_own[rows, :], h_sib[rows, :]], axis=1).astype(jnp.float32)
    for i in range(moved):
        peer = pairs[moved + 1 + i]
        value = both[i * steps : (i + 1) * steps].astype(outs[0].dtype)
        if split:
            k = jnp.bitwise_xor(me, peer)
            place = 2 * remainder(quotient(k, 2), 2) + quotient(k, 4)

            @pl.when(remainder(k, 2) == 0)
            def _():
                outs[0][place] = value

            @pl.when(remainder(k, 2) == 1)
            def _():
                outs[1][place] = value

        else:
            outs[0][peer] = value


def moved_project_kernel(pairs, w_here, w_there, before, *rest, moved, steps, split):
    backs, (cross, base, heads) = rest[:-3], rest[-3:]
    me = lax.axis_index("replica")
    for i in range(moved):
        peer = pairs[moved + 1 + i]
        part = slice(i * steps, (i + 1) * steps)
        if split:
            k = jnp.bitwise_xor(me, peer)
            places = {1: (0, 0), 2: (1, 0), 3: (1, 2), 4: (2, 0), 5: (2, 1), 6: (2, 2), 7: (2, 3)}
            for d, (which, index) in places.items():

                @pl.when(k == d)
                def _():
                    heads[part, :] = backs[which][index].astype(jnp.float32)

        else:
            heads[part, :] = backs[0][peer].astype(jnp.float32)
    both = heads[...].astype(cross.dtype)
    cross[...] = matmul(both, w_there[...], NN).astype(cross.dtype)
    base[...] = matmul(both, w_here[...], NN) + before[...]


def add_rows(total, out, first, steps):
    for b in range(total.shape[0] // steps):
        out[first + b] = total[b * steps : (b + 1) * steps].astype(out.dtype)


def finish_first_kernel(base, recv, out):
    rows, steps = out.shape[:2]
    part = pl.ds(pl.multiple_of(pl.program_id(0) * rows * steps, rows * steps), rows * steps)
    add_rows(base[part, :] + recv[part, :].astype(jnp.float32), out, 0, steps)


def finish_second_kernel(pairs, base, recv, base_moved, recv_moved, earlier, out, after, rows_out, sems, row_sems, *, moved):
    later, steps = rows_out.shape[:2]
    half = out.shape[0] - later
    branch = base_moved[...] + recv_moved[...].astype(jnp.float32)
    for i in range(moved):
        after[i] = branch[i * steps : (i + 1) * steps].astype(after.dtype)

        @pl.when(pairs[i] < half)
        def _():
            pltpu.make_async_copy(after.at[i], out.at[pairs[i]], sems.at[i]).start()

    size = 16
    done = []
    for part in range(later // size):
        low = part * size
        rows = slice((half + low) * steps, (half + low + size) * steps)
        got = slice(low * steps, (low + size) * steps)
        add_rows(base[rows, :] + recv[got, :].astype(jnp.float32), rows_out, low, steps)
        for i in range(moved):
            r = pairs[i] - half

            @pl.when((r >= low) & (r < low + size))
            def _():
                rows_out[r] = after[i]

        piece = pl.ds(low, size)
        done.append(load([(rows_out.at[piece], out.at[pl.ds(half + low, size)])], row_sems.at[part]))
    for i in range(moved):

        @pl.when(pairs[i] < half)
        def _():
            pltpu.make_async_copy(after.at[i], out.at[pairs[i]], sems.at[i]).wait()

    for wait in done:
        wait()


def row_buffers(count, steps, width, dtype):
    return [pltpu.VMEM((count, steps, size), dtype) for size in (width, HEAD_DIM, HEAD_DIM)]


def exchange_pack(
    fork, partner, row_slot, queries, new_keys, new_values, fork_table, prompt_keys, prompt_values, span, moved
):
    replicas = lax.axis_size("replica")
    me = lax.axis_index("replica")
    local_rows, steps, width = queries.shape
    groups = width // HEAD_DIM
    held, prefix = prompt_keys.shape[:2]
    dtype = queries.dtype
    pairs_shape = jax.ShapeDtypeStruct((2 * (moved + 1) + replicas,), jnp.int32)
    if replicas <= 8:
        shifts = tuple(range(1, replicas))
        count = len(shifts)
        *packed, pairs = pl.pallas_call(
            functools.partial(pack_kernel, replicas=replicas, moved=moved, shifts=shifts),
            out_shape=[pltpu.VMEM((2 * prefix + span, HEAD_DIM), dtype)] * count + [pairs_shape],
            in_specs=[SMEM, SMEM] + [ANY] * 5,
            out_specs=[VMEM] * count + [SMEM],
            scratch_shapes=row_buffers(count, steps, width, dtype)
            + [
                pltpu.SMEM((replicas,), jnp.int32),
                pltpu.SemaphoreType.DMA((count, 2)),
                pltpu.SemaphoreType.DMA((count, 3)),
            ],
            compiler_params=params(),
            name="pack",
        )(*in_hbm(fork, partner, queries, new_keys, new_values, prompt_keys, prompt_values))
        return packed, pairs
    chosen = (fork_table // held) == me
    offsets = jnp.sum(jnp.where(chosen, fork_table % held, 0), axis=1)
    peer_of = partner // local_rows
    pairing = (peer_of[None, :] == jnp.arange(replicas, dtype=jnp.int32)[:, None]) & (
        peer_of[None, :] != me
    )
    row_of = jnp.sum(jnp.where(pairing, jnp.arange(local_rows, dtype=jnp.int32)[None, :], 0), axis=1)
    q = queries[row_of].reshape(replicas, steps, groups, HEAD_DIM).transpose(0, 2, 1, 3)
    q = q.reshape(replicas, groups * steps, HEAD_DIM)
    pad = jnp.zeros((replicas, span - (groups + 2) * steps, HEAD_DIM), dtype)
    block = jnp.concatenate(
        [prompt_keys[offsets], prompt_values[offsets], q, new_keys[row_of], new_values[row_of], pad], axis=1
    )
    pairs = pl.pallas_call(
        functools.partial(pairs_kernel, replicas=replicas, local_rows=local_rows, moved=moved),
        out_shape=pairs_shape,
        in_specs=[SMEM],
        out_specs=SMEM,
        scratch_shapes=[pltpu.SMEM((replicas,), jnp.int32)],
        name="pairs",
    )(partner)
    return [block], pairs


def body(
    residual,
    queries,
    new_keys,
    new_values,
    cache_keys,
    cache_values,
    cache_lengths,
    finished,
    partner,
    row_slot,
    fork_table,
    prompt_keys,
    prompt_values,
    prompt_lengths,
    out_proj,
):
    replicas = lax.axis_size("replica")
    tensors = lax.axis_size("tensor")
    local_rows, steps, width = queries.shape
    groups = width // HEAD_DIM
    suffix = cache_keys.shape[1]
    held, prefix = prompt_keys.shape[:2]
    slots = fork_table.shape[1]
    moved = replicas // 2
    stacked = replicas > 8
    model = residual.shape[2]
    n = local_rows * steps
    span = 32
    dtype = queries.dtype
    fork = fork_table.T
    sibling = [(i, i ^ 1) for i in range(tensors)]
    across = [(i, i ^ 2) for i in range(tensors)]

    packed, pairs = exchange_pack(
        fork, partner, row_slot, queries, new_keys, new_values, fork_table, prompt_keys, prompt_values, span, moved
    )
    w_sib = lax.ppermute(out_proj, "tensor", sibling)
    nk2 = new_keys.reshape(n, HEAD_DIM)
    nv2 = new_values.reshape(n, HEAD_DIM)
    ck2 = cache_keys.reshape(local_rows * suffix, HEAD_DIM)
    cv2 = cache_values.reshape(local_rows * suffix, HEAD_DIM)
    lookup = (row_slot, prompt_lengths, cache_lengths, finished)

    dma = lambda *shape: pltpu.SemaphoreType.DMA(shape)
    blocks = local_rows // BLOCK
    nb = BLOCK * steps
    assert nb == HEAD_DIM
    if stacked:
        received = [lax.all_to_all(packed[0], "replica", split_axis=0, concat_axis=0, tiled=True)]
    else:
        received = [
            lax.ppermute(block, "replica", [(i, (i + k) % replicas) for i in range(replicas)])
            for k, block in enumerate(packed, 1)
        ]

    m = moved * steps
    half = FIRST
    nh = half * nb
    prompts = pltpu.VMEM((slots * prefix, HEAD_DIM), dtype)

    def work(count):
        rows = count * BLOCK
        return [
            pltpu.VMEM((rows, steps, width), dtype),
            pltpu.VMEM((rows * steps, HEAD_DIM), dtype),
            pltpu.VMEM((rows * steps, HEAD_DIM), dtype),
            pltpu.VMEM((rows * suffix, HEAD_DIM), dtype),
            pltpu.VMEM((rows * suffix, HEAD_DIM), dtype),
            pltpu.VMEM((rows * steps, width), dtype),
            pltpu.VMEM((count, 4, nb, HEAD_DIM), jnp.int32),
            pltpu.VMEM((count, groups, nb, HEAD_DIM), jnp.float32),
            pltpu.VMEM((count, groups * nb, slots * prefix + HEAD_DIM), jnp.bfloat16),
            pltpu.VMEM((count, groups, nb, 2 * HEAD_DIM), jnp.bfloat16),
            pltpu.VMEM((count, groups * nb, HEAD_DIM), jnp.float32),
            dma(3, 2),
        ]

    sizes = dict(slots=slots, steps=steps, suffix=suffix)
    by_replica = [x.reshape(replicas, local_rows) for x in (row_slot, cache_lengths, finished)]
    lookup = in_hbm(prompt_lengths, *by_replica)
    rows_in = in_hbm(queries, nk2, nv2, ck2, cv2)
    h_first, pk, pv, w_there = pl.pallas_call(
        functools.partial(first_kernel, stacked=stacked, replicas=replicas, moved=moved, span=span, **sizes),
        out_shape=[pltpu.VMEM((nh + m, width), dtype), prompts, prompts, pltpu.VMEM((2 * width, model), dtype)],
        in_specs=[SMEM] * 3 + [VMEM] * 3 + [ANY] * (9 + len(received)),
        out_specs=[VMEM] * 4,
        scratch_shapes=[
            pltpu.VMEM((moved * span, HEAD_DIM), dtype),
            pltpu.VMEM((moved * suffix, HEAD_DIM), dtype),
            pltpu.VMEM((moved * suffix, HEAD_DIM), dtype),
            pltpu.VMEM((4, moved * span, HEAD_DIM), jnp.int32),
        ]
        + work(half)
        + [dma(slots, 2), dma(2), dma(moved), dma(2 * moved)],
        compiler_params=params(),
        cost_estimate=SMALL,
        name="attend_first",
    )(*in_hbm(fork, pairs), *lookup, *rows_in, *in_hbm(prompt_keys, prompt_values, out_proj), w_sib, *received)

    def call(kernel, name, shapes, specs, operands, extra=()):
        return pl.pallas_call(
            kernel,
            out_shape=[pltpu.VMEM(shape, kind) for shape, kind in shapes],
            in_specs=specs,
            out_specs=[VMEM] * len(shapes),
            scratch_shapes=list(extra),
            compiler_params=params(),
            cost_estimate=SMALL,
            name=name,
        )(*operands)

    def cross(heads, rows):
        sib = lax.ppermute(heads, "tensor", sibling)
        (crossed,) = call(project_kernel, "project", [((rows, model), dtype)], [VMEM] * 3, (heads, sib, w_there))
        return sib, crossed, lax.ppermute(crossed, "tensor", across)

    s_first, c_first, got_first = cross(h_first, nh)
    options = dict(moved=moved, steps=steps, split=not stacked)
    shape = ((replicas if stacked else 4, steps, 2 * width), dtype)
    back = call(
        functools.partial(moved_send_kernel, **options),
        "moved_send",
        [shape] * (1 if stacked else 2),
        [SMEM, VMEM, VMEM, ANY],
        (*in_hbm(pairs), h_first, s_first, c_first),
    )
    (h_second,) = call(
        functools.partial(second_kernel, first_row=half * BLOCK, **sizes),
        "attend_second",
        [((n - nh, width), dtype)],
        [SMEM] * 2 + [VMEM] * 5 + [ANY] * 6,
        (*in_hbm(fork), *lookup, pk, pv, *rows_in, c_first),
        work(blocks - half),
    )
    s_second, c_second, got_second = cross(h_second, n - nh)
    if stacked:
        backs = [lax.all_to_all(back[0], "replica", split_axis=0, concat_axis=0, tiled=True)]
    else:
        flip = lambda x, bit: lax.ppermute(x, "replica", [(i, i ^ bit) for i in range(replicas)])
        kept = back[0]
        one = flip(back[1], 1)
        one, *_ = lax.optimization_barrier((one, c_second))
        two = flip(jnp.concatenate([kept[2:], one[2:]]), 2)
        two, *_ = lax.optimization_barrier((two, got_first))
        four = flip(jnp.concatenate([kept[1:2], one[1:2], two[1:2], two[3:4]]), 4)
        backs = [one, two, four]
    base, w_here, before = call(
        base_kernel,
        "base",
        [((n, model), jnp.float32), ((2 * width, model), dtype), ((m, model), jnp.float32)],
        [SMEM] + [VMEM] * 4 + [ANY] * 3,
        (*in_hbm(pairs), h_first, s_first, h_second, s_second, *in_hbm(out_proj), w_sib, *in_hbm(residual)),
        [pltpu.VMEM(residual.shape, dtype), dma(3)],
    )
    crossed_moved, base_moved = call(
        functools.partial(moved_project_kernel, **options),
        "moved_project",
        [((m, model), dtype), ((m, model), jnp.float32)],
        [SMEM] + [VMEM] * (3 + len(backs)),
        (*in_hbm(pairs), w_here, w_there, before, *backs),
        [pltpu.VMEM((m, 2 * width), jnp.float32)],
    )
    got_moved = lax.ppermute(crossed_moved, "tensor", across)

    whole = jax.ShapeDtypeStruct(residual.shape, residual.dtype)
    out = pl.pallas_call(
        finish_first_kernel,
        grid=(half,),
        in_specs=[VMEM, VMEM],
        out_specs=pl.BlockSpec((BLOCK, steps, model), lambda i: (i, 0, 0)),
        out_shape=whole,
        compiler_params=params(),
        name="finish_first",
    )(base, got_first)
    return pl.pallas_call(
        functools.partial(finish_second_kernel, moved=moved),
        in_specs=[SMEM, VMEM, VMEM, VMEM, VMEM, ANY],
        out_specs=ANY,
        out_shape=whole,
        input_output_aliases={5: 0},
        scratch_shapes=[
            pltpu.VMEM((moved, steps, model), dtype),
            pltpu.VMEM(((blocks - half) * BLOCK, steps, model), dtype),
            dma(moved),
            dma((blocks - half) * BLOCK // 16, 1),
        ],
        compiler_params=params(),
        name="finish_second",
    )(*in_hbm(pairs), base, got_second, base_moved, got_moved, out)


def solution(mesh):
    rows = P("replica", None, "tensor")
    in_specs = (rows,) * 6 + (P(), P(), P("replica"), P(), P(), rows, rows, P(), P("tensor", None))
    return jax.shard_map(body, mesh=mesh, in_specs=in_specs, out_specs=rows, check_vma=False)
```
